512 devices in a mesh: dp: 64 (over y, z_hi, x), tensor: 8 (over z_lo, core).
Axes of the slice: x: 4, y: 8, z: 8 (z_hi: 2, z_lo: 4; z = z_hi * 4 + z_lo), core: 2. Of those that a mesh axis runs over, the one named last changes fastest.
Arguments:
- inputs: bfloat16 [8192, 4096], P('dp'), may hold values from -6 to 6
- w_key: bfloat16 [4096, 1024], P(None, 'tensor'), may hold values from -0.09375 to 0.09375
- values: bfloat16 [8192, 1024], P('dp', 'tensor'), may hold values from -6 to 6
- queries: bfloat16 [8192, 4096], P('dp', 'tensor'), may hold values from -200 to 200
- d_out: bfloat16 [8192, 4096], P('dp', 'tensor'), may hold values from -6 to 6
- doc_lens: int32 [4], replicated, may hold values from 1 to 4096, 8192 in all
- block_pos: int32 [128], P('dp'), may hold values from 0 to 127, as said below
Outputs:
- d_query: bfloat16 [8192, 4096], P('dp', 'tensor')
- d_value: bfloat16 [8192, 1024], P('dp', 'tensor')
- d_input: bfloat16 [8192, 4096], P('dp', 'tensor')
- d_wkey: float32 [4096, 1024], P('dp', 'tensor')
The draws below stay inside these ranges and needn't reach their ends.
Inputs may be any that keep to these rules, and one draw needn't show every extreme that they name: `block_pos`: each stored block holds one block of 64 rows of the pack; every pack block is held once. `doc_lens`: lengths of the 4 documents in pack order; they sum to 8192.
All inputs are finite; a program needn't handle non-finite values.
Results may differ from the reference program's by a relative error of at most 0.023.
The reference program's roundings to bfloat16 on the way (of `key_rows` and `key_grad`) count: a program that leaves them out, or rounds other values in their place, can miss the bound.
Values may be sent and summed in bfloat16 or wider, within the bound.
A program may use at most 64 MiB of HBM per device.

```python
import math
import jax
import jax.numpy as jnp
import numpy as np
from jax import lax

D = 4096
HEADS = 32
KVH = 8
HD = 128
BLK = 64
NDOC = 4
TOKENS = 8192
BPD = 2
NB = 128


def draw_queries(key, part):
    key = jax.random.fold_in(key, 7)
    noise_key = jax.random.fold_in(key, 0)
    base = jnp.clip(jax.random.normal(noise_key, (TOKENS, HEADS * HD), jnp.float32), -6.0, 6.0)
    return base.astype(jnp.bfloat16)


def draw_block_pos(key, part):
    key = jax.random.fold_in(key, 11)
    pair_order = jax.random.permutation(key, NB // 2).astype(jnp.int32)
    pairs = pair_order.reshape(NB // BPD, BPD // 2)
    mirrored = NB - 1 - pairs
    return jnp.concatenate([pairs, mirrored], axis=1).reshape(NB).astype(jnp.int32)


def steps_of(own_key, extent, cuts, low, largest):
    gain = 1.0
    for dim, parts in cuts:
        draws = jax.random.uniform(jax.random.fold_in(jax.random.fold_in(own_key, 6), dim), (parts,), jnp.float32, low / len(cuts), largest / len(cuts))
        gain = gain * jnp.repeat(jnp.exp(draws), extent[dim] // parts).reshape((-1,) + (1,) * (len(extent) - 1 - dim))
    return gain


def length_profile(amount, total, bound, lean):
    weights = [(1 << 20) // math.isqrt(standing ** lean) + 1 for standing in range(2, amount + 1)]
    rest, counts = total - bound - (amount - 1), [1] * (amount - 1)
    while rest > 0:
        free = [i for i in range(amount - 1) if counts[i] < bound]
        mass, budget = sum([weights[i] for i in free]), rest
        for i in free:
            extra = min(bound - counts[i], max(1, budget * weights[i] // mass), rest)
            counts[i] = counts[i] + extra
            rest = rest - extra
    return np.array([bound] + counts)


def ragged(key, count, total, most, skew):
    if count == 2:
        one = jax.random.randint(key, (), max(1, total - most), min(most, total - 1) + 1)
        return jnp.stack([one, total - one])
    tallies = jnp.asarray(length_profile(count, total, most, skew), jnp.int32)
    twos = (count - 1) // 2
    donor, receiver = tallies[1:1 + 2 * twos:2], tallies[2:2 + 2 * twos:2]
    margin = jnp.minimum(donor - 1, most - receiver)
    moved = jax.random.randint(jax.random.fold_in(key, 1), (twos,), 0, 1 << 20) % (margin + 1)
    tallies = tallies.at[1:1 + 2 * twos:2].set(donor - moved).at[2:2 + 2 * twos:2].set(receiver + moved)
    return tallies[jax.random.permutation(jax.random.fold_in(key, 2), count)]


def bell_draw(own_key, extent, spread, bound, shards=(), held_as=jnp.bfloat16):
    array = jax.random.normal(own_key, extent, jnp.float32) * spread
    if len(shards) > 0:
        array = steps_of(own_key, extent, shards, -0.22, 0.18) * array
    return jnp.clip(array, min=-bound, max=bound).astype(held_as)


def setup_inputs(seed: int = 0) -> dict:
    seeds = jax.random.split(jax.random.key(seed), 8)
    return {
        "inputs": bell_draw(seeds[0], (TOKENS, D), 1.0, 6.0, ((0, 64),)),
        "w_key": bell_draw(seeds[1], (D, KVH * HD), D ** -0.5, 0.09375, ((1, 8),)),
        "values": bell_draw(seeds[2], (TOKENS, KVH * HD), 1.0, 6.0, ((0, 64), (1, 8))),
        "queries": draw_queries(jax.random.fold_in(seeds[7], 71), 0),
        "d_out": bell_draw(seeds[4], (TOKENS, HEADS * HD), 1.0, 6.0, ((0, 64), (1, 8))),
        "doc_lens": ragged(seeds[5], NDOC, TOKENS, TOKENS // 2, 2).astype(jnp.int32),
        "block_pos": draw_block_pos(jax.random.fold_in(seeds[7], 71), 0),
    }


def row_positions(block_pos):
    within = jnp.tile(jnp.arange(BLK, dtype=jnp.int32), block_pos.shape[0])
    return jnp.repeat(block_pos, BLK) * BLK + within

def documents(positions, doc_lens):
    starts = jnp.cumsum(doc_lens) - doc_lens
    return lax.optimization_barrier(jnp.sum((positions[:, None] >= starts[None, :]).astype(jnp.int32), axis=1)) - 1

def reference(inputs, w_key, values, queries, d_out, doc_lens, block_pos):
    score_scale = 1.0 / math.sqrt(HD)
    group_size = HEADS // KVH
    positions = row_positions(block_pos)
    doc_ids = documents(positions, doc_lens)
    key_rows = jnp.dot(inputs, w_key, preferred_element_type=jnp.float32).astype(jnp.bfloat16)
    query_block = math.gcd(512, TOKENS)
    block_count = TOKENS // query_block
    query_split = queries.reshape(block_count, query_block, KVH, group_size, HD)
    grad_split = d_out.reshape(block_count, query_block, KVH, group_size, HD)
    pos_split = positions.reshape(block_count, query_block)
    doc_split = doc_ids.reshape(block_count, query_block)
    key_all = key_rows.reshape(TOKENS, KVH, HD).astype(jnp.float32)
    value_all = values.reshape(TOKENS, KVH, HD).astype(jnp.float32)
    key_parts = []
    value_parts = []
    query_parts = []
    for head_index in range(KVH):
        key_head = key_all[:, head_index]
        value_head = value_all[:, head_index]

        def one_block(running, items):
            key_sum, value_sum = running
            query_here, grad_here, pos_here, doc_here = items
            query_float = query_here.astype(jnp.float32)
            grad_float = grad_here.astype(jnp.float32)
            scores = jnp.einsum('qgd,kd->gqk', query_float, key_head) * score_scale
            allowed = (doc_here[:, None] == doc_ids[None, :]) & (positions[None, :] <= pos_here[:, None])
            allowed = allowed[None]
            masked = jnp.where(allowed, scores, -1e+30)
            row_max = lax.optimization_barrier(jnp.max(masked, axis=2, keepdims=True))
            exp_terms = jnp.where(allowed, jnp.exp(scores - row_max), 0.0)
            probabilities = exp_terms / lax.optimization_barrier(jnp.sum(exp_terms, axis=2, keepdims=True))
            d_prob = jnp.einsum('qgd,kd->gqk', grad_float, value_head)
            delta = lax.optimization_barrier(jnp.sum(probabilities * d_prob, axis=2, keepdims=True))
            d_score = probabilities * (d_prob - delta)
            prob_bf = lax.optimization_barrier(probabilities.astype(jnp.bfloat16)).astype(jnp.float32)
            score_bf = lax.optimization_barrier(d_score.astype(jnp.bfloat16)).astype(jnp.float32)
            query_grad = (score_scale * jnp.einsum('gqk,kd->qgd', score_bf, key_head)).astype(jnp.bfloat16)
            key_sum = key_sum + score_scale * jnp.einsum('gqk,qgd->kd', score_bf, query_float)
            value_sum = value_sum + jnp.einsum('gqk,qgd->kd', prob_bf, grad_float)
            return ((key_sum, value_sum), query_grad)
        empty_sum = jnp.zeros((TOKENS, HD), jnp.float32)
        (key_sum, value_sum), query_grad = lax.scan(one_block, (empty_sum, empty_sum), (query_split[:, :, head_index], grad_split[:, :, head_index], pos_split, doc_split))
        key_parts.append(key_sum)
        value_parts.append(value_sum)
        query_parts.append(query_grad.reshape(TOKENS, group_size, HD))
    key_grad = jnp.stack(key_parts, axis=1).reshape(TOKENS, KVH * HD).astype(jnp.bfloat16)
    d_value = jnp.stack(value_parts, axis=1).reshape(TOKENS, KVH * HD).astype(jnp.bfloat16)
    d_query = jnp.stack(query_parts, axis=1).reshape(TOKENS, HEADS * HD)
    d_wkey = jnp.dot(inputs.T, key_grad, preferred_element_type=jnp.float32)
    d_input = jnp.dot(key_grad, w_key.T, preferred_element_type=jnp.float32).astype(jnp.bfloat16)
    return (d_query, d_value, d_input, d_wkey)
```

```python
import functools
import math

import jax
import jax.numpy as jnp
from jax import lax
from jax.experimental import pallas as pl
from jax.experimental.pallas import tpu as pltpu
from jax.sharding import PartitionSpec as P

MESH = pl.DeviceIdType.MESH
F32, BF16 = jnp.float32, jnp.bfloat16
HD, BLK, GROUP, ROWS = 128, 64, 4, 128
NX, NZ, NY, NC = 4, 2, 8, 2
HY, HX = NY // 2, NX // 2
KEY_BLOCKS = 2 * NZ * NY
QUERY_BLOCKS = 2 * NX
STACK = GROUP * BLK
CHUNK = 4
SCALE = 1.0 / math.sqrt(HD)
LOG2 = SCALE / math.log(2.0)
LOW = -1e30
FLOOR = -1e29
NT = (((1,), (1,)), ((), ()))
VMEM_LIMIT = 40 * 1024 * 1024

vmem = pl.BlockSpec(memory_space=pltpu.VMEM)
smem = pl.BlockSpec(memory_space=pltpu.SMEM)
anywhere = pl.BlockSpec(memory_space=pl.ANY)


def rem(a, n):
    return lax.rem(a, jnp.int32(n))


def place():
    dp, tensor = lax.axis_index("dp"), lax.axis_index("tensor")
    x = rem(dp, NX)
    rest = lax.div(dp, jnp.int32(NX))
    return lax.div(rest, jnp.int32(NZ)), rem(rest, NZ), x, tensor


def device(y, zh, x, tensor):
    return ((y * NZ + zh) * NX + x, tensor)


def meet(peers):
    barrier = pltpu.get_barrier_semaphore()
    for peer in peers:
        pl.semaphore_signal(barrier, inc=1, device_id=peer, device_id_type=MESH)
    pl.semaphore_wait(barrier, len(peers))


def send(src, dst, sems, index, peer):
    copy = pltpu.make_async_remote_copy(
        src_ref=src,
        dst_ref=dst,
        send_sem=sems[0].at[index],
        recv_sem=sems[1].at[index],
        device_id=peer,
        device_id_type=MESH,
    )
    copy.start()
    return copy


class Spread:
    def __init__(self, block, half, me, n, right, left, sems, base):
        self.block, self.half, self.me, self.n, self.h = block, half, me, n, n // 2
        self.right, self.left, self.sems, self.base = right, left, sems, base
        self.copies = []

    def step(self, s):
        if s > 1:
            for copy in self.copies[-1]:
                copy.wait_recv()
        pair = []
        for way, peer in enumerate((self.right, self.left)):
            shift = self.n - (s - 1) if way == 0 else s - 1
            ref = self.block(rem(self.me + shift, self.n))
            if s == self.h:
                ref = self.half(ref, way)
            pair.append(send(ref, ref, self.sems, self.base + 2 * (s - 1) + way, peer))
        self.copies.append(pair)

    def end(self):
        for copy in self.copies[-1]:
            copy.wait_recv()

    def drain(self):
        for pair in self.copies:
            for copy in pair:
                copy.wait_send()


class Reduce:
    def __init__(self, block, rows, me, n, right, left, got, made, sems, base):
        self.block, self.rows, self.me, self.n, self.h = block, rows, me, n, n // 2
        self.peers, self.got, self.made, self.sems, self.base = (right, left), got, made, sems, base
        self.copies = []

    def step(self, s):
        pair = []
        for way, peer in enumerate(self.peers):
            far = self.h - s + 1
            own = self.block(rem(self.me + (far if way == 0 else self.n - far), self.n))
            part = pl.ds(way * (self.rows // 2), self.rows // 2)
            other = pl.ds((1 - way) * (self.rows // 2), self.rows // 2)
            got, made = self.got[way], self.made[way]
            if s == 1:
                src, dst = own.at[part], got.at[0, part]
            else:
                self.copies[-1][way].wait_recv()
                out, before = made.at[s - 1], got.at[s - 2]
                if s == 2:
                    out[part] = (own[part].astype(F32) + before[part].astype(F32)).astype(BF16)
                    out[other] = own[other]
                else:
                    out[...] = (own[...].astype(F32) + before[...].astype(F32)).astype(BF16)
                src, dst = out, got.at[s - 1]
            pair.append(send(src, dst, self.sems, self.base + 2 * (s - 1) + way, peer))
        self.copies.append(pair)

    def total(self):
        for copy in self.copies[-1]:
            copy.wait_recv()
        last = self.h - 1
        return (
            self.block(self.me)[...].astype(F32)
            + self.got[0][last].astype(F32)
            + self.got[1][last].astype(F32)
        )

    def drain(self):
        for pair in self.copies:
            for copy in pair:
                copy.wait_send()


def gather_kernel(
    inputs, w_key, values, queries, d_out, block_pos, keys, vals, qs, gs, turned, places,
    x_buf, w_buf, y_send, y_recv, x_send, x_recv, z_send, z_recv, load_sem,
):
    y, zh, x, t = place()
    load_x = pltpu.make_async_copy(inputs, x_buf, load_sem.at[0])
    load_w = pltpu.make_async_copy(w_key, w_buf, load_sem.at[1])
    load_x.start()
    load_w.start()
    up, down = device(rem(y + 1, NY), zh, x, t), device(rem(y + NY - 1, NY), zh, x, t)
    right, left = device(y, zh, rem(x + 1, NX), t), device(y, zh, rem(x + NX - 1, NX), t)
    partner = device(y, 1 - zh, x, t)
    lane = lax.broadcasted_iota(jnp.int32, (16, ROWS), 1)
    first = 2 * (zh * NY + y)
    mine = jnp.where(lane == first, block_pos[0], 0) + jnp.where(lane == first + 1, block_pos[1], 0)
    seat = KEY_BLOCKS + 2 * x
    here = jnp.where(lane == seat, block_pos[0], 0) + jnp.where(lane == seat + 1, block_pos[1], 0)
    vals[zh, y, 0:ROWS, :] = values[...]
    vals[zh, y, ROWS : ROWS + 16, :] = mine.astype(F32).astype(BF16)
    qs[x] = queries[...]
    gs[x, 0:ROWS, :] = d_out[...]
    gs[x, ROWS : ROWS + 16, 0:HD] = here.astype(F32).astype(BF16)
    gs[x, ROWS : ROWS + 16, HD:] = jnp.zeros((16, (GROUP - 1) * HD), BF16)
    meet((up, down, right, left, partner))

    y_sems, x_sems, z_sems = (y_send, y_recv), (x_send, x_recv), (z_send, z_recv)

    def half_k(ref, way):
        return ref.at[pl.ds(way * 64, 64)]

    def half_v(ref, way):
        return ref.at[pl.ds(0, 64)] if way == 0 else ref.at[pl.ds(64, ROWS + 16 - 64)]

    def ring_y(arr, half, z, base):
        return Spread(lambda o: arr.at[z, o], half, y, NY, up, down, y_sems, base)

    v_own, v_far = ring_y(vals, half_v, zh, 0), ring_y(vals, half_v, 1 - zh, 2 * HY)
    k_own, k_far = ring_y(keys, half_k, zh, 4 * HY), ring_y(keys, half_k, 1 - zh, 6 * HY)
    q_ring = Spread(lambda o: qs.at[o], half_k, x, NX, right, left, x_sems, 0)
    g_ring = Spread(lambda o: gs.at[o], half_v, x, NX, right, left, x_sems, 2 * HX)

    z_v = send(vals.at[zh, y], vals.at[zh, y], z_sems, 0, partner)
    v_own.step(1)
    q_ring.step(1)
    g_ring.step(1)
    load_x.wait()
    load_w.wait()
    keys[zh, y] = jnp.dot(x_buf[...], w_buf[...], preferred_element_type=F32).astype(BF16)
    z_k = send(keys.at[zh, y], keys.at[zh, y], z_sems, 1, partner)
    k_own.step(1)

    def turn(first, last):
        def body(j, carry):
            tile = x_buf[:, pl.ds(pl.multiple_of(j * 128, 128), 128)].T
            for part in range(2):
                b = 2 * j + part
                turned[rem(b, NX), lax.div(b, jnp.int32(NX))] = tile[part * 64 : part * 64 + 64]
            return carry

        lax.fori_loop(first, last, body, 0)

    tiles = inputs.shape[1] // 128
    turn(0, tiles // 4)
    z_v.wait_recv()
    v_far.step(1)
    v_own.step(2)
    z_k.wait_recv()
    k_far.step(1)
    k_own.step(2)
    turn(tiles // 4, tiles // 2)
    q_ring.step(2)
    g_ring.step(2)
    v_far.step(2)
    k_far.step(2)
    v_own.step(3)
    k_own.step(3)
    turn(tiles // 2, 3 * tiles // 4)
    v_far.step(3)
    k_far.step(3)
    v_own.step(4)
    k_own.step(4)
    turn(3 * tiles // 4, tiles)
    v_far.step(4)
    k_far.step(4)
    rings = (v_own, k_own, v_far, k_far, q_ring, g_ring)
    for ring in rings:
        ring.end()
    total = jnp.zeros((16, ROWS), F32)
    for z in range(NZ):
        for j in range(NY):
            total = total + vals[z, j, ROWS : ROWS + 16, :].astype(F32)
    for j in range(NX):
        total = total + gs[j, ROWS : ROWS + 16, 0:HD].astype(F32)
    places[...] = total[0:8].astype(jnp.int32)
    z_v.wait_send()
    z_k.wait_send()
    for ring in rings:
        ring.drain()


def live_keys(places, doc_lens, listed, query):
    starts = [jnp.int32(0)]
    for d in range(3):
        starts.append(starts[-1] + doc_lens[d])
    mine = places[0, KEY_BLOCKS + query]
    first_row = mine * BLK
    start = jnp.int32(0)
    for s in starts[1:]:
        start = jnp.where(s <= first_row, s, start)
    low = lax.div(start, jnp.int32(BLK))
    count = jnp.int32(0)
    for b in range(KEY_BLOCKS):
        pk = places[0, b]
        listed[count] = jnp.int32(b)
        count = count + ((pk <= mine) & (pk >= low)).astype(jnp.int32)
    for j in range(CHUNK):
        listed[count + j] = jnp.int32(0)
    row = first_row + (lax.broadcasted_iota(jnp.int32, (1, 2 * BLK), 1) & (BLK - 1))
    opens = jnp.zeros((1, 2 * BLK), jnp.int32)
    for s in starts[1:]:
        opens = jnp.where(s <= row, s, opens)
    return count, row, opens


def key_chunk(places, listed, count, chunk, keys, vals, row, opens):
    iota = lax.broadcasted_iota(jnp.int32, (BLK, 2 * BLK), 0)
    ks, vs, terms, blocks = [], [], [], []
    for j in range(CHUNK):
        at = chunk * CHUNK + j
        b = listed[at]
        base = jnp.where(at < count, places[0, b] * BLK, jnp.int32(1 << 20))
        ks.append(keys[pl.ds(pl.multiple_of(b * BLK, BLK), BLK), :])
        vs.append(vals[b >> 1, pl.ds(pl.multiple_of((b & 1) * BLK, BLK), BLK), :])
        ok = (iota >= opens - base) & (iota <= row - base)
        term = jnp.where(ok, 0.0, LOW)
        terms.append(jnp.concatenate([term, term], axis=1))
        blocks.append(b)
    return (
        jnp.concatenate(ks, axis=0),
        jnp.concatenate(vs, axis=0),
        jnp.concatenate(terms, axis=0),
        blocks,
    )


def head_stack(ref, query):
    rows = pl.ds(pl.multiple_of((query & 1) * BLK, BLK), BLK)
    return jnp.concatenate(
        [ref[query >> 1, rows, h * HD : (h + 1) * HD] for h in range(GROUP)], axis=0
    )


def stats_kernel(places, doc_lens, keys, vals, qs, gs, out, kept, listed):
    def visit(query, carry):
        count, row, opens = live_keys(places, doc_lens, listed, query)
        q, g = head_stack(qs, query), head_stack(gs, query)

        def chunk_step(chunk, state):
            top, mass, weighted = state
            k, v, term, _ = key_chunk(places, listed, count, chunk, keys, vals, row, opens)
            score = lax.dot_general(k, q, NT, preferred_element_type=F32) * LOG2 + term
            d_prob = lax.dot_general(v, g, NT, preferred_element_type=F32)
            new = jnp.maximum(top, jnp.max(score, axis=0, keepdims=True))
            e = jnp.exp2(score - new)
            shrink = jnp.exp2(top - new)
            return (
                new,
                mass * shrink + jnp.sum(e, axis=0, keepdims=True),
                weighted * shrink + jnp.sum(e * d_prob, axis=0, keepdims=True),
            )

        zero = jnp.zeros((1, STACK), F32)
        chunks = lax.div(count + (CHUNK - 1), jnp.int32(CHUNK))
        top, mass, weighted = lax.fori_loop(
            0, chunks, chunk_step, (jnp.full((1, STACK), FLOOR, F32), zero, zero)
        )
        kept[query, 0:1] = top
        kept[query, 1:2] = mass
        kept[query, 2:3] = weighted
        return carry

    lax.fori_loop(0, QUERY_BLOCKS, visit, 0)
    for part in range(3):
        out[part] = jnp.concatenate([kept[i, part : part + 1] for i in range(QUERY_BLOCKS)], axis=0)


def share_kernel(stats, out, got, send_sem, recv_sem):
    y, zh, x, t = place()
    peers = [device(y, zh, rem(x + j, NX), t) for j in range(1, NX)]
    meet(peers)
    copies = [send(stats, got.at[j], (send_sem, recv_sem), j, peer) for j, peer in enumerate(peers)]
    for copy in copies:
        copy.wait_recv()
    parts = [[stats[i] for i in range(3)]] + [[got[j, i] for i in range(3)] for j in range(NX - 1)]
    top = parts[0][0]
    for p in parts[1:]:
        top = jnp.maximum(top, p[0])
    mass = jnp.zeros_like(top)
    weighted = jnp.zeros_like(top)
    for p in parts:
        shrink = jnp.exp2(p[0] - top)
        mass = mass + p[1] * shrink
        weighted = weighted + p[2] * shrink
    out[0] = top
    out[1] = 1.0 / mass
    out[2] = weighted / mass
    for copy in copies:
        copy.wait_send()


def back_kernel(
    places, doc_lens, stats, keys, vals, qs, gs, dq, dk, dv, dk_sum, dv_sum, listed
):
    dk_sum[...] = jnp.zeros_like(dk_sum)
    dv_sum[...] = jnp.zeros_like(dv_sum)

    def visit(query, carry):
        count, row, opens = live_keys(places, doc_lens, listed, query)
        q, g = head_stack(qs, query), head_stack(gs, query)
        top, scale, delta = [stats[i, pl.ds(query, 1), :] for i in range(3)]

        def chunk_step(chunk, dq_sum):
            k, v, term, blocks = key_chunk(places, listed, count, chunk, keys, vals, row, opens)
            score = lax.dot_general(k, q, NT, preferred_element_type=F32) * LOG2 + term
            d_prob = lax.dot_general(v, g, NT, preferred_element_type=F32)
            prob = jnp.exp2(score - top) * scale
            d_score = (prob * (d_prob - delta)).astype(BF16)
            dv_part = jnp.dot(prob.astype(BF16), g, preferred_element_type=F32)
            dk_part = jnp.dot(d_score, q, preferred_element_type=F32)
            for j, b in enumerate(blocks):
                rows = pl.ds(pl.multiple_of(b * BLK, BLK), BLK)
                dv_sum[rows, :] += dv_part[j * BLK : (j + 1) * BLK]
                dk_sum[rows, :] += dk_part[j * BLK : (j + 1) * BLK]
            return dq_sum + jnp.dot(k.T, d_score, preferred_element_type=F32)

        chunks = lax.div(count + (CHUNK - 1), jnp.int32(CHUNK))
        dq_sum = lax.fori_loop(0, chunks, chunk_step, jnp.zeros((HD, STACK), F32))
        dq_rows = (dq_sum * SCALE).T.astype(BF16)
        rows = pl.ds(pl.multiple_of((query & 1) * BLK, BLK), BLK)
        for h in range(GROUP):
            dq[query >> 1, rows, h * HD : (h + 1) * HD] = dq_rows[h * BLK : (h + 1) * BLK]
        return carry

    lax.fori_loop(0, QUERY_BLOCKS, visit, 0)
    dk[...] = (dk_sum[...] * SCALE).astype(BF16)
    dv[...] = dv_sum[...].astype(BF16)


def reduce_kernel(
    nl, dq, dk, dv, turned, w_key, d_query, d_value, d_input, d_wkey,
    kv_got, kv_made, q_got, q_made, w_got, w_made, z_out, z_got, kg, kg_pair, xg, x_hop, w_own, w_pair,
    w_part, in_part, in_got, zw_out, zw_got,
    y_send, y_recv, x_send, x_recv, z_send, z_recv, s_send, s_recv, load_sem,
):
    y, zh, x, t = place()
    zl, core = lax.div(t, jnp.int32(NC)), rem(t, NC)
    up, down = device(rem(y + 1, NY), zh, x, t), device(rem(y + NY - 1, NY), zh, x, t)
    others_x = [device(y, zh, rem(x + j, NX), t) for j in range(1, NX)]
    right, left = others_x[0], others_x[-1]
    partner = device(y, 1 - zh, x, t)
    sibling = device(y, zh, x, zl * NC + 1 - core)
    others_l = [device(y, zh, x, rem(zl + j, nl) * NC + core) for j in range(1, nl)]
    x_sems, y_sems = (x_send, x_recv), (y_send, y_recv)
    z_sems, s_sems = (z_send, z_recv), (s_send, s_recv)

    own_x = pltpu.make_async_copy(turned.at[x], xg.at[x], load_sem.at[0])
    own_w = pltpu.make_async_copy(w_key.at[:, core], w_own, load_sem.at[1])
    own_x.start()
    own_w.start()
    meet([up, down, partner, sibling] + others_x + others_l)

    def ring(arr, z, j):
        return Reduce(
            lambda o: arr.at[z, o], ROWS, y, NY, up, down,
            (kv_got.at[j, 0], kv_got.at[j, 1]), (kv_made.at[j, 0], kv_made.at[j, 1]),
            y_sems, 2 * HY * j,
        )

    k_far, v_far = ring(dk, 1 - zh, 0), ring(dv, 1 - zh, 1)
    k_own, v_own = ring(dk, zh, 2), ring(dv, zh, 3)
    rings = (k_far, k_own, v_far, v_own)
    for r in rings:
        r.step(1)
    pairs = NZ * NY
    opposite = rem(x + 2, NX)
    x_next = send(turned.at[rem(x + 1, NX)], xg.at[x], x_sems, 0, right)
    x_prev = send(turned.at[rem(x + NX - 1, NX)], xg.at[x], x_sems, 1, left)
    lower, upper = pl.ds(0, pairs // 2), pl.ds(pairs // 2, pairs // 2)
    hop_right = send(turned.at[opposite, lower], x_hop.at[0], x_sems, 2, right)
    hop_left = send(turned.at[opposite, upper], x_hop.at[1], x_sems, 3, left)
    w_swap = send(w_key.at[:, 1 - core], w_pair, s_sems, 0, sibling)
    q_ring = Reduce(
        lambda o: dq.at[o], ROWS, x, NX, right, left,
        (q_got.at[0], q_got.at[1]), (q_made.at[0], q_made.at[1]), x_sems, 4,
    )
    q_ring.step(1)
    for r in rings:
        r.step(2)
    hop_right.wait_recv()
    far_right = send(x_hop.at[0], xg.at[rem(x + NX - 1, NX), lower], x_sems, 8, right)
    hop_left.wait_recv()
    far_left = send(x_hop.at[1], xg.at[rem(x + 1, NX), upper], x_sems, 9, left)
    for r in rings:
        r.step(3)
    q_ring.step(2)
    for r in rings:
        r.step(4)
    z_out[0] = k_far.total().astype(BF16)
    z_key = send(z_out.at[0], z_got.at[0], z_sems, 0, partner)
    key_sum = k_own.total()
    z_out[1] = v_far.total().astype(BF16)
    z_val = send(z_out.at[1], z_got.at[1], z_sems, 1, partner)
    z_key.wait_recv()
    kg[x] = (key_sum + z_got[0].astype(F32)).astype(BF16)

    kg_swap = send(kg.at[x], kg_pair, s_sems, 1, sibling)
    kg_sends = [send(kg.at[x], kg.at[x], x_sems, 9 + j, others_x[j - 1]) for j in range(1, NX)]

    own_w.wait()
    w_swap.wait_recv()
    kg_swap.wait_recv()
    in_sends = []
    mine, pair = kg[x], kg_pair[...]

    def in_block(owner):
        return lax.dot_general(
            mine, w_own[owner], NT, preferred_element_type=F32
        ) + lax.dot_general(pair, w_pair[owner], NT, preferred_element_type=F32)

    for j in range(1, nl):
        in_part[j - 1] = in_block(rem(zl + j, nl)).astype(BF16)
        in_sends.append(send(in_part.at[j - 1], in_got.at[j - 1], s_sems, 1 + j, others_l[j - 1]))

    own_x.wait()
    x_next.wait_recv()
    x_prev.wait_recv()
    far_right.wait_recv()
    far_left.wait_recv()
    for copy in kg_sends:
        copy.wait_recv()
    product = jnp.zeros((pairs * BLK, HD), F32)
    for src in range(NX):
        block = xg[src].reshape(pairs * BLK, ROWS)
        product = product + jnp.dot(block, kg[src], preferred_element_type=F32)
    w_part[...] = product.astype(BF16).reshape(NY, NZ * BLK, HD)
    w_ring = Reduce(
        lambda o: w_part.at[o], NZ * BLK, y, NY, up, down,
        (w_got.at[0], w_got.at[1]), (w_made.at[0], w_made.at[1]), y_sems, 8 * HY,
    )
    w_ring.step(1)
    z_val.wait_recv()
    d_value[...] = (v_own.total() + z_got[1].astype(F32)).astype(BF16)
    w_ring.step(2)
    d_query[...] = q_ring.total().astype(BF16)
    w_ring.step(3)
    in_sum = in_block(zl)
    w_ring.step(4)
    zw_out[...] = w_ring.total()
    z_w = send(
        zw_out.at[pl.ds(pl.multiple_of((1 - zh) * BLK, BLK), BLK)], zw_got, z_sems, 2, partner
    )
    for j, copy in enumerate(in_sends):
        copy.wait_recv()
        in_sum = in_sum + in_got[j].astype(F32)
    d_input[...] = in_sum.astype(BF16)
    z_w.wait_recv()
    d_wkey[...] = zw_out[pl.ds(pl.multiple_of(zh * BLK, BLK), BLK), :] + zw_got[...]

    for r in rings + (q_ring, w_ring):
        r.drain()
    last = [x_next, x_prev, hop_right, hop_left, far_right, far_left, w_swap, z_key, z_val, kg_swap, z_w]
    for copy in last + kg_sends + in_sends:
        copy.wait_send()


def dma(n):
    return pltpu.SemaphoreType.DMA((n,))


def params(collective_id=None):
    return pltpu.CompilerParams(
        collective_id=collective_id,
        has_side_effects=collective_id is not None,
        vmem_limit_bytes=VMEM_LIMIT,
    )


def on_device(nl, inputs, w_key, values, queries, d_out, doc_lens, block_pos):
    width = inputs.shape[1]
    pairs = NZ * NY
    shape = jax.ShapeDtypeStruct
    keys, vals, qs, gs, turned, places = pl.pallas_call(
        gather_kernel,
        out_shape=(
            shape((NZ, NY, ROWS, HD), BF16),
            shape((NZ, NY, ROWS + 16, HD), BF16),
            shape((NX, ROWS, GROUP * HD), BF16),
            shape((NX, ROWS + 16, GROUP * HD), BF16),
            shape((NX, pairs, BLK, ROWS), BF16),
            shape((8, ROWS), jnp.int32),
        ),
        in_specs=[anywhere, anywhere, vmem, vmem, vmem, smem],
        out_specs=(vmem,) * 6,
        scratch_shapes=[
            pltpu.VMEM((ROWS, width), BF16),
            pltpu.VMEM((width, HD), BF16),
            dma(8 * HY), dma(8 * HY), dma(4 * HX), dma(4 * HX), dma(2), dma(2), dma(2),
        ],
        compiler_params=params(1),
        name="gather_rows",
    )(inputs, w_key, values, queries, d_out, block_pos)
    keys = keys.reshape(KEY_BLOCKS * BLK, HD)
    vals = vals.reshape(pairs, ROWS + 16, HD)
    stats = pl.pallas_call(
        stats_kernel,
        out_shape=shape((3, QUERY_BLOCKS, STACK), F32),
        in_specs=[smem, smem, vmem, vmem, vmem, vmem],
        out_specs=vmem,
        scratch_shapes=[
            pltpu.VMEM((QUERY_BLOCKS, 8, STACK), F32),
            pltpu.SMEM((KEY_BLOCKS + CHUNK,), jnp.int32),
        ],
        compiler_params=params(),
        name="row_stats",
    )(places, doc_lens, keys, vals, qs, gs)
    stats = pl.pallas_call(
        share_kernel,
        out_shape=shape((3, QUERY_BLOCKS, STACK), F32),
        in_specs=[vmem],
        out_specs=vmem,
        scratch_shapes=[
            pltpu.VMEM((NX - 1, 3, QUERY_BLOCKS, STACK), F32), dma(NX - 1), dma(NX - 1),
        ],
        compiler_params=params(2),
        name="share_stats",
    )(stats)
    dq, dk, dv = pl.pallas_call(
        back_kernel,
        out_shape=(
            shape((NX, ROWS, GROUP * HD), BF16),
            shape((KEY_BLOCKS * BLK, HD), BF16),
            shape((KEY_BLOCKS * BLK, HD), BF16),
        ),
        in_specs=[smem, smem, vmem, vmem, vmem, vmem, vmem],
        out_specs=(vmem,) * 3,
        scratch_shapes=[
            pltpu.VMEM((KEY_BLOCKS * BLK, HD), F32),
            pltpu.VMEM((KEY_BLOCKS * BLK, HD), F32),
            pltpu.SMEM((KEY_BLOCKS + CHUNK,), jnp.int32),
        ],
        compiler_params=params(),
        name="back_tiles",
    )(places, doc_lens, stats, keys, vals, qs, gs)
    slice_width = width // (nl * NC)
    w_split = w_key.reshape(nl, NC, slice_width, HD)
    block = (ROWS, HD)
    return pl.pallas_call(
        functools.partial(reduce_kernel, nl),
        out_shape=(
            shape((ROWS, GROUP * HD), BF16),
            shape((ROWS, HD), BF16),
            shape((ROWS, slice_width), BF16),
            shape((BLK, HD), F32),
        ),
        in_specs=[vmem, vmem, vmem, anywhere, anywhere],
        out_specs=(vmem,) * 4,
        scratch_shapes=[
            pltpu.VMEM((4, 2, HY) + block, BF16),
            pltpu.VMEM((4, 2, HY) + block, BF16),
            pltpu.VMEM((2, HX, ROWS, GROUP * HD), BF16),
            pltpu.VMEM((2, HX, ROWS, GROUP * HD), BF16),
            pltpu.VMEM((2, HY) + block, BF16),
            pltpu.VMEM((2, HY) + block, BF16),
            pltpu.VMEM((2,) + block, BF16),
            pltpu.VMEM((2,) + block, BF16),
            pltpu.VMEM((NX,) + block, BF16),
            pltpu.VMEM(block, BF16),
            pltpu.VMEM((NX, pairs, BLK, ROWS), BF16),
            pltpu.VMEM((2, pairs // 2, BLK, ROWS), BF16),
            pltpu.VMEM((nl, slice_width, HD), BF16),
            pltpu.VMEM((nl, slice_width, HD), BF16),
            pltpu.VMEM((NY,) + block, BF16),
            pltpu.VMEM((nl - 1, ROWS, slice_width), BF16),
            pltpu.VMEM((nl - 1, ROWS, slice_width), BF16),
            pltpu.VMEM(block, F32),
            pltpu.VMEM((BLK, HD), F32),
            dma(10 * HY), dma(10 * HY), dma(13), dma(13), dma(3), dma(3), dma(1 + nl), dma(1 + nl), dma(2),
        ],
        compiler_params=params(3),
        name="reduce_grads",
    )(dq, dk.reshape(NZ, NY, ROWS, HD), dv.reshape(NZ, NY, ROWS, HD), turned, w_split)


def solution(mesh):
    nl = mesh.shape["tensor"] // NC
    return jax.shard_map(
        functools.partial(on_device, nl),
        mesh=mesh,
        in_specs=(
            P("dp", None),
            P(None, "tensor"),
            P("dp", "tensor"),
            P("dp", "tensor"),
            P("dp", "tensor"),
            P(),
            P("dp"),
        ),
        out_specs=(P("dp", "tensor"), P("dp", "tensor"), P("dp", "tensor"), P("dp", "tensor")),
        check_vma=False,
    )
```

```python
import functools
import math

import jax
import jax.numpy as jnp
from jax import lax
from jax.experimental import pallas as pl
from jax.experimental.pallas import tpu as pltpu
from jax.sharding import PartitionSpec as P

MESH = pl.DeviceIdType.MESH
F32, BF16 = jnp.float32, jnp.bfloat16
HD, BLK, GROUP, ROWS = 128, 64, 4, 128
NX, NZ, NY, NC = 4, 2, 8, 2
HY, HX = NY // 2, NX // 2
KEY_BLOCKS = 2 * NZ * NY
QUERY_BLOCKS = 2 * NX
STACK = GROUP * BLK
CHUNK = 4
SCALE = 1.0 / math.sqrt(HD)
LOG2 = SCALE / math.log(2.0)
LOW = -1e30
FLOOR = -1e29
NT = (((1,), (1,)), ((), ()))
VMEM_LIMIT = 40 * 1024 * 1024

vmem = pl.BlockSpec(memory_space=pltpu.VMEM)
smem = pl.BlockSpec(memory_space=pltpu.SMEM)
hbm = pl.BlockSpec(memory_space=pltpu.HBM)


def rem(a, n):
    return lax.rem(a, jnp.int32(n))


def place():
    dp, tensor = lax.axis_index("dp"), lax.axis_index("tensor")
    x = rem(dp, NX)
    rest = lax.div(dp, jnp.int32(NX))
    return lax.div(rest, jnp.int32(NZ)), rem(rest, NZ), x, tensor


def device(y, zh, x, tensor):
    return ((y * NZ + zh) * NX + x, tensor)


def meet(peers):
    barrier = pltpu.get_barrier_semaphore()
    for peer in peers:
        pl.semaphore_signal(barrier, inc=1, device_id=peer, device_id_type=MESH)
    pl.semaphore_wait(barrier, len(peers))


def send(src, dst, sems, index, peer):
    copy = pltpu.make_async_remote_copy(
        src_ref=src,
        dst_ref=dst,
        send_sem=sems[0].at[index],
        recv_sem=sems[1].at[index],
        device_id=peer,
        device_id_type=MESH,
    )
    copy.start()
    return copy


class Spread:
    def __init__(self, block, half, me, n, right, left, sems, base):
        self.block, self.half, self.me, self.n, self.h = block, half, me, n, n // 2
        self.right, self.left, self.sems, self.base = right, left, sems, base
        self.copies = []

    def step(self, s):
        if s > 1:
            for copy in self.copies[-1]:
                copy.wait_recv()
        pair = []
        for way, peer in enumerate((self.right, self.left)):
            shift = self.n - (s - 1) if way == 0 else s - 1
            ref = self.block(rem(self.me + shift, self.n))
            if s == self.h:
                ref = self.half(ref, way)
            pair.append(send(ref, ref, self.sems, self.base + 2 * (s - 1) + way, peer))
        self.copies.append(pair)

    def end(self):
        for copy in self.copies[-1]:
            copy.wait_recv()

    def drain(self):
        for pair in self.copies:
            for copy in pair:
                copy.wait_send()


class Reduce:
    def __init__(self, block, rows, me, n, right, left, got, made, sems, base):
        self.block, self.rows, self.me, self.n, self.h = block, rows, me, n, n // 2
        self.peers, self.got, self.made, self.sems, self.base = (right, left), got, made, sems, base
        self.copies = []

    def step(self, s):
        pair = []
        for way, peer in enumerate(self.peers):
            far = self.h - s + 1
            own = self.block(rem(self.me + (far if way == 0 else self.n - far), self.n))
            part = pl.ds(way * (self.rows // 2), self.rows // 2)
            other = pl.ds((1 - way) * (self.rows // 2), self.rows // 2)
            got, made = self.got[way], self.made[way]
            if s == 1:
                src, dst = own.at[part], got.at[0, part]
            else:
                self.copies[-1][way].wait_recv()
                out, before = made.at[s - 1], got.at[s - 2]
                if s == 2:
                    out[part] = (own[part].astype(F32) + before[part].astype(F32)).astype(BF16)
                    out[other] = own[other]
                else:
                    out[...] = (own[...].astype(F32) + before[...].astype(F32)).astype(BF16)
                src, dst = out, got.at[s - 1]
            pair.append(send(src, dst, self.sems, self.base + 2 * (s - 1) + way, peer))
        self.copies.append(pair)

    def end(self):
        for copy in self.copies[-1]:
            copy.wait_recv()

    def total(self, z):
        last = self.h - 1
        return (
            self.block(self.me)[z].astype(F32)
            + self.got[0][last, z].astype(F32)
            + self.got[1][last, z].astype(F32)
        )

    def drain(self):
        for pair in self.copies:
            for copy in pair:
                copy.wait_send()


class Tree:
    def __init__(self, block, half, me, n, ups, downs, sems, base):
        self.block, self.half, self.me, self.n = block, half, me, n
        self.ups, self.downs, self.sems, self.base = ups, downs, sems, base

    def first(self):
        own = self.block(self.me)
        self.near = [
            send(own, own, self.sems, self.base + i, peer)
            for i, peer in enumerate((self.ups[1], self.downs[1], self.ups[0], self.downs[0]))
        ]

    def second(self):
        self.far = []
        for way, peers in enumerate((self.ups, self.downs)):
            self.near[way].wait_recv()
            ref = self.block(rem(self.me + (self.n - 2 if way == 0 else 2), self.n))
            half = self.half(ref, way)
            self.far.append(send(half, half, self.sems, self.base + 4 + 2 * way, peers[1]))
            self.far.append(send(ref, ref, self.sems, self.base + 5 + 2 * way, peers[0]))

    def end(self):
        for copy in self.near[2:] + self.far:
            copy.wait_recv()

    def drain(self):
        for copy in self.near + self.far:
            copy.wait_send()


def gather_kernel(
    inputs, w_key, values, queries, d_out, doc_lens, block_pos, keys, vals, qs, gs, turned, places,
    x_buf, w_buf, docs, pos, y_send, y_recv, x_send, x_recv, z_send, z_recv, load_sem,
):
    y, zh, x, t = place()
    loads = [
        pltpu.make_async_copy(src, dst, load_sem.at[i])
        for i, (src, dst) in enumerate(
            (
                (block_pos, pos),
                (values, vals.at[zh, y, pl.ds(0, ROWS)]),
                (queries, qs.at[x]),
                (d_out, gs.at[x, pl.ds(0, ROWS)]),
                (w_key, w_buf),
                (inputs, x_buf),
                (doc_lens, docs),
            )
        )
    ]
    for load in loads:
        load.start()
    ups = [device(rem(y + j, NY), zh, x, t) for j in (1, 2)]
    downs = [device(rem(y + NY - j, NY), zh, x, t) for j in (1, 2)]
    others_x = [device(y, zh, rem(x + j, NX), t) for j in range(1, NX)]
    partner = device(y, 1 - zh, x, t)
    loads[0].wait()
    lane = lax.broadcasted_iota(jnp.int32, (16, ROWS), 1)
    first = 2 * (zh * NY + y)
    mine = jnp.where(lane == first, pos[0], 0) + jnp.where(lane == first + 1, pos[1], 0)
    seat = KEY_BLOCKS + 2 * x
    here = jnp.where(lane == seat, pos[0], 0) + jnp.where(lane == seat + 1, pos[1], 0)
    vals[zh, y, ROWS : ROWS + 16, :] = mine.astype(F32).astype(BF16)
    gs[x, ROWS : ROWS + 16, 0:HD] = here.astype(F32).astype(BF16)
    gs[x, ROWS : ROWS + 16, HD:] = jnp.zeros((16, (GROUP - 1) * HD), BF16)
    loads[1].wait()
    meet(ups + downs + others_x + [partner])

    y_sems, x_sems, z_sems = (y_send, y_recv), (x_send, x_recv), (z_send, z_recv)

    def half_k(ref, way):
        return ref.at[pl.ds(way * 64, 64)]

    def half_v(ref, way):
        return ref.at[pl.ds(0, 64)] if way == 0 else ref.at[pl.ds(64, ROWS + 16 - 64)]

    def ring(arr, half, base):
        return Spread(lambda o: arr.at[zh, o], half, y, NY, ups[0], downs[0], y_sems, base)

    def tree(arr, half, base):
        return Tree(lambda o: arr.at[1 - zh, o], half, y, NY, ups, downs, y_sems, base)

    v_own, k_own = ring(vals, half_v, 0), ring(keys, half_k, 8)
    v_far, k_far = tree(vals, half_v, 16), tree(keys, half_k, 24)

    z_v = send(vals.at[zh, y], vals.at[zh, y], z_sems, 0, partner)
    v_own.step(1)
    loads[4].wait()
    loads[5].wait()
    keys[zh, y] = jnp.dot(x_buf[...], w_buf[...], preferred_element_type=F32).astype(BF16)
    z_k = send(keys.at[zh, y], keys.at[zh, y], z_sems, 1, partner)
    k_own.step(1)
    loads[2].wait()
    loads[3].wait()
    sideways = []
    for j in (2, 1, 3):
        sideways.append(send(gs.at[x], gs.at[x], x_sems, j - 1, others_x[j - 1]))
        sideways.append(send(qs.at[x], qs.at[x], x_sems, j + 2, others_x[j - 1]))

    def turn(first, last):
        def body(j, carry):
            tile = x_buf[:, pl.ds(pl.multiple_of(j * 128, 128), 128)].T
            for part in range(2):
                b = 2 * j + part
                turned[rem(b, NX), lax.div(b, jnp.int32(NX))] = tile[part * 64 : part * 64 + 64]
            return carry

        lax.fori_loop(first, last, body, 0)

    tiles = inputs.shape[1] // 128
    turn(0, tiles // 4)
    v_own.step(2)
    k_own.step(2)
    z_v.wait_recv()
    v_far.first()
    v_own.step(3)
    z_k.wait_recv()
    k_far.first()
    k_own.step(3)
    turn(tiles // 4, tiles // 2)
    v_far.second()
    v_own.step(4)
    k_far.second()
    k_own.step(4)
    turn(tiles // 2, tiles)
    loads[6].wait()
    rings = (v_own, k_own, v_far, k_far)
    for r in rings:
        r.end()
    for copy in sideways:
        copy.wait_recv()
    total = jnp.zeros((16, ROWS), F32)
    for z in range(NZ):
        for j in range(NY):
            total = total + vals[z, j, ROWS : ROWS + 16, :].astype(F32)
    for j in range(NX):
        total = total + gs[j, ROWS : ROWS + 16, 0:HD].astype(F32)
    seats = lax.broadcasted_iota(jnp.int32, (8, ROWS), 1)
    lengths = jnp.zeros((8, ROWS), jnp.int32)
    for d in range(4):
        lengths = lengths + jnp.where(seats == d, docs[d], 0)
    rows = lax.broadcasted_iota(jnp.int32, (8, ROWS), 0)
    places[...] = jnp.where(rows == 1, lengths, total[0:8].astype(jnp.int32))
    z_v.wait_send()
    z_k.wait_send()
    for r in rings:
        r.drain()
    for copy in sideways:
        copy.wait_send()


def live_keys(places, listed, query):
    starts = [jnp.int32(0)]
    for d in range(3):
        starts.append(starts[-1] + places[1, d])
    mine = places[0, KEY_BLOCKS + query]
    first_row = mine * BLK
    start = jnp.int32(0)
    for s in starts[1:]:
        start = jnp.where(s <= first_row, s, start)
    low = lax.div(start, jnp.int32(BLK))
    count = jnp.int32(0)
    for b in range(KEY_BLOCKS):
        pk = places[0, b]
        listed[count] = jnp.int32(b)
        count = count + ((pk <= mine) & (pk >= low)).astype(jnp.int32)
    for j in range(CHUNK):
        listed[count + j] = jnp.int32(0)
    row = first_row + (lax.broadcasted_iota(jnp.int32, (1, 2 * BLK), 1) & (BLK - 1))
    opens = jnp.zeros((1, 2 * BLK), jnp.int32)
    for s in starts[1:]:
        opens = jnp.where(s <= row, s, opens)
    return count, row, opens


def key_chunk(places, listed, count, chunk, keys, vals, row, opens):
    iota = lax.broadcasted_iota(jnp.int32, (BLK, 2 * BLK), 0)
    ks, vs, terms, blocks = [], [], [], []
    for j in range(CHUNK):
        at = chunk * CHUNK + j
        b = listed[at]
        base = jnp.where(at < count, places[0, b] * BLK, jnp.int32(1 << 20))
        ks.append(keys[pl.ds(pl.multiple_of(b * BLK, BLK), BLK), :])
        vs.append(vals[b >> 1, pl.ds(pl.multiple_of((b & 1) * BLK, BLK), BLK), :])
        ok = (iota >= opens - base) & (iota <= row - base)
        term = jnp.where(ok, 0.0, LOW)
        terms.append(jnp.concatenate([term, term], axis=1))
        blocks.append(b)
    return (
        jnp.concatenate(ks, axis=0),
        jnp.concatenate(vs, axis=0),
        jnp.concatenate(terms, axis=0),
        blocks,
    )


def head_stack(ref, query):
    rows = pl.ds(pl.multiple_of((query & 1) * BLK, BLK), BLK)
    return jnp.concatenate(
        [ref[query >> 1, rows, h * HD : (h + 1) * HD] for h in range(GROUP)], axis=0
    )


def stats_kernel(places, keys, vals, qs, gs, out, kept, listed):
    def visit(query, carry):
        count, row, opens = live_keys(places, listed, query)
        q, g = head_stack(qs, query), head_stack(gs, query)

        def chunk_step(chunk, state):
            top, mass, weighted = state
            k, v, term, _ = key_chunk(places, listed, count, chunk, keys, vals, row, opens)
            score = lax.dot_general(k, q, NT, preferred_element_type=F32) * LOG2 + term
            d_prob = lax.dot_general(v, g, NT, preferred_element_type=F32)
            new = jnp.maximum(top, jnp.max(score, axis=0, keepdims=True))
            e = jnp.exp2(score - new)
            shrink = jnp.exp2(top - new)
            return (
                new,
                mass * shrink + jnp.sum(e, axis=0, keepdims=True),
                weighted * shrink + jnp.sum(e * d_prob, axis=0, keepdims=True),
            )

        zero = jnp.zeros((1, STACK), F32)
        chunks = lax.div(count + (CHUNK - 1), jnp.int32(CHUNK))
        top, mass, weighted = lax.fori_loop(
            0, chunks, chunk_step, (jnp.full((1, STACK), FLOOR, F32), zero, zero)
        )
        kept[query, 0:1] = top
        kept[query, 1:2] = mass
        kept[query, 2:3] = weighted
        return carry

    lax.fori_loop(0, QUERY_BLOCKS, visit, 0)
    for part in range(3):
        out[part] = jnp.concatenate([kept[i, part : part + 1] for i in range(QUERY_BLOCKS)], axis=0)


def share_kernel(stats, out, got, send_sem, recv_sem):
    y, zh, x, t = place()
    peers = [device(y, zh, rem(x + j, NX), t) for j in range(1, NX)]
    meet(peers)
    copies = [send(stats, got.at[j], (send_sem, recv_sem), j, peer) for j, peer in enumerate(peers)]
    for copy in copies:
        copy.wait_recv()
    parts = [[stats[i] for i in range(3)]] + [[got[j, i] for i in range(3)] for j in range(NX - 1)]
    top = parts[0][0]
    for p in parts[1:]:
        top = jnp.maximum(top, p[0])
    mass = jnp.zeros_like(top)
    weighted = jnp.zeros_like(top)
    for p in parts:
        shrink = jnp.exp2(p[0] - top)
        mass = mass + p[1] * shrink
        weighted = weighted + p[2] * shrink
    out[0] = top
    out[1] = 1.0 / mass
    out[2] = weighted / mass
    for copy in copies:
        copy.wait_send()


def back_kernel(
    places, stats, keys, vals, qs, gs, dq, dk, dv, dk_sum, dv_sum, listed
):
    dk_sum[...] = jnp.zeros_like(dk_sum)
    dv_sum[...] = jnp.zeros_like(dv_sum)

    def visit(query, carry):
        count, row, opens = live_keys(places, listed, query)
        q, g = head_stack(qs, query), head_stack(gs, query)
        top, scale, delta = [stats[i, pl.ds(query, 1), :] for i in range(3)]

        def chunk_step(chunk, dq_sum):
            k, v, term, blocks = key_chunk(places, listed, count, chunk, keys, vals, row, opens)
            score = lax.dot_general(k, q, NT, preferred_element_type=F32) * LOG2 + term
            d_prob = lax.dot_general(v, g, NT, preferred_element_type=F32)
            prob = jnp.exp2(score - top) * scale
            d_score = (prob * (d_prob - delta)).astype(BF16)
            dv_part = jnp.dot(prob.astype(BF16), g, preferred_element_type=F32)
            dk_part = jnp.dot(d_score, q, preferred_element_type=F32)
            for j, b in enumerate(blocks):
                rows = pl.ds(pl.multiple_of(b * BLK, BLK), BLK)
                dv_sum[rows, :] += dv_part[j * BLK : (j + 1) * BLK]
                dk_sum[rows, :] += dk_part[j * BLK : (j + 1) * BLK]
            return dq_sum + jnp.dot(k.T, d_score, preferred_element_type=F32)

        chunks = lax.div(count + (CHUNK - 1), jnp.int32(CHUNK))
        dq_sum = lax.fori_loop(0, chunks, chunk_step, jnp.zeros((HD, STACK), F32))
        dq_rows = (dq_sum * SCALE).T.astype(BF16)
        rows = pl.ds(pl.multiple_of((query & 1) * BLK, BLK), BLK)
        for h in range(GROUP):
            dq[query >> 1, rows, h * HD : (h + 1) * HD] = dq_rows[h * BLK : (h + 1) * BLK]
        return carry

    lax.fori_loop(0, QUERY_BLOCKS, visit, 0)
    dk[...] = (dk_sum[...] * SCALE).astype(BF16)
    dv[...] = dv_sum[...].astype(BF16)


class Fold:
    def __init__(self, block, me, n, ups, downs, got_far, got_half, got_near, made, got_last, sems):
        self.block, self.me, self.n, self.peers, self.sems = block, me, n, (ups, downs), sems
        self.got_far, self.got_half, self.got_near = got_far, got_half, got_near
        self.made, self.got_last = made, got_last

    def at(self, way, far):
        return self.block(rem(self.me + (far if way == 0 else self.n - far), self.n))

    def first(self):
        self.far, self.half, self.near = [], [], []
        for way, peers in enumerate(self.peers):
            src = self.at(way, 4).at[way]
            self.half.append(send(src, self.got_half.at[way], self.sems, way, peers[1]))
            self.far.append(send(self.at(way, 3), self.got_far.at[way], self.sems, 2 + way, peers[0]))
        for way, peers in enumerate(self.peers):
            self.near.append(send(self.at(way, 1), self.got_near.at[way], self.sems, 4 + way, peers[0]))

    def second(self):
        self.last = []
        for way, peers in enumerate(self.peers):
            self.far[way].wait_recv()
            self.half[way].wait_recv()
            own, far, out = self.at(way, 2), self.got_far.at[way], self.made.at[way]
            out[1 - way] = (own[1 - way].astype(F32) + far[1 - way].astype(F32)).astype(BF16)
            out[way] = (
                own[way].astype(F32) + far[way].astype(F32) + self.got_half[way].astype(F32)
            ).astype(BF16)
            self.last.append(send(out, self.got_last.at[way], self.sems, 6 + way, peers[1]))

    def end(self):
        for copy in self.near + self.last:
            copy.wait_recv()

    def total(self, z):
        out = self.block(self.me)[z].astype(F32)
        for way in range(2):
            out = out + self.got_near[way, z].astype(F32) + self.got_last[way, z].astype(F32)
        return out

    def drain(self):
        for copy in self.far + self.half + self.near + self.last:
            copy.wait_send()


def reduce_kernel(
    nl, dq, dk, dv, turned, w_key, d_query, d_value, d_input, d_wkey,
    k_far, k_half, k_near, k_made, k_last, v_got, v_made, q_got, w_got, z_out, z_got,
    kg, kg_pair, xg, w_own, w_pair, w_part, in_part, in_got, zw_out, zw_got,
    k_send, k_recv, v_send, v_recv, w_send, w_recv, x_send, x_recv, z_send, z_recv, s_send, s_recv, load_sem,
):
    y, zh, x, t = place()
    zl, core = lax.div(t, jnp.int32(NC)), rem(t, NC)
    others_y = [device(rem(y + j, NY), zh, x, t) for j in range(1, NY)]
    ups, downs = others_y[:2], [others_y[-1], others_y[-2]]
    others_x = [device(y, zh, rem(x + j, NX), t) for j in range(1, NX)]
    partner = device(y, 1 - zh, x, t)
    sibling = device(y, zh, x, zl * NC + 1 - core)
    others_l = [device(y, zh, x, rem(zl + j, nl) * NC + core) for j in range(1, nl)]
    x_sems, z_sems, s_sems = (x_send, x_recv), (z_send, z_recv), (s_send, s_recv)

    own_x = pltpu.make_async_copy(turned.at[x], xg.at[x], load_sem.at[0])
    own_w = pltpu.make_async_copy(w_key.at[:, core], w_own, load_sem.at[1])
    own_x.start()
    own_w.start()
    meet(others_y + others_x + others_l + [partner, sibling])

    fold = Fold(
        lambda o: dk.at[:, o], y, NY, ups, downs, k_far, k_half, k_near, k_made, k_last, (k_send, k_recv)
    )
    fold.first()
    x_sends = [
        send(turned.at[rem(x + j, NX)], xg.at[x], x_sems, j - 1, others_x[j - 1]) for j in (2, 1, 3)
    ]
    w_swap = send(w_key.at[:, 1 - core], w_pair, s_sems, 0, sibling)
    v_ring = Reduce(
        lambda o: dv.at[:, o], NZ, y, NY, ups[0], downs[0],
        (v_got.at[0], v_got.at[1]), (v_made.at[0], v_made.at[1]), (v_send, v_recv), 0,
    )
    fold.second()
    v_ring.step(1)
    fold.end()
    z_out[0] = fold.total(1 - zh).astype(BF16)
    z_key = send(z_out.at[0], z_got.at[0], z_sems, 0, partner)
    v_ring.step(2)
    key_sum = fold.total(zh)
    v_ring.step(3)
    z_key.wait_recv()
    kg[x] = (key_sum + z_got[0].astype(F32)).astype(BF16)

    kg_swap = send(kg.at[x], kg_pair, s_sems, 1, sibling)
    kg_sends = [send(kg.at[x], kg.at[x], x_sems, 2 + j, others_x[j - 1]) for j in (2, 1, 3)]
    q_sends = [
        send(dq.at[rem(x + j, NX)], q_got.at[j - 1], x_sems, 5 + j, others_x[j - 1]) for j in (2, 1, 3)
    ]

    own_w.wait()
    w_swap.wait_recv()
    kg_swap.wait_recv()
    mine, pair = kg[x], kg_pair[...]

    def in_block(owner):
        return lax.dot_general(
            mine, w_own[owner], NT, preferred_element_type=F32
        ) + lax.dot_general(pair, w_pair[owner], NT, preferred_element_type=F32)

    in_sends = []
    for j in (2, 1, 3):
        in_part[j - 1] = in_block(rem(zl + j, nl)).astype(BF16)
        in_sends.append(send(in_part.at[j - 1], in_got.at[j - 1], s_sems, 1 + j, others_l[j - 1]))
    v_ring.step(4)

    own_x.wait()
    for copy in x_sends + kg_sends:
        copy.wait_recv()
    heads = [kg[src] for src in range(NX)]

    def w_block(owner):
        out = jnp.zeros((NZ * BLK, HD), F32)
        for src in range(NX):
            rows = xg[src, pl.ds(owner * NZ, NZ)].reshape(NZ * BLK, ROWS)
            out = out + jnp.dot(rows, heads[src], preferred_element_type=F32)
        return out

    w_sends = []
    for j in (4, 3, 5, 2, 6, 1, 7):
        w_part[j - 1] = w_block(rem(y + j, NY)).astype(BF16)
        w_sends.append(send(w_part.at[j - 1], w_got.at[j - 1], (w_send, w_recv), j - 1, others_y[j - 1]))
    zw_out[...] = w_block(y)
    v_ring.end()
    z_out[1] = v_ring.total(1 - zh).astype(BF16)
    z_val = send(z_out.at[1], z_got.at[1], z_sems, 1, partner)
    in_sum = in_block(zl)
    for copy in w_sends:
        copy.wait_recv()
    w_sum = zw_out[...]
    for j in range(NY - 1):
        w_sum = w_sum + w_got[j].astype(F32)
    zw_out[...] = w_sum
    z_w = send(
        zw_out.at[pl.ds(pl.multiple_of((1 - zh) * BLK, BLK), BLK)], zw_got, z_sems, 2, partner
    )
    q_sum = dq[x].astype(F32)
    for j, copy in enumerate(q_sends):
        copy.wait_recv()
    for j in range(NX - 1):
        q_sum = q_sum + q_got[j].astype(F32)
    d_query[...] = q_sum.astype(BF16)
    for copy in in_sends:
        copy.wait_recv()
    for j in range(nl - 1):
        in_sum = in_sum + in_got[j].astype(F32)
    d_input[...] = in_sum.astype(BF16)
    z_val.wait_recv()
    d_value[...] = (v_ring.total(zh) + z_got[1].astype(F32)).astype(BF16)
    z_w.wait_recv()
    d_wkey[...] = zw_out[pl.ds(pl.multiple_of(zh * BLK, BLK), BLK), :] + zw_got[...]

    fold.drain()
    v_ring.drain()
    for copy in [w_swap, z_key, z_val, kg_swap, z_w] + x_sends + kg_sends + q_sends + in_sends + w_sends:
        copy.wait_send()


def dma(n):
    return pltpu.SemaphoreType.DMA((n,))


def params(collective_id=None):
    return pltpu.CompilerParams(
        collective_id=collective_id,
        has_side_effects=collective_id is not None,
        vmem_limit_bytes=VMEM_LIMIT,
    )


def in_hbm(array):
    return pltpu.with_memory_space_constraint(array, pltpu.HBM)


def hand_over_kernel(*refs):
    n = (len(refs) - 1) // 2
    copies = [
        pltpu.make_async_copy(refs[i], refs[n + i], refs[-1].at[i]) for i in range(n)
    ]
    for copy in copies:
        copy.start()
    for copy in copies:
        copy.wait()


def on_device(nl, inputs, w_key, values, queries, d_out, doc_lens, block_pos):
    width = inputs.shape[1]
    pairs = NZ * NY
    shape = jax.ShapeDtypeStruct
    keys, vals, qs, gs, turned, places = pl.pallas_call(
        gather_kernel,
        out_shape=(
            shape((NZ, NY, ROWS, HD), BF16),
            shape((NZ, NY, ROWS + 16, HD), BF16),
            shape((NX, ROWS, GROUP * HD), BF16),
            shape((NX, ROWS + 16, GROUP * HD), BF16),
            shape((NX, pairs, BLK, ROWS), BF16),
            shape((8, ROWS), jnp.int32),
        ),
        in_specs=[hbm] * 7,
        out_specs=(vmem,) * 6,
        scratch_shapes=[
            pltpu.VMEM((ROWS, width), BF16),
            pltpu.VMEM((width, HD), BF16),
            pltpu.SMEM((4,), jnp.int32),
            pltpu.SMEM((2,), jnp.int32),
            dma(32), dma(32), dma(6), dma(6), dma(2), dma(2), dma(7),
        ],
        compiler_params=params(1),
        name="gather_rows",
    )(*(in_hbm(a) for a in (inputs, w_key, values, queries, d_out, doc_lens, block_pos)))
    keys = keys.reshape(KEY_BLOCKS * BLK, HD)
    vals = vals.reshape(pairs, ROWS + 16, HD)
    stats = pl.pallas_call(
        stats_kernel,
        out_shape=shape((3, QUERY_BLOCKS, STACK), F32),
        in_specs=[smem, vmem, vmem, vmem, vmem],
        out_specs=vmem,
        scratch_shapes=[
            pltpu.VMEM((QUERY_BLOCKS, 8, STACK), F32),
            pltpu.SMEM((KEY_BLOCKS + CHUNK,), jnp.int32),
        ],
        compiler_params=params(),
        name="row_stats",
    )(places, keys, vals, qs, gs)
    stats = pl.pallas_call(
        share_kernel,
        out_shape=shape((3, QUERY_BLOCKS, STACK), F32),
        in_specs=[vmem],
        out_specs=vmem,
        scratch_shapes=[
            pltpu.VMEM((NX - 1, 3, QUERY_BLOCKS, STACK), F32), dma(NX - 1), dma(NX - 1),
        ],
        compiler_params=params(2),
        name="share_stats",
    )(stats)
    dq, dk, dv = pl.pallas_call(
        back_kernel,
        out_shape=(
            shape((NX, ROWS, GROUP * HD), BF16),
            shape((KEY_BLOCKS * BLK, HD), BF16),
            shape((KEY_BLOCKS * BLK, HD), BF16),
        ),
        in_specs=[smem, vmem, vmem, vmem, vmem, vmem],
        out_specs=(vmem,) * 3,
        scratch_shapes=[
            pltpu.VMEM((KEY_BLOCKS * BLK, HD), F32),
            pltpu.VMEM((KEY_BLOCKS * BLK, HD), F32),
            pltpu.SMEM((KEY_BLOCKS + CHUNK,), jnp.int32),
        ],
        compiler_params=params(),
        name="back_tiles",
    )(places, stats, keys, vals, qs, gs)
    slice_width = width // (nl * NC)
    w_split = w_key.reshape(nl, NC, slice_width, HD)
    block = (ROWS, HD)
    results = pl.pallas_call(
        functools.partial(reduce_kernel, nl),
        out_shape=(
            shape((ROWS, GROUP * HD), BF16),
            shape((ROWS, HD), BF16),
            shape((ROWS, slice_width), BF16),
            shape((BLK, HD), F32),
        ),
        in_specs=[vmem, vmem, vmem, vmem, hbm],
        out_specs=(vmem,) * 4,
        scratch_shapes=[
            pltpu.VMEM((2, NZ) + block, BF16),
            pltpu.VMEM((2,) + block, BF16),
            pltpu.VMEM((2, NZ) + block, BF16),
            pltpu.VMEM((2, NZ) + block, BF16),
            pltpu.VMEM((2, NZ) + block, BF16),
            pltpu.VMEM((2, HY, NZ) + block, BF16),
            pltpu.VMEM((2, HY, NZ) + block, BF16),
            pltpu.VMEM((NX - 1, ROWS, GROUP * HD), BF16),
            pltpu.VMEM((NY - 1,) + block, BF16),
            pltpu.VMEM((2,) + block, BF16),
            pltpu.VMEM((2,) + block, BF16),
            pltpu.VMEM((NX,) + block, BF16),
            pltpu.VMEM(block, BF16),
            pltpu.VMEM((NX, pairs, BLK, ROWS), BF16),
            pltpu.VMEM((nl, slice_width, HD), BF16),
            pltpu.VMEM((nl, slice_width, HD), BF16),
            pltpu.VMEM((NY - 1,) + block, BF16),
            pltpu.VMEM((nl - 1, ROWS, slice_width), BF16),
            pltpu.VMEM((nl - 1, ROWS, slice_width), BF16),
            pltpu.VMEM(block, F32),
            pltpu.VMEM((BLK, HD), F32),
            dma(8), dma(8), dma(2 * HY), dma(2 * HY), dma(NY - 1), dma(NY - 1), dma(9), dma(9), dma(3), dma(3),
            dma(1 + nl), dma(1 + nl), dma(2),
        ],
        compiler_params=params(3),
        name="reduce_grads",
    )(dq, dk.reshape(NZ, NY, ROWS, HD), dv.reshape(NZ, NY, ROWS, HD), turned, in_hbm(w_split))
    return pl.pallas_call(
        hand_over_kernel,
        out_shape=tuple(shape(r.shape, r.dtype) for r in results),
        in_specs=[vmem] * 4,
        out_specs=(hbm,) * 4,
        scratch_shapes=[dma(4)],
        compiler_params=params(),
        name="hand_over",
    )(*results)


def solution(mesh):
    nl = mesh.shape["tensor"] // NC
    return jax.shard_map(
        functools.partial(on_device, nl),
        mesh=mesh,
        in_specs=(
            P("dp", None),
            P(None, "tensor"),
            P("dp", "tensor"),
            P("dp", "tensor"),
            P("dp", "tensor"),
            P(),
            P("dp"),
        ),
        out_specs=(P("dp", "tensor"), P("dp", "tensor"), P("dp", "tensor"), P("dp", "tensor")),
        check_vma=False,
    )
```

```python
import functools
import math

import jax
import jax.numpy as jnp
from jax import lax
from jax.experimental import pallas as pl
from jax.experimental.pallas import tpu as pltpu
from jax.sharding import PartitionSpec as P

MESH = pl.DeviceIdType.MESH
F32, BF16 = jnp.float32, jnp.bfloat16
HD, BLK, GROUP, ROWS = 128, 64, 4, 128
NX, NZ, NY, NC = 4, 2, 8, 2
HY, HX = NY // 2, NX // 2
KEY_BLOCKS = 2 * NZ * NY
QUERY_BLOCKS = 2 * NX
STACK = GROUP * BLK
CHUNK = 4
CHUNKS = KEY_BLOCKS // CHUNK
SIDE = 2
PARTS = 4
LIST, COUNTS, ITEMS, TOTAL, PLAN = 40, 320, 336, 416, 512
SCALE = 1.0 / math.sqrt(HD)
LOG2 = SCALE / math.log(2.0)
LOW = -1e30
FLOOR = -1e29
NT = (((1,), (1,)), ((), ()))
VMEM_LIMIT = 40 * 1024 * 1024

vmem = pl.BlockSpec(memory_space=pltpu.VMEM)
smem = pl.BlockSpec(memory_space=pltpu.SMEM)
hbm = pl.BlockSpec(memory_space=pltpu.HBM)


def rem(a, n):
    return lax.rem(a, jnp.int32(n))


def place():
    dp, tensor = lax.axis_index("dp"), lax.axis_index("tensor")
    x = rem(dp, NX)
    rest = lax.div(dp, jnp.int32(NX))
    return lax.div(rest, jnp.int32(NZ)), rem(rest, NZ), x, tensor


def device(y, zh, x, tensor):
    return ((y * NZ + zh) * NX + x, tensor)


def greet(peers):
    barrier = pltpu.get_barrier_semaphore()
    for peer in peers:
        pl.semaphore_signal(barrier, inc=1, device_id=peer, device_id_type=MESH)


def meet(peers):
    pl.semaphore_wait(pltpu.get_barrier_semaphore(), len(peers))


def send(src, dst, sems, index, peer):
    copy = pltpu.make_async_remote_copy(
        src_ref=src,
        dst_ref=dst,
        send_sem=sems[0].at[index],
        recv_sem=sems[1].at[index],
        device_id=peer,
        device_id_type=MESH,
    )
    copy.start()
    return copy


class Tree:
    def __init__(self, block, half, me, n, ups, downs, sems, base):
        self.block, self.half, self.me, self.n = block, half, me, n
        self.ups, self.downs, self.sems, self.base = ups, downs, sems, base

    def first(self):
        own = self.block(self.me)
        self.near = [
            send(own, own, self.sems, self.base + i, peer)
            for i, peer in enumerate((self.ups[1], self.downs[1], self.ups[0], self.downs[0]))
        ]

    def second(self):
        self.far = []
        for way, peers in enumerate((self.ups, self.downs)):
            self.near[way].wait_recv()
            ref = self.block(rem(self.me + (self.n - 2 if way == 0 else 2), self.n))
            half = self.half(ref, way)
            self.far.append(send(half, half, self.sems, self.base + 4 + 2 * way, peers[1]))
            self.far.append(send(ref, ref, self.sems, self.base + 5 + 2 * way, peers[0]))

    def end(self):
        for copy in self.near[2:] + self.far:
            copy.wait_recv()

    def drain(self):
        for copy in self.near + self.far:
            copy.wait_send()


def gather_kernel(
    inputs, w_key, values, queries, d_out, doc_lens, block_pos, keys, vals, qs, gs, turned, places,
    x_buf, w_buf, docs, pos, y_send, y_recv, x_send, x_recv, z_send, z_recv, load_sem,
):
    y, zh, x, t = place()
    ups = [device(rem(y + j, NY), zh, x, t) for j in (1, 2)]
    downs = [device(rem(y + NY - j, NY), zh, x, t) for j in (1, 2)]
    others_x = [device(y, zh, rem(x + j, NX), t) for j in range(1, NX)]
    partner = device(y, 1 - zh, x, t)
    peers = [partner] + ups + downs + others_x
    greet(peers)
    loads = [
        pltpu.make_async_copy(src, dst, load_sem.at[i])
        for i, (src, dst) in enumerate(
            (
                (block_pos, pos),
                (values, vals.at[zh, y, pl.ds(0, ROWS)]),
                (d_out, gs.at[x, pl.ds(0, ROWS)]),
                (queries, qs.at[x]),
                (doc_lens, docs),
            )
        )
    ]
    depth = inputs.shape[1] // PARTS
    parts = []
    for i in range(PARTS):
        cut = slice(i * depth, (i + 1) * depth)
        parts.append((
            pltpu.make_async_copy(w_key.at[cut], w_buf.at[cut], load_sem.at[5 + 2 * i]),
            pltpu.make_async_copy(inputs.at[:, cut], x_buf.at[:, cut], load_sem.at[6 + 2 * i]),
        ))
    for load in loads + [load for pair in parts for load in pair]:
        load.start()
    loads[0].wait()
    lane = lax.broadcasted_iota(jnp.int32, (16, ROWS), 1)
    first = 2 * (zh * NY + y)
    mine = jnp.where(lane == first, pos[0], 0) + jnp.where(lane == first + 1, pos[1], 0)
    seat = KEY_BLOCKS + 2 * x
    here = jnp.where(lane == seat, pos[0], 0) + jnp.where(lane == seat + 1, pos[1], 0)
    vals[zh, y, ROWS : ROWS + 16, :] = mine.astype(F32).astype(BF16)
    gs[x, ROWS : ROWS + 16, 0:HD] = here.astype(F32).astype(BF16)
    gs[x, ROWS : ROWS + 16, HD:] = jnp.zeros((16, (GROUP - 1) * HD), BF16)
    loads[1].wait()
    meet(peers)

    y_sems, x_sems, z_sems = (y_send, y_recv), (x_send, x_recv), (z_send, z_recv)

    def half_k(ref, way):
        return ref.at[pl.ds(way * 64, 64)]

    def half_v(ref, way):
        return ref.at[pl.ds(0, 64)] if way == 0 else ref.at[pl.ds(64, ROWS + 16 - 64)]

    def tree(arr, half, z, base):
        return Tree(lambda o: arr.at[z, o], half, y, NY, ups, downs, y_sems, base)

    v_own, k_own = tree(vals, half_v, zh, 0), tree(keys, half_k, zh, 8)
    v_far, k_far = tree(vals, half_v, 1 - zh, 16), tree(keys, half_k, 1 - zh, 24)

    z_v = send(vals.at[zh, y], vals.at[zh, y], z_sems, 0, partner)
    v_own.first()
    sideways = []
    loads[2].wait()
    for j in (2, 1, 3):
        sideways.append(send(gs.at[x], gs.at[x], x_sems, j - 1, others_x[j - 1]))
    loads[3].wait()
    for j in (2, 1, 3):
        sideways.append(send(qs.at[x], qs.at[x], x_sems, j + 2, others_x[j - 1]))
    projected = jnp.zeros((ROWS, HD), F32)
    for i, pair in enumerate(parts):
        cut = slice(i * depth, (i + 1) * depth)
        for load in pair:
            load.wait()
        projected = projected + jnp.dot(
            x_buf[:, cut], w_buf[cut, :], preferred_element_type=F32
        )
    keys[zh, y] = projected.astype(BF16)
    z_k = send(keys.at[zh, y], keys.at[zh, y], z_sems, 1, partner)
    k_own.first()

    def turn(first, last):
        def body(j, carry):
            tile = x_buf[:, pl.ds(pl.multiple_of(j * 128, 128), 128)].T
            for part in range(2):
                b = 2 * j + part
                pair = lax.div(b, jnp.int32(NX))
                turned[rem(b, NX), rem(pair, NZ), lax.div(pair, jnp.int32(NZ))] = tile[
                    part * 64 : part * 64 + 64
                ]
            return carry

        lax.fori_loop(first, last, body, 0)

    tiles = inputs.shape[1] // 128
    turn(0, tiles // 4)
    v_own.second()
    z_v.wait_recv()
    v_far.first()
    k_own.second()
    z_k.wait_recv()
    k_far.first()
    turn(tiles // 4, tiles // 2)
    v_far.second()
    k_far.second()
    turn(tiles // 2, tiles)
    loads[4].wait()
    rings = (v_own, k_own, v_far, k_far)
    for r in rings:
        r.end()
    for copy in sideways:
        copy.wait_recv()
    total = jnp.zeros((16, ROWS), F32)
    for z in range(NZ):
        for j in range(NY):
            total = total + vals[z, j, ROWS : ROWS + 16, :].astype(F32)
    for j in range(NX):
        total = total + gs[j, ROWS : ROWS + 16, 0:HD].astype(F32)
    seats = lax.broadcasted_iota(jnp.int32, (8, ROWS), 1)
    lengths = jnp.zeros((8, ROWS), jnp.int32)
    for d in range(4):
        lengths = lengths + jnp.where(seats == d, docs[d], 0)
    rows = lax.broadcasted_iota(jnp.int32, (8, ROWS), 0)
    places[...] = jnp.where(rows == 1, lengths, total[0:8].astype(jnp.int32))
    z_v.wait_send()
    z_k.wait_send()
    for r in rings:
        r.drain()
    for copy in sideways:
        copy.wait_send()


def doc_starts(places):
    starts = [jnp.int32(0)]
    for d in range(3):
        starts.append(starts[-1] + places[1, d])
    return starts


def make_plan(places, plan):
    starts = doc_starts(places)

    def visit(query, items):
        mine = places[0, KEY_BLOCKS + query]
        start = jnp.int32(0)
        for s in starts[1:]:
            start = jnp.where(s <= mine * BLK, s, start)
        low = lax.div(start, jnp.int32(BLK))
        begin = query * LIST
        count = jnp.int32(0)
        for b in range(KEY_BLOCKS):
            pk = places[0, b]
            plan[begin + count] = jnp.int32(b)
            count = count + ((pk <= mine) & (pk >= low)).astype(jnp.int32)
        for j in range(CHUNK):
            plan[begin + count + j] = jnp.int32(0)
        plan[COUNTS + query] = count
        for c in range(CHUNKS):
            plan[ITEMS + items] = query * 16 + c
            items = items + (count > c * CHUNK).astype(jnp.int32)
        return items

    items = lax.fori_loop(0, QUERY_BLOCKS, visit, jnp.int32(0))
    plan[ITEMS + items] = jnp.int32(0)
    plan[TOTAL] = items


def item_of(places, plan, starts, at):
    real = at < plan[TOTAL]
    code = plan[ITEMS + at]
    query, chunk = code >> 4, code & 15
    count = jnp.where(real, plan[COUNTS + query], 0)
    row = places[0, KEY_BLOCKS + query] * BLK + (
        lax.broadcasted_iota(jnp.int32, (1, 2 * BLK), 1) & (BLK - 1)
    )
    opens = jnp.zeros((1, 2 * BLK), jnp.int32)
    for s in starts[1:]:
        opens = jnp.where(s <= row, s, opens)
    return query, chunk, real, count, row, opens


def key_chunk(places, plan, item, keys, vals):
    query, chunk, _, count, row, opens = item
    iota = lax.broadcasted_iota(jnp.int32, (BLK, 2 * BLK), 0)
    ks, vs, terms, blocks = [], [], [], []
    for j in range(CHUNK):
        at = chunk * CHUNK + j
        b = plan[query * LIST + at]
        base = jnp.where(at < count, places[0, b] * BLK, jnp.int32(1 << 20))
        ks.append(keys[pl.ds(pl.multiple_of(b * BLK, BLK), BLK), :])
        vs.append(vals[b >> 1, pl.ds(pl.multiple_of((b & 1) * BLK, BLK), BLK), :])
        ok = (iota >= opens - base) & (iota <= row - base)
        term = jnp.where(ok, 0.0, LOW)
        terms.append(jnp.concatenate([term, term], axis=1))
        blocks.append(b)
    return (
        jnp.concatenate(ks, axis=0),
        jnp.concatenate(vs, axis=0),
        jnp.concatenate(terms, axis=0),
        blocks,
    )


def head_stack(ref, query):
    rows = pl.ds(pl.multiple_of((query & 1) * BLK, BLK), BLK)
    return jnp.concatenate(
        [ref[query >> 1, rows, h * HD : (h + 1) * HD] for h in range(GROUP)], axis=0
    )


def stats_kernel(places, keys, vals, qs, gs, out, plan, kept):
    make_plan(places, plan)
    starts = doc_starts(places)
    for c in range(CHUNKS):
        kept[c, 0] = jnp.full((QUERY_BLOCKS, STACK), FLOOR, F32)
        kept[c, 1] = jnp.zeros((QUERY_BLOCKS, STACK), F32)
        kept[c, 2] = jnp.zeros((QUERY_BLOCKS, STACK), F32)

    def step(i, carry):
        found = []
        for part in range(SIDE):
            item = item_of(places, plan, starts, i * SIDE + part)
            k, v, term, _ = key_chunk(places, plan, item, keys, vals)
            q, g = head_stack(qs, item[0]), head_stack(gs, item[0])
            score = lax.dot_general(k, q, NT, preferred_element_type=F32) * LOG2 + term
            d_prob = lax.dot_general(v, g, NT, preferred_element_type=F32)
            top = jnp.maximum(FLOOR, jnp.max(score, axis=0, keepdims=True))
            e = jnp.exp2(score - top)
            found.append((
                item, top, jnp.sum(e, axis=0, keepdims=True), jnp.sum(e * d_prob, axis=0, keepdims=True)
            ))
        for item, top, mass, weighted in found:
            slot = jnp.where(item[2], item[1], CHUNKS)
            for j, value in enumerate((top, mass, weighted)):
                kept[slot, j, pl.ds(item[0], 1), :] = value
        return carry

    lax.fori_loop(0, lax.div(plan[TOTAL] + (SIDE - 1), jnp.int32(SIDE)), step, 0)
    top = kept[0, 0]
    for c in range(1, CHUNKS):
        top = jnp.maximum(top, kept[c, 0])
    mass, weighted = jnp.zeros_like(top), jnp.zeros_like(top)
    for c in range(CHUNKS):
        shrink = jnp.exp2(kept[c, 0] - top)
        mass = mass + kept[c, 1] * shrink
        weighted = weighted + kept[c, 2] * shrink
    out[0], out[1], out[2] = top, mass, weighted


def share_kernel(stats, out, got, send_sem, recv_sem):
    y, zh, x, t = place()
    peers = [device(y, zh, rem(x + j, NX), t) for j in range(1, NX)]
    greet(peers)
    meet(peers)
    copies = [send(stats, got.at[j], (send_sem, recv_sem), j, peer) for j, peer in enumerate(peers)]
    for copy in copies:
        copy.wait_recv()
    parts = [[stats[i] for i in range(3)]] + [[got[j, i] for i in range(3)] for j in range(NX - 1)]
    top = parts[0][0]
    for p in parts[1:]:
        top = jnp.maximum(top, p[0])
    mass = jnp.zeros_like(top)
    weighted = jnp.zeros_like(top)
    for p in parts:
        shrink = jnp.exp2(p[0] - top)
        mass = mass + p[1] * shrink
        weighted = weighted + p[2] * shrink
    out[0] = top
    out[1] = 1.0 / mass
    out[2] = weighted / mass
    for copy in copies:
        copy.wait_send()


def back_kernel(
    places, plan, stats, keys, vals, qs, gs, dq, dk, dv, dq_sum, dk_sum, dv_sum
):
    starts = doc_starts(places)
    dq_sum[...] = jnp.zeros_like(dq_sum)
    dk_sum[...] = jnp.zeros_like(dk_sum)
    dv_sum[...] = jnp.zeros_like(dv_sum)

    def step(i, carry):
        found = []
        for part in range(SIDE):
            item = item_of(places, plan, starts, i * SIDE + part)
            query = item[0]
            k, v, term, blocks = key_chunk(places, plan, item, keys, vals)
            q, g = head_stack(qs, query), head_stack(gs, query)
            top, scale, delta = [stats[j, pl.ds(query, 1), :] for j in range(3)]
            score = lax.dot_general(k, q, NT, preferred_element_type=F32) * LOG2 + term
            d_prob = lax.dot_general(v, g, NT, preferred_element_type=F32)
            prob = jnp.exp2(score - top) * scale
            d_score = (prob * (d_prob - delta)).astype(BF16)
            dv_part = jnp.dot(prob.astype(BF16), g, preferred_element_type=F32)
            dk_part = jnp.dot(d_score, q, preferred_element_type=F32)
            dq_part = jnp.dot(k.T, d_score, preferred_element_type=F32)
            found.append((query, blocks, dq_part, dk_part, dv_part))
        for query, blocks, dq_part, dk_part, dv_part in found:
            dq_sum[query] += dq_part
            for j, b in enumerate(blocks):
                rows = pl.ds(pl.multiple_of(b * BLK, BLK), BLK)
                dv_sum[rows, :] += dv_part[j * BLK : (j + 1) * BLK]
                dk_sum[rows, :] += dk_part[j * BLK : (j + 1) * BLK]
        return carry

    lax.fori_loop(0, lax.div(plan[TOTAL] + (SIDE - 1), jnp.int32(SIDE)), step, 0)
    for query in range(QUERY_BLOCKS):
        dq_rows = (dq_sum[query] * SCALE).T.astype(BF16)
        rows = slice((query % 2) * BLK, (query % 2 + 1) * BLK)
        for h in range(GROUP):
            dq[query // 2, rows, h * HD : (h + 1) * HD] = dq_rows[h * BLK : (h + 1) * BLK]
    dk[...] = (dk_sum[...] * SCALE).astype(BF16)
    dv[...] = dv_sum[...].astype(BF16)


class Fold:
    def __init__(self, block, me, n, ups, downs, far, near, made, last, sems, base):
        self.block, self.me, self.n, self.peers, self.sems, self.base = block, me, n, (ups, downs), sems, base
        self.got_far, self.got_near, self.made, self.got_last = far, near, made, last

    def at(self, way, far):
        return self.block(rem(self.me + (far if way == 0 else self.n - far), self.n))

    def go(self, src, dst, i, peer):
        return send(src, dst, self.sems, self.base + i, peer)

    def first(self):
        self.far, self.half, self.near = [], [], []
        for way, peers in enumerate(self.peers):
            part = pl.ds(way * (ROWS // 2), ROWS // 2)
            self.half.append(
                self.go(self.at(way, 4).at[part], self.got_far.at[way, pl.ds(ROWS, ROWS // 2)], way, peers[1])
            )
            self.far.append(
                self.go(self.at(way, 3), self.got_far.at[way, pl.ds(0, ROWS)], 2 + way, peers[0])
            )
        for way, peers in enumerate(self.peers):
            self.near.append(self.go(self.at(way, 1), self.got_near.at[way], 4 + way, peers[0]))

    def second(self):
        self.last = []
        middle = ROWS // 2
        for way, peers in enumerate(self.peers):
            self.far[way].wait_recv()
            self.half[way].wait_recv()
            own, far, out = self.at(way, 2), self.got_far.at[way], self.made.at[way]
            with_half = pl.ds(way * middle, middle)
            without = pl.ds((1 - way) * middle, middle)
            out[without] = (own[without].astype(F32) + far[without].astype(F32)).astype(BF16)
            out[with_half] = (
                own[with_half].astype(F32)
                + far[with_half].astype(F32)
                + far[pl.ds(ROWS, middle)].astype(F32)
            ).astype(BF16)
            self.last.append(self.go(out, self.got_last.at[way], 6 + way, peers[1]))

    def total(self):
        for copy in self.near + self.last:
            copy.wait_recv()
        out = self.block(self.me)[...].astype(F32)
        for way in range(2):
            out = out + self.got_near[way].astype(F32) + self.got_last[way].astype(F32)
        return out

    def drain(self):
        for copy in self.far + self.half + self.near + self.last:
            copy.wait_send()


def reduce_kernel(
    dq, dk, dv, turned, w_key, d_query, d_value, d_input, d_wkey,
    f_far, f_near, f_made, f_last, q_got, w_got, z_out, z_got,
    kg, kg_quad, xg, w_all, w_part, in_part, in_got, zw_out, zw_got,
    f_send, f_recv, w_send, w_recv, x_send, x_recv, z_send, z_recv, s_send, s_recv, load_sem,
):
    y, zh, x, t = place()
    zl, core = lax.div(t, jnp.int32(NC)), rem(t, NC)
    others_y = [device(rem(y + j, NY), zh, x, t) for j in range(1, NY)]
    ups, downs = others_y[:2], [others_y[-1], others_y[-2]]
    others_x = [device(y, zh, rem(x + j, NX), t) for j in range(1, NX)]
    partner = device(y, 1 - zh, x, t)
    half, quarter = lax.div(zl, jnp.int32(2)), rem(zl, 2)
    sibling = device(y, zh, x, zl * NC + 1 - core)
    across = [device(y, zh, x, (zl + 1 - 2 * quarter) * NC + c) for c in (core, 1 - core)]
    quad = [sibling] + across
    over = device(y, zh, x, rem(zl + 2, 4) * NC + core)
    x_sems, z_sems, s_sems = (x_send, x_recv), (z_send, z_recv), (s_send, s_recv)
    peers = [partner] + others_y + others_x + quad + [over]
    greet(peers)
    own_x = pltpu.make_async_copy(turned.at[x], xg.at[x], load_sem.at[0])
    own_w = pltpu.make_async_copy(w_key.at[:, quarter, core], w_all.at[0], load_sem.at[1])
    own_x.start()
    own_w.start()
    meet(peers)

    def fold(arr, z, i):
        return Fold(
            lambda o: arr.at[z, o], y, NY, ups, downs,
            f_far.at[i], f_near.at[i], f_made.at[i], f_last.at[i], (f_send, f_recv), 8 * i,
        )

    far = 1 - zh
    k_far, k_own = fold(dk, far, 0), fold(dk, zh, 1)
    v_far, v_own = fold(dv, far, 2), fold(dv, zh, 3)
    k_far.first()
    k_own.first()
    x_sends = [
        send(turned.at[rem(x + j, NX)], xg.at[x], x_sems, j - 1, others_x[j - 1]) for j in (2, 1, 3)
    ]
    w_sides = ((quarter, 1 - core), (1 - quarter, core), (1 - quarter, 1 - core))
    w_swaps = [
        send(w_key.at[:, q, c], w_all.at[j + 1], s_sems, j, quad[j]) for j, (q, c) in enumerate(w_sides)
    ]
    k_far.second()
    k_own.second()
    z_out[0] = k_far.total().astype(BF16)
    z_key = send(z_out.at[0], z_got.at[0], z_sems, 0, partner)
    v_far.first()
    v_own.first()
    key_sum = k_own.total()
    z_key.wait_recv()
    kg[x] = (key_sum + z_got[0].astype(F32)).astype(BF16)

    kg_sends = [send(kg.at[x], kg.at[x], x_sems, 2 + j, others_x[j - 1]) for j in (2, 1, 3)]
    kg_swaps = [send(kg.at[x], kg_quad.at[j], s_sems, 3 + j, quad[j]) for j in range(3)]
    q_sends = [
        send(dq.at[rem(x + j, NX)], q_got.at[j - 1], x_sems, 5 + j, others_x[j - 1]) for j in (2, 1, 3)
    ]
    v_far.second()
    v_own.second()
    own_w.wait()
    for copy in w_swaps + kg_swaps:
        copy.wait_recv()
    quad_heads = [kg[x]] + [kg_quad[j] for j in range(3)]

    def in_block(h):
        out = jnp.zeros((ROWS, w_all.shape[2]), F32)
        for j, head in enumerate(quad_heads):
            out = out + lax.dot_general(head, w_all[j, h], NT, preferred_element_type=F32)
        return out

    in_part[...] = in_block(1 - half).astype(BF16)
    in_send = send(in_part, in_got, s_sems, 6, over)

    own_x.wait()
    for copy in x_sends + kg_sends:
        copy.wait_recv()
    heads = [kg[src] for src in range(NX)]
    w_sends = []
    for turn, z in enumerate((far, zh)):
        product = jnp.zeros((NY * BLK, HD), F32)
        for src in range(NX):
            rows = xg[src, z].reshape(NY * BLK, ROWS)
            product = product + jnp.dot(rows, heads[src], preferred_element_type=F32)
        w_part[turn] = product.astype(BF16).reshape(NY, BLK, HD)
        for j in (4, 3, 5, 2, 6, 1, 7):
            w_sends.append(
                send(
                    w_part.at[turn, rem(y + j, NY)], w_got.at[turn, j - 1],
                    (w_send, w_recv), turn * (NY - 1) + j - 1, others_y[j - 1],
                )
            )

    def w_total(turn):
        for copy in w_sends[turn * (NY - 1) : (turn + 1) * (NY - 1)]:
            copy.wait_recv()
        out = w_part[turn, y].astype(F32)
        for j in range(NY - 1):
            out = out + w_got[turn, j].astype(F32)
        return out

    z_out[1] = v_far.total().astype(BF16)
    z_val = send(z_out.at[1], z_got.at[1], z_sems, 1, partner)
    in_sum = in_block(half)
    zw_out[...] = w_total(0)
    z_w = send(zw_out, zw_got, z_sems, 2, partner)
    q_sum = dq[x].astype(F32)
    for copy in q_sends:
        copy.wait_recv()
    for j in range(NX - 1):
        q_sum = q_sum + q_got[j].astype(F32)
    d_query[...] = q_sum.astype(BF16)
    in_send.wait_recv()
    d_input[...] = (in_sum + in_got[...].astype(F32)).astype(BF16)
    z_val.wait_recv()
    d_value[...] = (v_own.total() + z_got[1].astype(F32)).astype(BF16)
    w_sum = w_total(1)
    z_w.wait_recv()
    d_wkey[...] = w_sum + zw_got[...]

    for f in (k_far, k_own, v_far, v_own):
        f.drain()
    for copy in [z_key, z_val, z_w, in_send] + x_sends + kg_sends + q_sends + w_sends + w_swaps + kg_swaps:
        copy.wait_send()


def dma(n):
    return pltpu.SemaphoreType.DMA((n,))


def params(collective_id=None):
    return pltpu.CompilerParams(
        collective_id=collective_id,
        has_side_effects=collective_id is not None,
        vmem_limit_bytes=VMEM_LIMIT,
    )


def in_hbm(array):
    return pltpu.with_memory_space_constraint(array, pltpu.HBM)


def hand_over_kernel(*refs):
    n = (len(refs) - 1) // 2
    copies = [
        pltpu.make_async_copy(refs[i], refs[n + i], refs[-1].at[i]) for i in range(n)
    ]
    for copy in copies:
        copy.start()
    for copy in copies:
        copy.wait()


def on_device(nl, inputs, w_key, values, queries, d_out, doc_lens, block_pos):
    width = inputs.shape[1]
    pairs = NZ * NY
    shape = jax.ShapeDtypeStruct
    keys, vals, qs, gs, turned, places = pl.pallas_call(
        gather_kernel,
        out_shape=(
            shape((NZ, NY, ROWS, HD), BF16),
            shape((NZ, NY, ROWS + 16, HD), BF16),
            shape((NX, ROWS, GROUP * HD), BF16),
            shape((NX, ROWS + 16, GROUP * HD), BF16),
            shape((NX, NZ, NY, BLK, ROWS), BF16),
            shape((8, ROWS), jnp.int32),
        ),
        in_specs=[hbm] * 7,
        out_specs=(vmem,) * 6,
        scratch_shapes=[
            pltpu.VMEM((ROWS, width), BF16),
            pltpu.VMEM((width, HD), BF16),
            pltpu.SMEM((4,), jnp.int32),
            pltpu.SMEM((2,), jnp.int32),
            dma(32), dma(32), dma(6), dma(6), dma(2), dma(2), dma(5 + 2 * PARTS),
        ],
        compiler_params=params(1),
        name="gather_rows",
    )(*(in_hbm(a) for a in (inputs, w_key, values, queries, d_out, doc_lens, block_pos)))
    keys = keys.reshape(KEY_BLOCKS * BLK, HD)
    vals = vals.reshape(pairs, ROWS + 16, HD)
    stats, plan = pl.pallas_call(
        stats_kernel,
        out_shape=(shape((3, QUERY_BLOCKS, STACK), F32), shape((PLAN,), jnp.int32)),
        in_specs=[smem, vmem, vmem, vmem, vmem],
        out_specs=(vmem, smem),
        scratch_shapes=[pltpu.VMEM((CHUNKS + 1, 3, QUERY_BLOCKS, STACK), F32)],
        compiler_params=params(),
        name="row_stats",
    )(places, keys, vals, qs, gs)
    stats = pl.pallas_call(
        share_kernel,
        out_shape=shape((3, QUERY_BLOCKS, STACK), F32),
        in_specs=[vmem],
        out_specs=vmem,
        scratch_shapes=[
            pltpu.VMEM((NX - 1, 3, QUERY_BLOCKS, STACK), F32), dma(NX - 1), dma(NX - 1),
        ],
        compiler_params=params(2),
        name="share_stats",
    )(stats)
    dq, dk, dv = pl.pallas_call(
        back_kernel,
        out_shape=(
            shape((NX, ROWS, GROUP * HD), BF16),
            shape((KEY_BLOCKS * BLK, HD), BF16),
            shape((KEY_BLOCKS * BLK, HD), BF16),
        ),
        in_specs=[smem, smem, vmem, vmem, vmem, vmem, vmem],
        out_specs=(vmem,) * 3,
        scratch_shapes=[
            pltpu.VMEM((QUERY_BLOCKS, HD, STACK), F32),
            pltpu.VMEM((KEY_BLOCKS * BLK, HD), F32),
            pltpu.VMEM((KEY_BLOCKS * BLK, HD), F32),
        ],
        compiler_params=params(),
        name="back_tiles",
    )(places, plan, stats, keys, vals, qs, gs)
    slice_width = width // (nl * NC)
    w_split = w_key.reshape(2, 2, NC, slice_width, HD)
    block = (ROWS, HD)
    results = pl.pallas_call(
        reduce_kernel,
        out_shape=(
            shape((ROWS, GROUP * HD), BF16),
            shape((ROWS, HD), BF16),
            shape((ROWS, slice_width), BF16),
            shape((BLK, HD), F32),
        ),
        in_specs=[vmem, vmem, vmem, vmem, hbm],
        out_specs=(vmem,) * 4,
        scratch_shapes=[
            pltpu.VMEM((4, 2, ROWS + ROWS // 2, HD), BF16),
            pltpu.VMEM((4, 2) + block, BF16),
            pltpu.VMEM((4, 2) + block, BF16),
            pltpu.VMEM((4, 2) + block, BF16),
            pltpu.VMEM((NX - 1, ROWS, GROUP * HD), BF16),
            pltpu.VMEM((NZ, NY - 1, BLK, HD), BF16),
            pltpu.VMEM((2,) + block, BF16),
            pltpu.VMEM((2,) + block, BF16),
            pltpu.VMEM((NX,) + block, BF16),
            pltpu.VMEM((3,) + block, BF16),
            pltpu.VMEM((NX, NZ, NY, BLK, ROWS), BF16),
            pltpu.VMEM((4, 2, slice_width, HD), BF16),
            pltpu.VMEM((NZ, NY, BLK, HD), BF16),
            pltpu.VMEM((ROWS, slice_width), BF16),
            pltpu.VMEM((ROWS, slice_width), BF16),
            pltpu.VMEM((BLK, HD), F32),
            pltpu.VMEM((BLK, HD), F32),
            dma(32), dma(32), dma(2 * (NY - 1)), dma(2 * (NY - 1)), dma(9), dma(9), dma(3), dma(3),
            dma(7), dma(7), dma(2),
        ],
        compiler_params=params(3),
        name="reduce_grads",
    )(dq, dk.reshape(NZ, NY, ROWS, HD), dv.reshape(NZ, NY, ROWS, HD), turned, in_hbm(w_split))
    return pl.pallas_call(
        hand_over_kernel,
        out_shape=tuple(shape(r.shape, r.dtype) for r in results),
        in_specs=[vmem] * 4,
        out_specs=(hbm,) * 4,
        scratch_shapes=[dma(4)],
        compiler_params=params(),
        name="hand_over",
    )(*results)


def solution(mesh):
    nl = mesh.shape["tensor"] // NC
    return jax.shard_map(
        functools.partial(on_device, nl),
        mesh=mesh,
        in_specs=(
            P("dp", None),
            P(None, "tensor"),
            P("dp", "tensor"),
            P("dp", "tensor"),
            P("dp", "tensor"),
            P(),
            P("dp"),
        ),
        out_specs=(P("dp", "tensor"), P("dp", "tensor"), P("dp", "tensor"), P("dp", "tensor")),
        check_vma=False,
    )
```

```python
import functools
import math

import jax
import jax.numpy as jnp
from jax import lax
from jax.experimental import pallas as pl
from jax.experimental.pallas import tpu as pltpu
from jax.sharding import PartitionSpec as P

MESH = pl.DeviceIdType.MESH
F32, BF16 = jnp.float32, jnp.bfloat16
HD, BLK, GROUP, ROWS = 128, 64, 4, 128
NX, NZ, NY, NC = 4, 2, 8, 2
HY, HX = NY // 2, NX // 2
KEY_BLOCKS = 2 * NZ * NY
QUERY_BLOCKS = 2 * NX
STACK = GROUP * BLK
CHUNK = 4
CHUNKS = KEY_BLOCKS // CHUNK
SIDE = 4
PARTS = 4
LIST, COUNTS, ITEMS, TOTAL, PLAN = 40, 320, 336, 416, 512
SCALE = 1.0 / math.sqrt(HD)
LOG2 = SCALE / math.log(2.0)
LOW = -1e30
FLOOR = -1e29
NT = (((1,), (1,)), ((), ()))
VMEM_LIMIT = 40 * 1024 * 1024

vmem = pl.BlockSpec(memory_space=pltpu.VMEM)
smem = pl.BlockSpec(memory_space=pltpu.SMEM)
hbm = pl.BlockSpec(memory_space=pltpu.HBM)


def rem(a, n):
    return lax.rem(a, jnp.int32(n))


def place():
    dp, tensor = lax.axis_index("dp"), lax.axis_index("tensor")
    x = rem(dp, NX)
    rest = lax.div(dp, jnp.int32(NX))
    return lax.div(rest, jnp.int32(NZ)), rem(rest, NZ), x, tensor


def device(y, zh, x, tensor):
    return ((y * NZ + zh) * NX + x, tensor)


def quad_of(y, zh, x, zl, core):
    quarter = rem(zl, 2)
    near = zl + 1 - 2 * quarter
    places = ((zl, 1 - core), (near, core), (near, 1 - core))
    return quarter, [device(y, zh, x, chip * NC + c) for chip, c in places]


def greet(peers):
    barrier = pltpu.get_barrier_semaphore()
    for peer in peers:
        pl.semaphore_signal(barrier, inc=1, device_id=peer, device_id_type=MESH)


def meet(peers):
    pl.semaphore_wait(pltpu.get_barrier_semaphore(), len(peers))


def send(src, dst, sems, index, peer):
    copy = pltpu.make_async_remote_copy(
        src_ref=src,
        dst_ref=dst,
        send_sem=sems[0].at[index],
        recv_sem=sems[1].at[index],
        device_id=peer,
        device_id_type=MESH,
    )
    copy.start()
    return copy


class Tree:
    def __init__(self, block, half, me, n, ups, downs, sems, base):
        self.block, self.half, self.me, self.n = block, half, me, n
        self.ups, self.downs, self.sems, self.base = ups, downs, sems, base

    def first(self):
        own = self.block(self.me)
        self.near = [
            send(own, own, self.sems, self.base + i, peer)
            for i, peer in enumerate((self.ups[1], self.downs[1], self.ups[0], self.downs[0]))
        ]

    def second(self):
        self.far = []
        for way, peers in enumerate((self.ups, self.downs)):
            self.near[way].wait_recv()
            ref = self.block(rem(self.me + (self.n - 2 if way == 0 else 2), self.n))
            half = self.half(ref, way)
            self.far.append(send(half, half, self.sems, self.base + 4 + 2 * way, peers[1]))
            self.far.append(send(ref, ref, self.sems, self.base + 5 + 2 * way, peers[0]))

    def end(self):
        for copy in self.near[2:] + self.far:
            copy.wait_recv()

    def drain(self):
        for copy in self.near + self.far:
            copy.wait_send()


def gather_kernel(
    inputs, w_key, w_split, values, queries, d_out, doc_lens, block_pos,
    keys, vals, qs, gs, turned, w_all, places,
    x_buf, w_buf, docs, pos, y_send, y_recv, x_send, x_recv, z_send, z_recv, s_send, s_recv, load_sem,
):
    y, zh, x, t = place()
    ups = [device(rem(y + j, NY), zh, x, t) for j in (1, 2)]
    downs = [device(rem(y + NY - j, NY), zh, x, t) for j in (1, 2)]
    others_x = [device(y, zh, rem(x + j, NX), t) for j in range(1, NX)]
    partner = device(y, 1 - zh, x, t)
    zl, core = lax.div(t, jnp.int32(NC)), rem(t, NC)
    quarter, quad = quad_of(y, zh, x, zl, core)
    peers = [partner] + ups + downs + others_x + quad[:2]
    greet(peers)
    loads = [
        pltpu.make_async_copy(src, dst, load_sem.at[i])
        for i, (src, dst) in enumerate(
            (
                (block_pos, pos),
                (values, vals.at[zh, y, pl.ds(0, ROWS)]),
                (d_out, gs.at[x, pl.ds(0, ROWS)]),
                (queries, qs.at[x]),
                (doc_lens, docs),
                (w_split.at[:, quarter, core], w_all.at[0]),
            )
        )
    ]
    depth = inputs.shape[1] // PARTS
    parts = []
    for i in range(PARTS):
        cut = slice(i * depth, (i + 1) * depth)
        parts.append((
            pltpu.make_async_copy(w_key.at[cut], w_buf.at[cut], load_sem.at[6 + 2 * i]),
            pltpu.make_async_copy(inputs.at[:, cut], x_buf.at[:, cut], load_sem.at[7 + 2 * i]),
        ))
    for load in loads[:5] + [load for pair in parts for load in pair] + loads[5:]:
        load.start()
    loads[0].wait()
    lane = lax.broadcasted_iota(jnp.int32, (16, ROWS), 1)
    first = 2 * (zh * NY + y)
    mine = jnp.where(lane == first, pos[0], 0) + jnp.where(lane == first + 1, pos[1], 0)
    seat = KEY_BLOCKS + 2 * x
    here = jnp.where(lane == seat, pos[0], 0) + jnp.where(lane == seat + 1, pos[1], 0)
    vals[zh, y, ROWS : ROWS + 16, :] = mine.astype(F32).astype(BF16)
    gs[x, ROWS : ROWS + 16, 0:HD] = here.astype(F32).astype(BF16)
    gs[x, ROWS : ROWS + 16, HD:] = jnp.zeros((16, (GROUP - 1) * HD), BF16)
    projected = jnp.zeros((ROWS, HD), F32)
    for i, pair in enumerate(parts):
        cut = slice(i * depth, (i + 1) * depth)
        for load in pair:
            load.wait()
        projected = projected + jnp.dot(
            x_buf[:, cut], w_buf[cut, :], preferred_element_type=F32
        )
    keys[zh, y] = projected.astype(BF16)
    for load in loads[1:4]:
        load.wait()
    meet(peers)

    y_sems, x_sems, z_sems = (y_send, y_recv), (x_send, x_recv), (z_send, z_recv)

    def half_k(ref, way):
        return ref.at[pl.ds(way * 64, 64)]

    def half_v(ref, way):
        return ref.at[pl.ds(0, 64)] if way == 0 else ref.at[pl.ds(64, ROWS + 16 - 64)]

    def tree(arr, half, z, base):
        return Tree(lambda o: arr.at[z, o], half, y, NY, ups, downs, y_sems, base)

    v_own, k_own = tree(vals, half_v, zh, 0), tree(keys, half_k, zh, 8)
    v_far, k_far = tree(vals, half_v, 1 - zh, 16), tree(keys, half_k, 1 - zh, 24)

    z_k = send(keys.at[zh, y], keys.at[zh, y], z_sems, 1, partner)
    z_v = send(vals.at[zh, y], vals.at[zh, y], z_sems, 0, partner)
    k_own.first()
    v_own.first()
    right, left = others_x[0], others_x[-1]
    sideways = []
    for i, (arr, _) in enumerate(((gs, half_v), (qs, half_k))):
        for way, peer in enumerate((right, left)):
            sideways.append(send(arr.at[x], arr.at[x], x_sems, 2 * i + way, peer))

    def turn(first, last):
        def body(j, carry):
            tile = x_buf[:, pl.ds(pl.multiple_of(j * 128, 128), 128)].T
            for part in range(2):
                b = 2 * j + part
                pair = lax.div(b, jnp.int32(NX))
                turned[rem(b, NX), rem(pair, NZ), lax.div(pair, jnp.int32(NZ))] = tile[
                    part * 64 : part * 64 + 64
                ]
            return carry

        lax.fori_loop(first, last, body, 0)

    tiles = inputs.shape[1] // 128
    onward = []

    def pass_on(i, arr, half):
        for way, peer in enumerate((right, left)):
            sideways[2 * i + way].wait_recv()
            ref = half(arr.at[rem(x + (NX - 1 if way == 0 else 1), NX)], way)
            onward.append(send(ref, ref, x_sems, 4 + 2 * i + way, peer))

    turn(0, tiles // 4)
    k_own.second()
    v_own.second()
    z_k.wait_recv()
    k_far.first()
    z_v.wait_recv()
    v_far.first()
    sides = ((quarter, 1 - core), (1 - quarter, core))
    swaps = [
        send(w_split.at[:, q, c], w_all.at[j + 1], (s_send, s_recv), j, quad[j])
        for j, (q, c) in enumerate(sides)
    ]
    pass_on(0, gs, half_v)
    turn(tiles // 4, tiles // 2)
    k_far.second()
    pass_on(1, qs, half_k)
    v_far.second()
    turn(tiles // 2, tiles)
    loads[4].wait()
    loads[5].wait()
    rings = (v_own, k_own, v_far, k_far)
    for r in rings:
        r.end()
    for copy in onward + swaps:
        copy.wait_recv()
    total = jnp.zeros((16, ROWS), F32)
    for z in range(NZ):
        for j in range(NY):
            total = total + vals[z, j, ROWS : ROWS + 16, :].astype(F32)
    for j in range(NX):
        total = total + gs[j, ROWS : ROWS + 16, 0:HD].astype(F32)
    seats = lax.broadcasted_iota(jnp.int32, (8, ROWS), 1)
    lengths = jnp.zeros((8, ROWS), jnp.int32)
    for d in range(4):
        lengths = lengths + jnp.where(seats == d, docs[d], 0)
    rows = lax.broadcasted_iota(jnp.int32, (8, ROWS), 0)
    places[...] = jnp.where(rows == 1, lengths, total[0:8].astype(jnp.int32))
    z_v.wait_send()
    z_k.wait_send()
    for r in rings:
        r.drain()
    for copy in sideways + onward + swaps:
        copy.wait_send()


def doc_starts(places):
    starts = [jnp.int32(0)]
    for d in range(3):
        starts.append(starts[-1] + places[1, d])
    return starts


def make_plan(places, plan):
    starts = doc_starts(places)

    def visit(pair, items):
        queries = [pair * 2, pair * 2 + 1]
        mine = [places[0, KEY_BLOCKS + query] for query in queries]
        low = []
        for m in mine:
            start = jnp.int32(0)
            for s in starts[1:]:
                start = jnp.where(s <= m * BLK, s, start)
            low.append(lax.div(start, jnp.int32(BLK)))
        at = [query * LIST for query in queries]
        for b in range(KEY_BLOCKS):
            pk = places[0, b]
            for i in range(2):
                plan[at[i]] = jnp.int32(b)
                at[i] = at[i] + ((pk <= mine[i]) & (pk >= low[i])).astype(jnp.int32)
        for i, query in enumerate(queries):
            for j in range(CHUNK):
                plan[at[i] + j] = jnp.int32(0)
            count = at[i] - query * LIST
            plan[COUNTS + query] = count
            for c in range(CHUNKS):
                plan[ITEMS + items] = query * 16 + c
                items = items + (count > c * CHUNK).astype(jnp.int32)
        return items

    items = lax.fori_loop(0, QUERY_BLOCKS // 2, visit, jnp.int32(0))
    plan[ITEMS + items] = jnp.int32(0)
    plan[TOTAL] = items


def item_of(places, plan, starts, at):
    real = at < plan[TOTAL]
    code = plan[ITEMS + at]
    query, chunk = code >> 4, code & 15
    count = jnp.where(real, plan[COUNTS + query], 0)
    row = places[0, KEY_BLOCKS + query] * BLK + (
        lax.broadcasted_iota(jnp.int32, (1, 2 * BLK), 1) & (BLK - 1)
    )
    opens = jnp.zeros((1, 2 * BLK), jnp.int32)
    for s in starts[1:]:
        opens = jnp.where(s <= row, s, opens)
    return query, chunk, real, count, row, opens


def key_chunk(places, plan, item, keys, vals):
    query, chunk, _, count, row, opens = item
    iota = lax.broadcasted_iota(jnp.int32, (BLK, 2 * BLK), 0)
    ks, vs, terms, blocks = [], [], [], []
    for j in range(CHUNK):
        at = chunk * CHUNK + j
        b = plan[query * LIST + at]
        base = jnp.where(at < count, places[0, b] * BLK, jnp.int32(1 << 20))
        ks.append(keys[pl.ds(pl.multiple_of(b * BLK, BLK), BLK), :])
        vs.append(vals[b >> 1, pl.ds(pl.multiple_of((b & 1) * BLK, BLK), BLK), :])
        ok = (iota >= opens - base) & (iota <= row - base)
        term = jnp.where(ok, 0.0, LOW)
        terms.append(jnp.concatenate([term, term], axis=1))
        blocks.append(b)
    return (
        jnp.concatenate(ks, axis=0),
        jnp.concatenate(vs, axis=0),
        jnp.concatenate(terms, axis=0),
        blocks,
    )


def head_stack(ref, query):
    rows = pl.ds(pl.multiple_of((query & 1) * BLK, BLK), BLK)
    return jnp.concatenate(
        [ref[query >> 1, rows, h * HD : (h + 1) * HD] for h in range(GROUP)], axis=0
    )


def stats_kernel(places, keys, vals, qs, gs, out, plan, kept):
    make_plan(places, plan)
    starts = doc_starts(places)
    for c in range(CHUNKS):
        kept[c, 0] = jnp.full((QUERY_BLOCKS, STACK), FLOOR, F32)
        kept[c, 1] = jnp.zeros((QUERY_BLOCKS, STACK), F32)
        kept[c, 2] = jnp.zeros((QUERY_BLOCKS, STACK), F32)

    def step(i, carry):
        found = []
        for part in range(SIDE):
            item = item_of(places, plan, starts, i * SIDE + part)
            k, v, term, _ = key_chunk(places, plan, item, keys, vals)
            q, g = head_stack(qs, item[0]), head_stack(gs, item[0])
            score = lax.dot_general(k, q, NT, preferred_element_type=F32) * LOG2 + term
            d_prob = lax.dot_general(v, g, NT, preferred_element_type=F32)
            top = jnp.maximum(FLOOR, jnp.max(score, axis=0, keepdims=True))
            e = jnp.exp2(score - top)
            found.append((
                item, top, jnp.sum(e, axis=0, keepdims=True), jnp.sum(e * d_prob, axis=0, keepdims=True)
            ))
        for item, top, mass, weighted in found:
            slot = jnp.where(item[2], item[1], CHUNKS)
            for j, value in enumerate((top, mass, weighted)):
                kept[slot, j, pl.ds(item[0], 1), :] = value
        return carry

    lax.fori_loop(0, lax.div(plan[TOTAL] + (SIDE - 1), jnp.int32(SIDE)), step, 0)
    top = kept[0, 0]
    for c in range(1, CHUNKS):
        top = jnp.maximum(top, kept[c, 0])
    mass, weighted = jnp.zeros_like(top), jnp.zeros_like(top)
    for c in range(CHUNKS):
        shrink = jnp.exp2(kept[c, 0] - top)
        mass = mass + kept[c, 1] * shrink
        weighted = weighted + kept[c, 2] * shrink
    out[0], out[1], out[2] = top, mass, weighted


def share_kernel(stats, out, got, send_sem, recv_sem):
    y, zh, x, t = place()
    peers = [device(y, zh, rem(x + j, NX), t) for j in range(1, NX)]
    greet(peers)
    meet(peers)
    copies = [send(stats, got.at[j], (send_sem, recv_sem), j, peer) for j, peer in enumerate(peers)]
    for copy in copies:
        copy.wait_recv()
    parts = [[stats[i] for i in range(3)]] + [[got[j, i] for i in range(3)] for j in range(NX - 1)]
    top = parts[0][0]
    for p in parts[1:]:
        top = jnp.maximum(top, p[0])
    mass = jnp.zeros_like(top)
    weighted = jnp.zeros_like(top)
    for p in parts:
        shrink = jnp.exp2(p[0] - top)
        mass = mass + p[1] * shrink
        weighted = weighted + p[2] * shrink
    out[0] = top
    out[1] = 1.0 / mass
    out[2] = weighted / mass
    for copy in copies:
        copy.wait_send()


def back_kernel(
    places, plan, stats, keys, vals, qs, gs, dq, dk, dv, dq_sum, dk_sum, dv_sum
):
    starts = doc_starts(places)
    dq_sum[...] = jnp.zeros_like(dq_sum)
    dk_sum[...] = jnp.zeros_like(dk_sum)
    dv_sum[...] = jnp.zeros_like(dv_sum)

    def step(i, carry):
        found = []
        for part in range(SIDE):
            item = item_of(places, plan, starts, i * SIDE + part)
            query = item[0]
            k, v, term, blocks = key_chunk(places, plan, item, keys, vals)
            q, g = head_stack(qs, query), head_stack(gs, query)
            top, scale, delta = [stats[j, pl.ds(query, 1), :] for j in range(3)]
            score = lax.dot_general(k, q, NT, preferred_element_type=F32) * LOG2 + term
            d_prob = lax.dot_general(v, g, NT, preferred_element_type=F32)
            prob = jnp.exp2(score - top) * scale
            d_score = (prob * (d_prob - delta)).astype(BF16)
            dv_part = jnp.dot(prob.astype(BF16), g, preferred_element_type=F32)
            dk_part = jnp.dot(d_score, q, preferred_element_type=F32)
            dq_part = jnp.dot(k.T, d_score, preferred_element_type=F32)
            found.append((query, blocks, dq_part, dk_part, dv_part))
        for query, blocks, dq_part, dk_part, dv_part in found:
            dq_sum[query] += dq_part
            for j, b in enumerate(blocks):
                rows = pl.ds(pl.multiple_of(b * BLK, BLK), BLK)
                dv_sum[rows, :] += dv_part[j * BLK : (j + 1) * BLK]
                dk_sum[rows, :] += dk_part[j * BLK : (j + 1) * BLK]
        return carry

    lax.fori_loop(0, lax.div(plan[TOTAL] + (SIDE - 1), jnp.int32(SIDE)), step, 0)
    for query in range(QUERY_BLOCKS):
        dq_rows = (dq_sum[query] * SCALE).astype(BF16).T
        rows = slice((query % 2) * BLK, (query % 2 + 1) * BLK)
        for h in range(GROUP):
            dq[query // 2, rows, h * HD : (h + 1) * HD] = dq_rows[h * BLK : (h + 1) * BLK]
    dk[...] = (dk_sum[...] * SCALE).astype(BF16)
    dv[...] = dv_sum[...].astype(BF16)


class Fold:
    def __init__(self, block, me, n, ups, downs, far, near, made, last, sems, base):
        self.block, self.me, self.n, self.peers, self.sems, self.base = block, me, n, (ups, downs), sems, base
        self.got_far, self.got_near, self.made, self.got_last = far, near, made, last

    def at(self, way, far):
        return self.block(rem(self.me + (far if way == 0 else self.n - far), self.n))

    def go(self, src, dst, i, peer):
        return send(src, dst, self.sems, self.base + i, peer)

    def first(self):
        self.far, self.half, self.near = [], [], []
        for way, peers in enumerate(self.peers):
            part = pl.ds(way * (ROWS // 2), ROWS // 2)
            self.half.append(
                self.go(self.at(way, 4).at[part], self.got_far.at[way, pl.ds(ROWS, ROWS // 2)], way, peers[1])
            )
            self.far.append(
                self.go(self.at(way, 3), self.got_far.at[way, pl.ds(0, ROWS)], 2 + way, peers[0])
            )
        for way, peers in enumerate(self.peers):
            self.near.append(self.go(self.at(way, 1), self.got_near.at[way], 4 + way, peers[0]))

    def second(self):
        self.last = []
        middle = ROWS // 2
        for way, peers in enumerate(self.peers):
            self.far[way].wait_recv()
            self.half[way].wait_recv()
            own, far, out = self.at(way, 2), self.got_far.at[way], self.made.at[way]
            with_half = pl.ds(way * middle, middle)
            without = pl.ds((1 - way) * middle, middle)
            out[without] = (own[without].astype(F32) + far[without].astype(F32)).astype(BF16)
            out[with_half] = (
                own[with_half].astype(F32)
                + far[with_half].astype(F32)
                + far[pl.ds(ROWS, middle)].astype(F32)
            ).astype(BF16)
            self.last.append(self.go(out, self.got_last.at[way], 6 + way, peers[1]))

    def total(self):
        for copy in self.near + self.last:
            copy.wait_recv()
        out = self.block(self.me)[...].astype(F32)
        for way in range(2):
            out = out + self.got_near[way].astype(F32) + self.got_last[way].astype(F32)
        return out

    def drain(self):
        for copy in self.far + self.half + self.near + self.last:
            copy.wait_send()


def reduce_kernel(
    dq, dk, dv, turned, w_all, w_split, d_query, d_value, d_input, d_wkey,
    k_got, f_far, f_near, f_made, f_last, q_got, w_got, z_out, z_got,
    kg, kg_quad, xg, w_last, w_part, in_part, in_got, zw_out, zw_got,
    k_send, k_recv, f_send, f_recv, w_send, w_recv, x_send, x_recv, z_send, z_recv, s_send, s_recv, load_sem,
):
    y, zh, x, t = place()
    zl, core = lax.div(t, jnp.int32(NC)), rem(t, NC)
    others_y = [device(rem(y + j, NY), zh, x, t) for j in range(1, NY)]
    ups, downs = others_y[:2], [others_y[-1], others_y[-2]]
    others_x = [device(y, zh, rem(x + j, NX), t) for j in range(1, NX)]
    partner = device(y, 1 - zh, x, t)
    half = lax.div(zl, jnp.int32(2))
    quarter, quad = quad_of(y, zh, x, zl, core)
    over = device(y, zh, x, rem(zl + 2, 4) * NC + core)
    x_sems, z_sems, s_sems = (x_send, x_recv), (z_send, z_recv), (s_send, s_recv)
    peers = [partner] + others_y + others_x + quad + [over]
    greet(peers)
    own_x = pltpu.make_async_copy(turned.at[x], xg.at[x], load_sem.at[0])
    own_x.start()
    meet(peers)

    def fold(arr, z, i):
        return Fold(
            lambda o: arr.at[z, o], y, NY, ups, downs,
            f_far.at[i], f_near.at[i], f_made.at[i], f_last.at[i], (f_send, f_recv), 8 * i,
        )

    far = 1 - zh
    v_far, v_own = fold(dv, far, 0), fold(dv, zh, 1)

    def straight(i, z):
        return [
            send(
                dk.at[z, rem(y + j, NY)], k_got.at[i, j - 1], (k_send, k_recv), i * (NY - 1) + j - 1,
                others_y[j - 1],
            )
            for j in (4, 3, 5, 2, 6, 1, 7)
        ]

    def k_total(i, z, copies):
        for copy in copies:
            copy.wait_recv()
        out = dk[z, y].astype(F32)
        for j in range(NY - 1):
            out = out + k_got[i, j].astype(F32)
        return out

    k_far = straight(0, far)
    x_sends = [
        send(turned.at[rem(x + j, NX)], xg.at[x], x_sems, j - 1, others_x[j - 1]) for j in (2, 1, 3)
    ]
    w_swap = send(w_split.at[:, 1 - quarter, 1 - core], w_last, s_sems, 4, quad[2])
    for copy in k_far:
        copy.wait_send()
    k_own = straight(1, zh)
    z_out[0] = k_total(0, far, k_far).astype(BF16)
    z_key = send(z_out.at[0], z_got.at[0], z_sems, 0, partner)
    v_far.first()
    v_own.first()
    key_sum = k_total(1, zh, k_own)
    z_key.wait_recv()
    kg[x] = (key_sum + z_got[0].astype(F32)).astype(BF16)

    kg_sends = [send(kg.at[x], kg.at[x], x_sems, 2 + j, others_x[j - 1]) for j in (2, 1, 3)]
    kg_swaps = [send(kg.at[x], kg_quad.at[j], s_sems, j, quad[j]) for j in range(3)]
    q_sends = [
        send(dq.at[rem(x + j, NX)], q_got.at[j - 1], x_sems, 5 + j, others_x[j - 1]) for j in (2, 1, 3)
    ]
    v_far.second()
    v_own.second()
    own_x.wait()
    for copy in x_sends + kg_sends:
        copy.wait_recv()
    heads = [kg[src] for src in range(NX)]
    w_sends = []

    def spread_product(turn, z):
        product = jnp.zeros((NY * BLK, HD), F32)
        for src in range(NX):
            rows = xg[src, z].reshape(NY * BLK, ROWS)
            product = product + jnp.dot(rows, heads[src], preferred_element_type=F32)
        w_part[turn] = product.astype(BF16).reshape(NY, BLK, HD)
        for j in (4, 3, 5, 2, 6, 1, 7):
            w_sends.append(
                send(
                    w_part.at[turn, rem(y + j, NY)], w_got.at[turn, j - 1],
                    (w_send, w_recv), turn * (NY - 1) + j - 1, others_y[j - 1],
                )
            )

    spread_product(0, far)

    def w_total(turn):
        for copy in w_sends[turn * (NY - 1) : (turn + 1) * (NY - 1)]:
            copy.wait_recv()
        out = w_part[turn, y].astype(F32)
        for j in range(NY - 1):
            out = out + w_got[turn, j].astype(F32)
        return out

    for copy in [w_swap] + kg_swaps:
        copy.wait_recv()
    quad_heads = [kg[x]] + [kg_quad[j] for j in range(3)]

    def in_block(h):
        out = jnp.zeros((ROWS, w_all.shape[2]), F32)
        for j, head in enumerate(quad_heads):
            rows = w_all[j, h] if j < 3 else w_last[h]
            out = out + lax.dot_general(head, rows, NT, preferred_element_type=F32)
        return out

    in_part[...] = in_block(1 - half).astype(BF16)
    in_send = send(in_part, in_got, s_sems, 3, over)

    spread_product(1, zh)
    z_out[1] = v_far.total().astype(BF16)
    z_val = send(z_out.at[1], z_got.at[1], z_sems, 1, partner)
    in_sum = in_block(half)
    zw_out[...] = w_total(0).astype(BF16)
    z_w = send(zw_out, zw_got, z_sems, 2, partner)
    q_sum = dq[x].astype(F32)
    for copy in q_sends:
        copy.wait_recv()
    for j in range(NX - 1):
        q_sum = q_sum + q_got[j].astype(F32)
    d_query[...] = q_sum.astype(BF16)
    in_send.wait_recv()
    d_input[...] = (in_sum + in_got[...].astype(F32)).astype(BF16)
    z_val.wait_recv()
    d_value[...] = (v_own.total() + z_got[1].astype(F32)).astype(BF16)
    w_sum = w_total(1)
    z_w.wait_recv()
    d_wkey[...] = w_sum + zw_got[...].astype(F32)

    for f in (v_far, v_own):
        f.drain()
    for copy in [z_key, z_val, z_w, in_send, w_swap] + k_own + x_sends + kg_sends + q_sends + w_sends + kg_swaps:
        copy.wait_send()


def dma(n):
    return pltpu.SemaphoreType.DMA((n,))


def params(collective_id=None):
    return pltpu.CompilerParams(
        collective_id=collective_id,
        has_side_effects=collective_id is not None,
        vmem_limit_bytes=VMEM_LIMIT,
    )


def in_hbm(array):
    return pltpu.with_memory_space_constraint(array, pltpu.HBM)


def hand_over_kernel(*refs):
    n = (len(refs) - 1) // 2
    copies = [
        pltpu.make_async_copy(refs[i], refs[n + i], refs[-1].at[i]) for i in range(n)
    ]
    for copy in copies:
        copy.start()
    for copy in copies:
        copy.wait()


def on_device(nl, inputs, w_key, values, queries, d_out, doc_lens, block_pos):
    width = inputs.shape[1]
    pairs = NZ * NY
    shape = jax.ShapeDtypeStruct
    slice_width = width // (nl * NC)
    w_split = w_key.reshape(2, 2, NC, slice_width, HD)
    keys, vals, qs, gs, turned, w_all, places = pl.pallas_call(
        gather_kernel,
        out_shape=(
            shape((NZ, NY, ROWS, HD), BF16),
            shape((NZ, NY, ROWS + 16, HD), BF16),
            shape((NX, ROWS, GROUP * HD), BF16),
            shape((NX, ROWS + 16, GROUP * HD), BF16),
            shape((NX, NZ, NY, BLK, ROWS), BF16),
            shape((3, 2, slice_width, HD), BF16),
            shape((8, ROWS), jnp.int32),
        ),
        in_specs=[hbm] * 8,
        out_specs=(vmem,) * 7,
        scratch_shapes=[
            pltpu.VMEM((ROWS, width), BF16),
            pltpu.VMEM((width, HD), BF16),
            pltpu.SMEM((4,), jnp.int32),
            pltpu.SMEM((2,), jnp.int32),
            dma(32), dma(32), dma(8), dma(8), dma(2), dma(2), dma(2), dma(2), dma(6 + 2 * PARTS),
        ],
        compiler_params=params(1),
        name="gather_rows",
    )(*(in_hbm(a) for a in (inputs, w_key, w_split, values, queries, d_out, doc_lens, block_pos)))
    keys = keys.reshape(KEY_BLOCKS * BLK, HD)
    vals = vals.reshape(pairs, ROWS + 16, HD)
    stats, plan = pl.pallas_call(
        stats_kernel,
        out_shape=(shape((3, QUERY_BLOCKS, STACK), F32), shape((PLAN,), jnp.int32)),
        in_specs=[smem, vmem, vmem, vmem, vmem],
        out_specs=(vmem, smem),
        scratch_shapes=[pltpu.VMEM((CHUNKS + 1, 3, QUERY_BLOCKS, STACK), F32)],
        compiler_params=params(),
        name="row_stats",
    )(places, keys, vals, qs, gs)
    stats = pl.pallas_call(
        share_kernel,
        out_shape=shape((3, QUERY_BLOCKS, STACK), F32),
        in_specs=[vmem],
        out_specs=vmem,
        scratch_shapes=[
            pltpu.VMEM((NX - 1, 3, QUERY_BLOCKS, STACK), F32), dma(NX - 1), dma(NX - 1),
        ],
        compiler_params=params(2),
        name="share_stats",
    )(stats)
    dq, dk, dv = pl.pallas_call(
        back_kernel,
        out_shape=(
            shape((NX, ROWS, GROUP * HD), BF16),
            shape((KEY_BLOCKS * BLK, HD), BF16),
            shape((KEY_BLOCKS * BLK, HD), BF16),
        ),
        in_specs=[smem, smem, vmem, vmem, vmem, vmem, vmem],
        out_specs=(vmem,) * 3,
        scratch_shapes=[
            pltpu.VMEM((QUERY_BLOCKS, HD, STACK), F32),
            pltpu.VMEM((KEY_BLOCKS * BLK, HD), F32),
            pltpu.VMEM((KEY_BLOCKS * BLK, HD), F32),
        ],
        compiler_params=params(),
        name="back_tiles",
    )(places, plan, stats, keys, vals, qs, gs)
    block = (ROWS, HD)
    results = pl.pallas_call(
        reduce_kernel,
        out_shape=(
            shape((ROWS, GROUP * HD), BF16),
            shape((ROWS, HD), BF16),
            shape((ROWS, slice_width), BF16),
            shape((BLK, HD), F32),
        ),
        in_specs=[vmem] * 5 + [hbm],
        out_specs=(vmem,) * 4,
        scratch_shapes=[
            pltpu.VMEM((NZ, NY - 1) + block, BF16),
            pltpu.VMEM((2, 2, ROWS + ROWS // 2, HD), BF16),
            pltpu.VMEM((2, 2) + block, BF16),
            pltpu.VMEM((2, 2) + block, BF16),
            pltpu.VMEM((2, 2) + block, BF16),
            pltpu.VMEM((NX - 1, ROWS, GROUP * HD), BF16),
            pltpu.VMEM((NZ, NY - 1, BLK, HD), BF16),
            pltpu.VMEM((2,) + block, BF16),
            pltpu.VMEM((2,) + block, BF16),
            pltpu.VMEM((NX,) + block, BF16),
            pltpu.VMEM((3,) + block, BF16),
            pltpu.VMEM((NX, NZ, NY, BLK, ROWS), BF16),
            pltpu.VMEM((2, slice_width, HD), BF16),
            pltpu.VMEM((NZ, NY, BLK, HD), BF16),
            pltpu.VMEM((ROWS, slice_width), BF16),
            pltpu.VMEM((ROWS, slice_width), BF16),
            pltpu.VMEM((BLK, HD), BF16),
            pltpu.VMEM((BLK, HD), BF16),
            dma(2 * (NY - 1)), dma(2 * (NY - 1)), dma(16), dma(16), dma(2 * (NY - 1)), dma(2 * (NY - 1)), dma(9), dma(9), dma(3), dma(3),
            dma(5), dma(5), dma(1),
        ],
        compiler_params=params(3),
        name="reduce_grads",
    )(dq, dk.reshape(NZ, NY, ROWS, HD), dv.reshape(NZ, NY, ROWS, HD), turned, w_all, in_hbm(w_split))
    return pl.pallas_call(
        hand_over_kernel,
        out_shape=tuple(shape(r.shape, r.dtype) for r in results),
        in_specs=[vmem] * 4,
        out_specs=(hbm,) * 4,
        scratch_shapes=[dma(4)],
        compiler_params=params(),
        name="hand_over",
    )(*results)


def solution(mesh):
    nl = mesh.shape["tensor"] // NC
    return jax.shard_map(
        functools.partial(on_device, nl),
        mesh=mesh,
        in_specs=(
            P("dp", None),
            P(None, "tensor"),
            P("dp", "tensor"),
            P("dp", "tensor"),
            P("dp", "tensor"),
            P(),
            P("dp"),
        ),
        out_specs=(P("dp", "tensor"), P("dp", "tensor"), P("dp", "tensor"), P("dp", "tensor")),
        check_vma=False,
    )
```

```python
import functools
import math

import jax
import jax.numpy as jnp
from jax import lax
from jax.experimental import pallas as pl
from jax.experimental.pallas import tpu as pltpu
from jax.sharding import PartitionSpec as P

MESH = pl.DeviceIdType.MESH
F32, BF16 = jnp.float32, jnp.bfloat16
HD, BLK, GROUP, ROWS = 128, 64, 4, 128
NX, NZ, NY, NC = 4, 2, 8, 2
HY, HX = NY // 2, NX // 2
KEY_BLOCKS = 2 * NZ * NY
QUERY_BLOCKS = 2 * NX
STACK = GROUP * BLK
CHUNK = 4
CHUNKS = KEY_BLOCKS // CHUNK
SIDE, WIDE = 4, 8
PARTS = 4
LIST, COUNTS, ITEMS, TOTAL, PLAN = 40, 320, 336, 416, 512
SCALE = 1.0 / math.sqrt(HD)
LOG2 = SCALE / math.log(2.0)
LOW = -1e30
FLOOR = -1e29
NT = (((1,), (1,)), ((), ()))
VMEM_LIMIT = 40 * 1024 * 1024

vmem = pl.BlockSpec(memory_space=pltpu.VMEM)
smem = pl.BlockSpec(memory_space=pltpu.SMEM)
hbm = pl.BlockSpec(memory_space=pltpu.HBM)


def rem(a, n):
    return lax.rem(a, jnp.int32(n))


def place():
    dp, tensor = lax.axis_index("dp"), lax.axis_index("tensor")
    x = rem(dp, NX)
    rest = lax.div(dp, jnp.int32(NX))
    return lax.div(rest, jnp.int32(NZ)), rem(rest, NZ), x, tensor


def device(y, zh, x, tensor):
    return ((y * NZ + zh) * NX + x, tensor)


def quad_of(y, zh, x, zl, core):
    quarter = rem(zl, 2)
    near = zl + 1 - 2 * quarter
    places = ((zl, 1 - core), (near, core), (near, 1 - core))
    return quarter, [device(y, zh, x, chip * NC + c) for chip, c in places]


def greet(peers):
    barrier = pltpu.get_barrier_semaphore()
    for peer in peers:
        pl.semaphore_signal(barrier, inc=1, device_id=peer, device_id_type=MESH)


def meet(peers):
    pl.semaphore_wait(pltpu.get_barrier_semaphore(), len(peers))


def send(src, dst, sems, index, peer):
    copy = pltpu.make_async_remote_copy(
        src_ref=src,
        dst_ref=dst,
        send_sem=sems[0].at[index],
        recv_sem=sems[1].at[index],
        device_id=peer,
        device_id_type=MESH,
    )
    copy.start()
    return copy


class Tree:
    def __init__(self, block, half, me, n, ups, downs, sems, base):
        self.block, self.half, self.me, self.n = block, half, me, n
        self.ups, self.downs, self.sems, self.base = ups, downs, sems, base

    def first(self):
        own = self.block(self.me)
        self.near = [
            send(own, own, self.sems, self.base + i, peer)
            for i, peer in enumerate((self.ups[1], self.downs[1], self.ups[0], self.downs[0]))
        ]

    def second(self):
        self.far = []
        for way, peers in enumerate((self.ups, self.downs)):
            self.near[way].wait_recv()
            ref = self.block(rem(self.me + (self.n - 2 if way == 0 else 2), self.n))
            half = self.half(ref, way)
            self.far.append(send(half, half, self.sems, self.base + 4 + 2 * way, peers[1]))
            self.far.append(send(ref, ref, self.sems, self.base + 5 + 2 * way, peers[0]))

    def end(self):
        for copy in self.near[2:] + self.far:
            copy.wait_recv()

    def drain(self):
        for copy in self.near + self.far:
            copy.wait_send()


def gather_kernel(
    inputs, w_key, w_split, values, queries, d_out, doc_lens, block_pos,
    keys, vals, qs, gs, turned, w_all, places,
    x_buf, w_buf, docs, pos, y_send, y_recv, x_send, x_recv, z_send, z_recv, s_send, s_recv, load_sem,
):
    y, zh, x, t = place()
    ups = [device(rem(y + j, NY), zh, x, t) for j in (1, 2)]
    downs = [device(rem(y + NY - j, NY), zh, x, t) for j in (1, 2)]
    others_x = [device(y, zh, rem(x + j, NX), t) for j in range(1, NX)]
    partner = device(y, 1 - zh, x, t)
    zl, core = lax.div(t, jnp.int32(NC)), rem(t, NC)
    quarter, quad = quad_of(y, zh, x, zl, core)
    peers = [partner] + ups + downs + others_x + quad[:2]
    greet(peers)
    loads = [
        pltpu.make_async_copy(src, dst, load_sem.at[i])
        for i, (src, dst) in enumerate(
            (
                (block_pos, pos),
                (values, vals.at[zh, y, pl.ds(0, ROWS)]),
                (d_out, gs.at[x, pl.ds(0, ROWS)]),
                (queries, qs.at[x]),
                (doc_lens, docs),
                (w_split.at[:, quarter, core], w_all.at[0]),
            )
        )
    ]
    depth = inputs.shape[1] // PARTS
    parts = []
    for i in range(PARTS):
        cut = slice(i * depth, (i + 1) * depth)
        parts.append((
            pltpu.make_async_copy(w_key.at[cut], w_buf.at[cut], load_sem.at[6 + 2 * i]),
            pltpu.make_async_copy(inputs.at[:, cut], x_buf.at[:, cut], load_sem.at[7 + 2 * i]),
        ))
    for load in loads[:5] + [load for pair in parts for load in pair] + loads[5:]:
        load.start()
    loads[0].wait()
    lane = lax.broadcasted_iota(jnp.int32, (16, ROWS), 1)
    first = 2 * (zh * NY + y)
    mine = jnp.where(lane == first, pos[0], 0) + jnp.where(lane == first + 1, pos[1], 0)
    seat = KEY_BLOCKS + 2 * x
    here = jnp.where(lane == seat, pos[0], 0) + jnp.where(lane == seat + 1, pos[1], 0)
    vals[zh, y, ROWS : ROWS + 16, :] = mine.astype(F32).astype(BF16)
    gs[x, ROWS : ROWS + 16, 0:HD] = here.astype(F32).astype(BF16)
    gs[x, ROWS : ROWS + 16, HD:] = jnp.zeros((16, (GROUP - 1) * HD), BF16)
    projected = jnp.zeros((ROWS, HD), F32)
    for i, pair in enumerate(parts):
        cut = slice(i * depth, (i + 1) * depth)
        for load in pair:
            load.wait()
        projected = projected + jnp.dot(
            x_buf[:, cut], w_buf[cut, :], preferred_element_type=F32
        )
    keys[zh, y] = projected.astype(BF16)
    for load in loads[1:4]:
        load.wait()
    meet(peers)

    y_sems, x_sems, z_sems = (y_send, y_recv), (x_send, x_recv), (z_send, z_recv)

    def half_k(ref, way):
        return ref.at[pl.ds(way * 64, 64)]

    def half_v(ref, way):
        return ref.at[pl.ds(0, 64)] if way == 0 else ref.at[pl.ds(64, ROWS + 16 - 64)]

    def tree(arr, half, z, base):
        return Tree(lambda o: arr.at[z, o], half, y, NY, ups, downs, y_sems, base)

    v_own, k_own = tree(vals, half_v, zh, 0), tree(keys, half_k, zh, 8)
    v_far, k_far = tree(vals, half_v, 1 - zh, 16), tree(keys, half_k, 1 - zh, 24)

    z_k = send(keys.at[zh, y], keys.at[zh, y], z_sems, 1, partner)
    z_v = send(vals.at[zh, y], vals.at[zh, y], z_sems, 0, partner)
    k_own.first()
    v_own.first()
    right, left = others_x[0], others_x[-1]
    sideways = []
    for i, (arr, _) in enumerate(((gs, half_v), (qs, half_k))):
        for way, peer in enumerate((right, left)):
            sideways.append(send(arr.at[x], arr.at[x], x_sems, 2 * i + way, peer))

    def turn(first, last):
        def body(j, carry):
            tile = x_buf[:, pl.ds(pl.multiple_of(j * 128, 128), 128)].T
            for part in range(2):
                b = 2 * j + part
                pair = lax.div(b, jnp.int32(NX))
                turned[rem(b, NX), rem(pair, NZ), lax.div(pair, jnp.int32(NZ))] = tile[
                    part * 64 : part * 64 + 64
                ]
            return carry

        lax.fori_loop(first, last, body, 0)

    tiles = inputs.shape[1] // 128
    onward = []

    def pass_on(i, arr, half):
        for way, peer in enumerate((right, left)):
            sideways[2 * i + way].wait_recv()
            ref = half(arr.at[rem(x + (NX - 1 if way == 0 else 1), NX)], way)
            onward.append(send(ref, ref, x_sems, 4 + 2 * i + way, peer))

    turn(0, tiles // 4)
    k_own.second()
    v_own.second()
    z_k.wait_recv()
    k_far.first()
    z_v.wait_recv()
    v_far.first()
    sides = ((quarter, 1 - core), (1 - quarter, core))
    swaps = [
        send(w_split.at[:, q, c], w_all.at[j + 1], (s_send, s_recv), j, quad[j])
        for j, (q, c) in enumerate(sides)
    ]
    pass_on(0, gs, half_v)
    turn(tiles // 4, tiles // 2)
    k_far.second()
    pass_on(1, qs, half_k)
    v_far.second()
    turn(tiles // 2, tiles)
    loads[4].wait()
    loads[5].wait()
    rings = (v_own, k_own, v_far, k_far)
    for r in rings:
        r.end()
    for copy in onward + swaps:
        copy.wait_recv()
    total = jnp.zeros((16, ROWS), F32)
    for z in range(NZ):
        for j in range(NY):
            total = total + vals[z, j, ROWS : ROWS + 16, :].astype(F32)
    for j in range(NX):
        total = total + gs[j, ROWS : ROWS + 16, 0:HD].astype(F32)
    seats = lax.broadcasted_iota(jnp.int32, (8, ROWS), 1)
    lengths = jnp.zeros((8, ROWS), jnp.int32)
    for d in range(4):
        lengths = lengths + jnp.where(seats == d, docs[d], 0)
    rows = lax.broadcasted_iota(jnp.int32, (8, ROWS), 0)
    places[...] = jnp.where(rows == 1, lengths, total[0:8].astype(jnp.int32))
    z_v.wait_send()
    z_k.wait_send()
    for r in rings:
        r.drain()
    for copy in sideways + onward + swaps:
        copy.wait_send()


def doc_starts(places):
    starts = [jnp.int32(0)]
    for d in range(3):
        starts.append(starts[-1] + places[1, d])
    return starts


def make_plan(places, plan):
    starts = doc_starts(places)

    def visit(pair, items):
        queries = [pair * 2, pair * 2 + 1]
        mine = [places[0, KEY_BLOCKS + query] for query in queries]
        low = []
        for m in mine:
            start = jnp.int32(0)
            for s in starts[1:]:
                start = jnp.where(s <= m * BLK, s, start)
            low.append(lax.div(start, jnp.int32(BLK)))
        at = [query * LIST for query in queries]
        for b in range(KEY_BLOCKS):
            pk = places[0, b]
            for i in range(2):
                plan[at[i]] = jnp.int32(b)
                at[i] = at[i] + ((pk <= mine[i]) & (pk >= low[i])).astype(jnp.int32)
        for i, query in enumerate(queries):
            for j in range(CHUNK):
                plan[at[i] + j] = jnp.int32(0)
            count = at[i] - query * LIST
            plan[COUNTS + query] = count
            for c in range(CHUNKS):
                plan[ITEMS + items] = query * 16 + c
                items = items + (count > c * CHUNK).astype(jnp.int32)
        return items

    items = lax.fori_loop(0, QUERY_BLOCKS // 2, visit, jnp.int32(0))
    for j in range(SIDE):
        plan[ITEMS + items + j] = jnp.int32(0)
    plan[TOTAL] = items


def item_of(places, plan, starts, at):
    real = at < plan[TOTAL]
    code = plan[ITEMS + at]
    query, chunk = code >> 4, code & 15
    count = jnp.where(real, plan[COUNTS + query], 0)
    row = places[0, KEY_BLOCKS + query] * BLK + (
        lax.broadcasted_iota(jnp.int32, (1, 2 * BLK), 1) & (BLK - 1)
    )
    opens = jnp.zeros((1, 2 * BLK), jnp.int32)
    for s in starts[1:]:
        opens = jnp.where(s <= row, s, opens)
    return query, chunk, real, count, row, opens


def key_chunk(places, plan, item, keys, vals):
    query, chunk, _, count, row, opens = item
    iota = lax.broadcasted_iota(jnp.int32, (BLK, 2 * BLK), 0)
    ks, vs, terms, blocks = [], [], [], []
    for j in range(CHUNK):
        at = chunk * CHUNK + j
        b = plan[query * LIST + at]
        base = jnp.where(at < count, places[0, b] * BLK, jnp.int32(1 << 20))
        ks.append(keys[pl.ds(pl.multiple_of(b * BLK, BLK), BLK), :])
        vs.append(vals[b >> 1, pl.ds(pl.multiple_of((b & 1) * BLK, BLK), BLK), :])
        ok = (iota >= opens - base) & (iota <= row - base)
        term = jnp.where(ok, 0.0, LOW)
        terms.append(jnp.concatenate([term, term], axis=1))
        blocks.append(b)
    return (
        jnp.concatenate(ks, axis=0),
        jnp.concatenate(vs, axis=0),
        jnp.concatenate(terms, axis=0),
        blocks,
    )


def over_items(plan, step):
    total = plan[TOTAL]
    wide = lax.div(total, jnp.int32(WIDE))
    rest = lax.div(total - wide * WIDE + (SIDE - 1), jnp.int32(SIDE))

    def wide_step(i, carry):
        step(i * WIDE, WIDE)
        return carry

    def side_step(i, carry):
        step(wide * WIDE + i * SIDE, SIDE)
        return carry

    lax.fori_loop(0, wide, wide_step, 0)
    lax.fori_loop(0, rest, side_step, 0)


def head_stack(ref, query):
    rows = pl.ds(pl.multiple_of((query & 1) * BLK, BLK), BLK)
    return jnp.concatenate(
        [ref[query >> 1, rows, h * HD : (h + 1) * HD] for h in range(GROUP)], axis=0
    )


def stats_kernel(places, keys, vals, qs, gs, out, plan, kept):
    make_plan(places, plan)
    starts = doc_starts(places)
    for c in range(CHUNKS):
        kept[c, 0] = jnp.full((QUERY_BLOCKS, STACK), FLOOR, F32)
        kept[c, 1] = jnp.zeros((QUERY_BLOCKS, STACK), F32)
        kept[c, 2] = jnp.zeros((QUERY_BLOCKS, STACK), F32)

    def step(first, width):
        found = []
        for part in range(width):
            item = item_of(places, plan, starts, first + part)
            k, v, term, _ = key_chunk(places, plan, item, keys, vals)
            q, g = head_stack(qs, item[0]), head_stack(gs, item[0])
            score = lax.dot_general(k, q, NT, preferred_element_type=F32) * LOG2 + term
            d_prob = lax.dot_general(v, g, NT, preferred_element_type=F32)
            top = jnp.maximum(FLOOR, jnp.max(score, axis=0, keepdims=True))
            e = jnp.exp2(score - top)
            found.append((
                item, top, jnp.sum(e, axis=0, keepdims=True), jnp.sum(e * d_prob, axis=0, keepdims=True)
            ))
        for item, top, mass, weighted in found:
            slot = jnp.where(item[2], item[1], CHUNKS)
            for j, value in enumerate((top, mass, weighted)):
                kept[slot, j, pl.ds(item[0], 1), :] = value

    over_items(plan, step)
    top = kept[0, 0]
    for c in range(1, CHUNKS):
        top = jnp.maximum(top, kept[c, 0])
    mass, weighted = jnp.zeros_like(top), jnp.zeros_like(top)
    for c in range(CHUNKS):
        shrink = jnp.exp2(kept[c, 0] - top)
        mass = mass + kept[c, 1] * shrink
        weighted = weighted + kept[c, 2] * shrink
    out[0], out[1], out[2] = top, mass, weighted


def share_kernel(stats, out, got, send_sem, recv_sem):
    y, zh, x, t = place()
    peers = [device(y, zh, rem(x + j, NX), t) for j in range(1, NX)]
    greet(peers)
    meet(peers)
    copies = [send(stats, got.at[j], (send_sem, recv_sem), j, peer) for j, peer in enumerate(peers)]
    for copy in copies:
        copy.wait_recv()
    parts = [[stats[i] for i in range(3)]] + [[got[j, i] for i in range(3)] for j in range(NX - 1)]
    top = parts[0][0]
    for p in parts[1:]:
        top = jnp.maximum(top, p[0])
    mass = jnp.zeros_like(top)
    weighted = jnp.zeros_like(top)
    for p in parts:
        shrink = jnp.exp2(p[0] - top)
        mass = mass + p[1] * shrink
        weighted = weighted + p[2] * shrink
    out[0] = top
    out[1] = 1.0 / mass
    out[2] = weighted / mass
    for copy in copies:
        copy.wait_send()


def back_kernel(
    places, plan, stats, keys, vals, qs, gs, dq, dk, dv, dq_sum, dk_sum, dv_sum
):
    starts = doc_starts(places)
    dq_sum[...] = jnp.zeros_like(dq_sum)
    dk_sum[...] = jnp.zeros_like(dk_sum)
    dv_sum[...] = jnp.zeros_like(dv_sum)

    def step(first, width):
        found = []
        for part in range(width):
            item = item_of(places, plan, starts, first + part)
            query = item[0]
            k, v, term, blocks = key_chunk(places, plan, item, keys, vals)
            q, g = head_stack(qs, query), head_stack(gs, query)
            top, scale, delta = [stats[j, pl.ds(query, 1), :] for j in range(3)]
            score = lax.dot_general(k, q, NT, preferred_element_type=F32) * LOG2 + term
            d_prob = lax.dot_general(v, g, NT, preferred_element_type=F32)
            prob = jnp.exp2(score - top) * scale
            d_score = (prob * (d_prob - delta)).astype(BF16)
            dv_part = jnp.dot(prob.astype(BF16), g, preferred_element_type=F32)
            dk_part = jnp.dot(d_score, q, preferred_element_type=F32)
            dq_part = jnp.dot(k.T, d_score, preferred_element_type=F32)
            found.append((query, blocks, dq_part, dk_part, dv_part))
        for query, blocks, dq_part, dk_part, dv_part in found:
            dq_sum[query] += dq_part
            for j, b in enumerate(blocks):
                rows = pl.ds(pl.multiple_of(b * BLK, BLK), BLK)
                dv_sum[rows, :] += dv_part[j * BLK : (j + 1) * BLK]
                dk_sum[rows, :] += dk_part[j * BLK : (j + 1) * BLK]

    over_items(plan, step)
    for query in range(QUERY_BLOCKS):
        dq_rows = (dq_sum[query] * SCALE).astype(BF16).T
        rows = slice((query % 2) * BLK, (query % 2 + 1) * BLK)
        for h in range(GROUP):
            dq[query // 2, rows, h * HD : (h + 1) * HD] = dq_rows[h * BLK : (h + 1) * BLK]
    dk[...] = (dk_sum[...] * SCALE).astype(BF16)
    dv[...] = dv_sum[...].astype(BF16)


class Fold:
    def __init__(self, block, me, n, ups, downs, far, near, made, last, sems, base):
        self.block, self.me, self.n, self.peers, self.sems, self.base = block, me, n, (ups, downs), sems, base
        self.got_far, self.got_near, self.made, self.got_last = far, near, made, last

    def at(self, way, far):
        return self.block(rem(self.me + (far if way == 0 else self.n - far), self.n))

    def go(self, src, dst, i, peer):
        return send(src, dst, self.sems, self.base + i, peer)

    def first(self):
        self.far, self.half, self.near = [], [], []
        for way, peers in enumerate(self.peers):
            part = pl.ds(way * (ROWS // 2), ROWS // 2)
            self.half.append(
                self.go(self.at(way, 4).at[part], self.got_far.at[way, pl.ds(ROWS, ROWS // 2)], way, peers[1])
            )
            self.far.append(
                self.go(self.at(way, 3), self.got_far.at[way, pl.ds(0, ROWS)], 2 + way, peers[0])
            )
        for way, peers in enumerate(self.peers):
            self.near.append(self.go(self.at(way, 1), self.got_near.at[way], 4 + way, peers[0]))

    def second(self):
        self.last = []
        middle = ROWS // 2
        for way, peers in enumerate(self.peers):
            self.far[way].wait_recv()
            self.half[way].wait_recv()
            own, far, out = self.at(way, 2), self.got_far.at[way], self.made.at[way]
            with_half = pl.ds(way * middle, middle)
            without = pl.ds((1 - way) * middle, middle)
            out[without] = (own[without].astype(F32) + far[without].astype(F32)).astype(BF16)
            out[with_half] = (
                own[with_half].astype(F32)
                + far[with_half].astype(F32)
                + far[pl.ds(ROWS, middle)].astype(F32)
            ).astype(BF16)
            self.last.append(self.go(out, self.got_last.at[way], 6 + way, peers[1]))

    def total(self):
        for copy in self.near + self.last:
            copy.wait_recv()
        out = self.block(self.me)[...].astype(F32)
        for way in range(2):
            out = out + self.got_near[way].astype(F32) + self.got_last[way].astype(F32)
        return out

    def drain(self):
        for copy in self.far + self.half + self.near + self.last:
            copy.wait_send()


def reduce_kernel(
    dq, dk, dv, turned, w_all, w_split, d_query, d_value, d_input, d_wkey,
    k_got, f_far, f_near, f_made, f_last, q_got, w_got, z_out, z_got,
    kg, kg_quad, xg, w_last, w_part, in_part, in_got, zw_out, zw_got,
    k_send, k_recv, f_send, f_recv, w_send, w_recv, x_send, x_recv, z_send, z_recv, s_send, s_recv, load_sem,
):
    y, zh, x, t = place()
    zl, core = lax.div(t, jnp.int32(NC)), rem(t, NC)
    others_y = [device(rem(y + j, NY), zh, x, t) for j in range(1, NY)]
    ups, downs = others_y[:2], [others_y[-1], others_y[-2]]
    others_x = [device(y, zh, rem(x + j, NX), t) for j in range(1, NX)]
    partner = device(y, 1 - zh, x, t)
    half = lax.div(zl, jnp.int32(2))
    quarter, quad = quad_of(y, zh, x, zl, core)
    over = device(y, zh, x, rem(zl + 2, 4) * NC + core)
    x_sems, z_sems, s_sems = (x_send, x_recv), (z_send, z_recv), (s_send, s_recv)
    peers = [partner] + others_y + others_x + quad + [over]
    greet(peers)
    own_x = pltpu.make_async_copy(turned.at[x], xg.at[x], load_sem.at[0])
    own_x.start()
    meet(peers)

    def fold(arr, z, i):
        return Fold(
            lambda o: arr.at[z, o], y, NY, ups, downs,
            f_far.at[i], f_near.at[i], f_made.at[i], f_last.at[i], (f_send, f_recv), 8 * i,
        )

    far = 1 - zh
    v_far, v_own = fold(dv, far, 0), fold(dv, zh, 1)

    def straight(i, z):
        return [
            send(
                dk.at[z, rem(y + j, NY)], k_got.at[i, j - 1], (k_send, k_recv), i * (NY - 1) + j - 1,
                others_y[j - 1],
            )
            for j in (4, 3, 5, 2, 6, 1, 7)
        ]

    def k_total(i, z, copies):
        for copy in copies:
            copy.wait_recv()
        out = dk[z, y].astype(F32)
        for j in range(NY - 1):
            out = out + k_got[i, j].astype(F32)
        return out

    k_far = straight(0, far)
    x_sends = [
        send(turned.at[rem(x + j, NX)], xg.at[x], x_sems, j - 1, others_x[j - 1]) for j in (2, 1, 3)
    ]
    w_swap = send(w_split.at[:, 1 - quarter, 1 - core], w_last, s_sems, 4, quad[2])
    for copy in k_far:
        copy.wait_send()
    k_own = straight(1, zh)
    z_out[0] = k_total(0, far, k_far).astype(BF16)
    z_key = send(z_out.at[0], z_got.at[0], z_sems, 0, partner)
    v_far.first()
    v_own.first()
    key_sum = k_total(1, zh, k_own)
    z_key.wait_recv()
    kg[x] = (key_sum + z_got[0].astype(F32)).astype(BF16)

    kg_sends = [send(kg.at[x], kg.at[x], x_sems, 2 + j, others_x[j - 1]) for j in (2, 1, 3)]
    kg_swaps = [send(kg.at[x], kg_quad.at[j], s_sems, j, quad[j]) for j in range(3)]
    q_sends = [
        send(dq.at[rem(x + j, NX)], q_got.at[j - 1], x_sems, 5 + j, others_x[j - 1]) for j in (2, 1, 3)
    ]
    v_far.second()
    v_own.second()
    own_x.wait()
    for copy in x_sends + kg_sends:
        copy.wait_recv()
    heads = [kg[src] for src in range(NX)]
    w_sends = []

    def spread_product(turn, z):
        product = jnp.zeros((NY * BLK, HD), F32)
        for src in range(NX):
            rows = xg[src, z].reshape(NY * BLK, ROWS)
            product = product + jnp.dot(rows, heads[src], preferred_element_type=F32)
        w_part[turn] = product.astype(BF16).reshape(NY, BLK, HD)
        for j in (4, 3, 5, 2, 6, 1, 7):
            w_sends.append(
                send(
                    w_part.at[turn, rem(y + j, NY)], w_got.at[turn, j - 1],
                    (w_send, w_recv), turn * (NY - 1) + j - 1, others_y[j - 1],
                )
            )

    spread_product(0, far)

    def w_total(turn):
        for copy in w_sends[turn * (NY - 1) : (turn + 1) * (NY - 1)]:
            copy.wait_recv()
        out = w_part[turn, y].astype(F32)
        for j in range(NY - 1):
            out = out + w_got[turn, j].astype(F32)
        return out

    for copy in [w_swap] + kg_swaps:
        copy.wait_recv()
    quad_heads = [kg[x]] + [kg_quad[j] for j in range(3)]

    def in_block(h):
        out = jnp.zeros((ROWS, w_all.shape[2]), F32)
        for j, head in enumerate(quad_heads):
            rows = w_all[j, h] if j < 3 else w_last[h]
            out = out + lax.dot_general(head, rows, NT, preferred_element_type=F32)
        return out

    in_part[...] = in_block(1 - half).astype(BF16)
    in_send = send(in_part, in_got, s_sems, 3, over)

    spread_product(1, zh)
    z_out[1] = v_far.total().astype(BF16)
    z_val = send(z_out.at[1], z_got.at[1], z_sems, 1, partner)
    in_sum = in_block(half)
    zw_out[...] = w_total(0).astype(BF16)
    z_w = send(zw_out, zw_got, z_sems, 2, partner)
    q_sum = dq[x].astype(F32)
    for copy in q_sends:
        copy.wait_recv()
    for j in range(NX - 1):
        q_sum = q_sum + q_got[j].astype(F32)
    d_query[...] = q_sum.astype(BF16)
    in_send.wait_recv()
    d_input[...] = (in_sum + in_got[...].astype(F32)).astype(BF16)
    z_val.wait_recv()
    d_value[...] = (v_own.total() + z_got[1].astype(F32)).astype(BF16)
    w_sum = w_total(1)
    z_w.wait_recv()
    d_wkey[...] = w_sum + zw_got[...].astype(F32)

    for f in (v_far, v_own):
        f.drain()
    for copy in [z_key, z_val, z_w, in_send, w_swap] + k_own + x_sends + kg_sends + q_sends + w_sends + kg_swaps:
        copy.wait_send()


def dma(n):
    return pltpu.SemaphoreType.DMA((n,))


def params(collective_id=None):
    return pltpu.CompilerParams(
        collective_id=collective_id,
        has_side_effects=collective_id is not None,
        vmem_limit_bytes=VMEM_LIMIT,
    )


def in_hbm(array):
    return pltpu.with_memory_space_constraint(array, pltpu.HBM)


def hand_over_kernel(*refs):
    n = (len(refs) - 1) // 2
    copies = [
        pltpu.make_async_copy(refs[i], refs[n + i], refs[-1].at[i]) for i in range(n)
    ]
    for copy in copies:
        copy.start()
    for copy in copies:
        copy.wait()


def on_device(nl, inputs, w_key, values, queries, d_out, doc_lens, block_pos):
    width = inputs.shape[1]
    pairs = NZ * NY
    shape = jax.ShapeDtypeStruct
    slice_width = width // (nl * NC)
    w_split = w_key.reshape(2, 2, NC, slice_width, HD)
    keys, vals, qs, gs, turned, w_all, places = pl.pallas_call(
        gather_kernel,
        out_shape=(
            shape((NZ, NY, ROWS, HD), BF16),
            shape((NZ, NY, ROWS + 16, HD), BF16),
            shape((NX, ROWS, GROUP * HD), BF16),
            shape((NX, ROWS + 16, GROUP * HD), BF16),
            shape((NX, NZ, NY, BLK, ROWS), BF16),
            shape((3, 2, slice_width, HD), BF16),
            shape((8, ROWS), jnp.int32),
        ),
        in_specs=[hbm] * 8,
        out_specs=(vmem,) * 7,
        scratch_shapes=[
            pltpu.VMEM((ROWS, width), BF16),
            pltpu.VMEM((width, HD), BF16),
            pltpu.SMEM((4,), jnp.int32),
            pltpu.SMEM((2,), jnp.int32),
            dma(32), dma(32), dma(8), dma(8), dma(2), dma(2), dma(2), dma(2), dma(6 + 2 * PARTS),
        ],
        compiler_params=params(1),
        name="gather_rows",
    )(*(in_hbm(a) for a in (inputs, w_key, w_split, values, queries, d_out, doc_lens, block_pos)))
    keys = keys.reshape(KEY_BLOCKS * BLK, HD)
    vals = vals.reshape(pairs, ROWS + 16, HD)
    stats, plan = pl.pallas_call(
        stats_kernel,
        out_shape=(shape((3, QUERY_BLOCKS, STACK), F32), shape((PLAN,), jnp.int32)),
        in_specs=[smem, vmem, vmem, vmem, vmem],
        out_specs=(vmem, smem),
        scratch_shapes=[pltpu.VMEM((CHUNKS + 1, 3, QUERY_BLOCKS, STACK), F32)],
        compiler_params=params(),
        name="row_stats",
    )(places, keys, vals, qs, gs)
    stats = pl.pallas_call(
        share_kernel,
        out_shape=shape((3, QUERY_BLOCKS, STACK), F32),
        in_specs=[vmem],
        out_specs=vmem,
        scratch_shapes=[
            pltpu.VMEM((NX - 1, 3, QUERY_BLOCKS, STACK), F32), dma(NX - 1), dma(NX - 1),
        ],
        compiler_params=params(2),
        name="share_stats",
    )(stats)
    dq, dk, dv = pl.pallas_call(
        back_kernel,
        out_shape=(
            shape((NX, ROWS, GROUP * HD), BF16),
            shape((KEY_BLOCKS * BLK, HD), BF16),
            shape((KEY_BLOCKS * BLK, HD), BF16),
        ),
        in_specs=[smem, smem, vmem, vmem, vmem, vmem, vmem],
        out_specs=(vmem,) * 3,
        scratch_shapes=[
            pltpu.VMEM((QUERY_BLOCKS, HD, STACK), F32),
            pltpu.VMEM((KEY_BLOCKS * BLK, HD), F32),
            pltpu.VMEM((KEY_BLOCKS * BLK, HD), F32),
        ],
        compiler_params=params(),
        name="back_tiles",
    )(places, plan, stats, keys, vals, qs, gs)
    block = (ROWS, HD)
    results = pl.pallas_call(
        reduce_kernel,
        out_shape=(
            shape((ROWS, GROUP * HD), BF16),
            shape((ROWS, HD), BF16),
            shape((ROWS, slice_width), BF16),
            shape((BLK, HD), F32),
        ),
        in_specs=[vmem] * 5 + [hbm],
        out_specs=(vmem,) * 4,
        scratch_shapes=[
            pltpu.VMEM((NZ, NY - 1) + block, BF16),
            pltpu.VMEM((2, 2, ROWS + ROWS // 2, HD), BF16),
            pltpu.VMEM((2, 2) + block, BF16),
            pltpu.VMEM((2, 2) + block, BF16),
            pltpu.VMEM((2, 2) + block, BF16),
            pltpu.VMEM((NX - 1, ROWS, GROUP * HD), BF16),
            pltpu.VMEM((NZ, NY - 1, BLK, HD), BF16),
            pltpu.VMEM((2,) + block, BF16),
            pltpu.VMEM((2,) + block, BF16),
            pltpu.VMEM((NX,) + block, BF16),
            pltpu.VMEM((3,) + block, BF16),
            pltpu.VMEM((NX, NZ, NY, BLK, ROWS), BF16),
            pltpu.VMEM((2, slice_width, HD), BF16),
            pltpu.VMEM((NZ, NY, BLK, HD), BF16),
            pltpu.VMEM((ROWS, slice_width), BF16),
            pltpu.VMEM((ROWS, slice_width), BF16),
            pltpu.VMEM((BLK, HD), BF16),
            pltpu.VMEM((BLK, HD), BF16),
            dma(2 * (NY - 1)), dma(2 * (NY - 1)), dma(16), dma(16), dma(2 * (NY - 1)), dma(2 * (NY - 1)), dma(9), dma(9), dma(3), dma(3),
            dma(5), dma(5), dma(1),
        ],
        compiler_params=params(3),
        name="reduce_grads",
    )(dq, dk.reshape(NZ, NY, ROWS, HD), dv.reshape(NZ, NY, ROWS, HD), turned, w_all, in_hbm(w_split))
    return pl.pallas_call(
        hand_over_kernel,
        out_shape=tuple(shape(r.shape, r.dtype) for r in results),
        in_specs=[vmem] * 4,
        out_specs=(hbm,) * 4,
        scratch_shapes=[dma(4)],
        compiler_params=params(),
        name="hand_over",
    )(*results)


def solution(mesh):
    nl = mesh.shape["tensor"] // NC
    return jax.shard_map(
        functools.partial(on_device, nl),
        mesh=mesh,
        in_specs=(
            P("dp", None),
            P(None, "tensor"),
            P("dp", "tensor"),
            P("dp", "tensor"),
            P("dp", "tensor"),
            P(),
            P("dp"),
        ),
        out_specs=(P("dp", "tensor"), P("dp", "tensor"), P("dp", "tensor"), P("dp", "tensor")),
        check_vma=False,
    )
```

```python
import functools
import math

import jax
import jax.numpy as jnp
from jax import lax
from jax.experimental import pallas as pl
from jax.experimental.pallas import tpu as pltpu
from jax.sharding import PartitionSpec as P

MESH = pl.DeviceIdType.MESH
F32, BF16 = jnp.float32, jnp.bfloat16
HD, BLK, GROUP, ROWS = 128, 64, 4, 128
NX, NZ, NY, NC = 4, 2, 8, 2
HY, HX = NY // 2, NX // 2
KEY_BLOCKS = 2 * NZ * NY
QUERY_BLOCKS = 2 * NX
STACK = GROUP * BLK
CHUNK = 4
CHUNKS = KEY_BLOCKS // CHUNK
SIDE, WIDE = 4, 8
PARTS = 4
LIST, COUNTS, ITEMS, TOTAL, PLAN = 40, 320, 336, 416, 512
SCALE = 1.0 / math.sqrt(HD)
LOG2 = SCALE / math.log(2.0)
LOW = -1e30
FLOOR = -1e29
NT = (((1,), (1,)), ((), ()))
VMEM_LIMIT = 40 * 1024 * 1024

vmem = pl.BlockSpec(memory_space=pltpu.VMEM)
smem = pl.BlockSpec(memory_space=pltpu.SMEM)
hbm = pl.BlockSpec(memory_space=pltpu.HBM)


def rem(a, n):
    return lax.rem(a, jnp.int32(n))


def place():
    dp, tensor = lax.axis_index("dp"), lax.axis_index("tensor")
    x = rem(dp, NX)
    rest = lax.div(dp, jnp.int32(NX))
    return lax.div(rest, jnp.int32(NZ)), rem(rest, NZ), x, tensor


def device(y, zh, x, tensor):
    return ((y * NZ + zh) * NX + x, tensor)


def quad_of(y, zh, x, zl, core):
    quarter = rem(zl, 2)
    near = zl + 1 - 2 * quarter
    places = ((zl, 1 - core), (near, core), (near, 1 - core))
    return quarter, [device(y, zh, x, chip * NC + c) for chip, c in places]


def greet(peers):
    barrier = pltpu.get_barrier_semaphore()
    for peer in peers:
        pl.semaphore_signal(barrier, inc=1, device_id=peer, device_id_type=MESH)


def meet(peers):
    pl.semaphore_wait(pltpu.get_barrier_semaphore(), len(peers))


def send(src, dst, sems, index, peer):
    copy = pltpu.make_async_remote_copy(
        src_ref=src,
        dst_ref=dst,
        send_sem=sems[0].at[index],
        recv_sem=sems[1].at[index],
        device_id=peer,
        device_id_type=MESH,
    )
    copy.start()
    return copy


class Tree:
    def __init__(self, block, half, me, n, ups, downs, sems, base):
        self.block, self.half, self.me, self.n = block, half, me, n
        self.ups, self.downs, self.sems, self.base = ups, downs, sems, base

    def first(self):
        own = self.block(self.me)
        self.near = [
            send(own, own, self.sems, self.base + i, peer)
            for i, peer in enumerate((self.ups[1], self.downs[1], self.ups[0], self.downs[0]))
        ]

    def second(self):
        self.far = []
        for way, peers in enumerate((self.ups, self.downs)):
            self.near[way].wait_recv()
            ref = self.block(rem(self.me + (self.n - 2 if way == 0 else 2), self.n))
            half = self.half(ref, way)
            self.far.append(send(half, half, self.sems, self.base + 4 + 2 * way, peers[1]))
            self.far.append(send(ref, ref, self.sems, self.base + 5 + 2 * way, peers[0]))

    def end(self):
        for copy in self.near[2:] + self.far:
            copy.wait_recv()

    def drain(self):
        for copy in self.near + self.far:
            copy.wait_send()


def gather_kernel(
    inputs, w_key, w_split, values, queries, d_out, doc_lens, block_pos,
    keys, vals, qs, gs, turned, w_all, places,
    x_buf, w_buf, docs, pos, y_send, y_recv, x_send, x_recv, z_send, z_recv, s_send, s_recv, load_sem,
):
    y, zh, x, t = place()
    ups = [device(rem(y + j, NY), zh, x, t) for j in (1, 2)]
    downs = [device(rem(y + NY - j, NY), zh, x, t) for j in (1, 2)]
    others_x = [device(y, zh, rem(x + j, NX), t) for j in range(1, NX)]
    partner = device(y, 1 - zh, x, t)
    zl, core = lax.div(t, jnp.int32(NC)), rem(t, NC)
    quarter, quad = quad_of(y, zh, x, zl, core)
    peers = [partner] + ups + downs + others_x + quad[:2]
    greet(peers)
    loads = [
        pltpu.make_async_copy(src, dst, load_sem.at[i])
        for i, (src, dst) in enumerate(
            (
                (block_pos, pos),
                (values, vals.at[zh, y, pl.ds(0, ROWS)]),
                (d_out, gs.at[x, pl.ds(0, ROWS)]),
                (queries, qs.at[x]),
                (doc_lens, docs),
                (w_split.at[:, quarter, core], w_all.at[0]),
            )
        )
    ]
    depth = inputs.shape[1] // PARTS
    parts = []
    for i in range(PARTS):
        cut = slice(i * depth, (i + 1) * depth)
        parts.append((
            pltpu.make_async_copy(w_key.at[cut], w_buf.at[cut], load_sem.at[6 + 2 * i]),
            pltpu.make_async_copy(inputs.at[:, cut], x_buf.at[:, cut], load_sem.at[7 + 2 * i]),
        ))
    for load in loads[:5] + [load for pair in parts for load in pair] + loads[5:]:
        load.start()
    loads[0].wait()
    lane = lax.broadcasted_iota(jnp.int32, (16, ROWS), 1)
    first = 2 * (zh * NY + y)
    mine = jnp.where(lane == first, pos[0], 0) + jnp.where(lane == first + 1, pos[1], 0)
    seat = KEY_BLOCKS + 2 * x
    here = jnp.where(lane == seat, pos[0], 0) + jnp.where(lane == seat + 1, pos[1], 0)
    vals[zh, y, ROWS : ROWS + 16, :] = mine.astype(F32).astype(BF16)
    gs[x, ROWS : ROWS + 16, 0:HD] = here.astype(F32).astype(BF16)
    gs[x, ROWS : ROWS + 16, HD:] = jnp.zeros((16, (GROUP - 1) * HD), BF16)
    projected = jnp.zeros((ROWS, HD), F32)
    for i, pair in enumerate(parts):
        cut = slice(i * depth, (i + 1) * depth)
        for load in pair:
            load.wait()
        projected = projected + jnp.dot(
            x_buf[:, cut], w_buf[cut, :], preferred_element_type=F32
        )
    keys[zh, y] = projected.astype(BF16)
    for load in loads[1:4]:
        load.wait()
    meet(peers)

    y_sems, x_sems, z_sems = (y_send, y_recv), (x_send, x_recv), (z_send, z_recv)

    def half_k(ref, way):
        return ref.at[pl.ds(way * 64, 64)]

    def half_v(ref, way):
        return ref.at[pl.ds(0, 64)] if way == 0 else ref.at[pl.ds(64, ROWS + 16 - 64)]

    def tree(arr, half, z, base):
        return Tree(lambda o: arr.at[z, o], half, y, NY, ups, downs, y_sems, base)

    v_own, k_own = tree(vals, half_v, zh, 0), tree(keys, half_k, zh, 8)
    v_far, k_far = tree(vals, half_v, 1 - zh, 16), tree(keys, half_k, 1 - zh, 24)

    z_k = send(keys.at[zh, y], keys.at[zh, y], z_sems, 1, partner)
    z_v = send(vals.at[zh, y], vals.at[zh, y], z_sems, 0, partner)
    k_own.first()
    v_own.first()
    right, left = others_x[0], others_x[-1]
    sideways = []
    for i, (arr, _) in enumerate(((gs, half_v), (qs, half_k))):
        for way, peer in enumerate((right, left)):
            sideways.append(send(arr.at[x], arr.at[x], x_sems, 2 * i + way, peer))

    def turn(first, last):
        def body(j, carry):
            tile = x_buf[:, pl.ds(pl.multiple_of(j * 128, 128), 128)].T
            for part in range(2):
                b = 2 * j + part
                pair = lax.div(b, jnp.int32(NX))
                turned[rem(b, NX), rem(pair, NZ), lax.div(pair, jnp.int32(NZ))] = tile[
                    part * 64 : part * 64 + 64
                ]
            return carry

        lax.fori_loop(first, last, body, 0)

    tiles = inputs.shape[1] // 128
    onward = []

    def pass_on(i, arr, half):
        for way, peer in enumerate((right, left)):
            sideways[2 * i + way].wait_recv()
            ref = half(arr.at[rem(x + (NX - 1 if way == 0 else 1), NX)], way)
            onward.append(send(ref, ref, x_sems, 4 + 2 * i + way, peer))

    turn(0, tiles // 4)
    k_own.second()
    v_own.second()
    z_k.wait_recv()
    k_far.first()
    z_v.wait_recv()
    v_far.first()
    sides = ((quarter, 1 - core), (1 - quarter, core))
    swaps = [
        send(w_split.at[:, q, c], w_all.at[j + 1], (s_send, s_recv), j, quad[j])
        for j, (q, c) in enumerate(sides)
    ]
    pass_on(0, gs, half_v)
    turn(tiles // 4, tiles // 2)
    k_far.second()
    pass_on(1, qs, half_k)
    v_far.second()
    turn(tiles // 2, tiles)
    loads[4].wait()
    loads[5].wait()
    rings = (v_own, k_own, v_far, k_far)
    for r in rings:
        r.end()
    for copy in onward + swaps:
        copy.wait_recv()
    total = jnp.zeros((16, ROWS), F32)
    for z in range(NZ):
        for j in range(NY):
            total = total + vals[z, j, ROWS : ROWS + 16, :].astype(F32)
    for j in range(NX):
        total = total + gs[j, ROWS : ROWS + 16, 0:HD].astype(F32)
    seats = lax.broadcasted_iota(jnp.int32, (8, ROWS), 1)
    lengths = jnp.zeros((8, ROWS), jnp.int32)
    for d in range(4):
        lengths = lengths + jnp.where(seats == d, docs[d], 0)
    rows = lax.broadcasted_iota(jnp.int32, (8, ROWS), 0)
    places[...] = jnp.where(rows == 1, lengths, total[0:8].astype(jnp.int32))
    z_v.wait_send()
    z_k.wait_send()
    for r in rings:
        r.drain()
    for copy in sideways + onward + swaps:
        copy.wait_send()


def doc_starts(places):
    starts = [jnp.int32(0)]
    for d in range(3):
        starts.append(starts[-1] + places[1, d])
    return starts


def make_plan(places, plan):
    starts = doc_starts(places)

    def visit(pair, items):
        queries = [pair * 2, pair * 2 + 1]
        mine = [places[0, KEY_BLOCKS + query] for query in queries]
        low = []
        for m in mine:
            start = jnp.int32(0)
            for s in starts[1:]:
                start = jnp.where(s <= m * BLK, s, start)
            low.append(lax.div(start, jnp.int32(BLK)))
        at = [query * LIST for query in queries]
        for b in range(KEY_BLOCKS):
            pk = places[0, b]
            for i in range(2):
                plan[at[i]] = jnp.int32(b)
                at[i] = at[i] + ((pk <= mine[i]) & (pk >= low[i])).astype(jnp.int32)
        for i, query in enumerate(queries):
            for j in range(CHUNK):
                plan[at[i] + j] = jnp.int32(0)
            count = at[i] - query * LIST
            plan[COUNTS + query] = count
            for c in range(CHUNKS):
                plan[ITEMS + items] = query * 16 + c
                items = items + (count > c * CHUNK).astype(jnp.int32)
        return items

    items = lax.fori_loop(0, QUERY_BLOCKS // 2, visit, jnp.int32(0))
    for j in range(SIDE):
        plan[ITEMS + items + j] = jnp.int32(0)
    plan[TOTAL] = items


def item_of(places, plan, starts, at):
    real = at < plan[TOTAL]
    code = plan[ITEMS + at]
    query, chunk = code >> 4, code & 15
    count = jnp.where(real, plan[COUNTS + query], 0)
    row = places[0, KEY_BLOCKS + query] * BLK + (
        lax.broadcasted_iota(jnp.int32, (1, 2 * BLK), 1) & (BLK - 1)
    )
    opens = jnp.zeros((1, 2 * BLK), jnp.int32)
    for s in starts[1:]:
        opens = jnp.where(s <= row, s, opens)
    return query, chunk, real, count, row, opens


def key_chunk(places, plan, item, keys, vals):
    query, chunk, _, count, row, opens = item
    iota = lax.broadcasted_iota(jnp.int32, (BLK, 2 * BLK), 0)
    ks, vs, terms, blocks = [], [], [], []
    for j in range(CHUNK):
        at = chunk * CHUNK + j
        b = plan[query * LIST + at]
        base = jnp.where(at < count, places[0, b] * BLK, jnp.int32(1 << 20))
        ks.append(keys[pl.ds(pl.multiple_of(b * BLK, BLK), BLK), :])
        vs.append(vals[b >> 1, pl.ds(pl.multiple_of((b & 1) * BLK, BLK), BLK), :])
        ok = (iota >= opens - base) & (iota <= row - base)
        term = jnp.where(ok, 0.0, LOW)
        terms.append(jnp.concatenate([term, term], axis=1))
        blocks.append(b)
    return (
        jnp.concatenate(ks, axis=0),
        jnp.concatenate(vs, axis=0),
        jnp.concatenate(terms, axis=0),
        blocks,
    )


def over_items(plan, step):
    total = plan[TOTAL]
    wide = lax.div(total, jnp.int32(WIDE))
    rest = lax.div(total - wide * WIDE + (SIDE - 1), jnp.int32(SIDE))

    def wide_step(i, carry):
        step(i * WIDE, WIDE)
        return carry

    def side_step(i, carry):
        step(wide * WIDE + i * SIDE, SIDE)
        return carry

    lax.fori_loop(0, wide, wide_step, 0)
    lax.fori_loop(0, rest, side_step, 0)


def head_stack(ref, query):
    rows = pl.ds(pl.multiple_of((query & 1) * BLK, BLK), BLK)
    return jnp.concatenate(
        [ref[query >> 1, rows, h * HD : (h + 1) * HD] for h in range(GROUP)], axis=0
    )


def stats_kernel(places, keys, vals, qs, gs, out, plan, kept):
    make_plan(places, plan)
    starts = doc_starts(places)
    for c in range(CHUNKS):
        kept[c, 0] = jnp.full((QUERY_BLOCKS, STACK), FLOOR, F32)
        kept[c, 1] = jnp.zeros((QUERY_BLOCKS, STACK), F32)
        kept[c, 2] = jnp.zeros((QUERY_BLOCKS, STACK), F32)

    def step(first, width):
        found = []
        for part in range(width):
            item = item_of(places, plan, starts, first + part)
            k, v, term, _ = key_chunk(places, plan, item, keys, vals)
            q, g = head_stack(qs, item[0]), head_stack(gs, item[0])
            score = lax.dot_general(k, q, NT, preferred_element_type=F32) * LOG2 + term
            d_prob = lax.dot_general(v, g, NT, preferred_element_type=F32)
            top = jnp.maximum(FLOOR, jnp.max(score, axis=0, keepdims=True))
            e = jnp.exp2(score - top)
            found.append((
                item, top, jnp.sum(e, axis=0, keepdims=True), jnp.sum(e * d_prob, axis=0, keepdims=True)
            ))
        for item, top, mass, weighted in found:
            slot = jnp.where(item[2], item[1], CHUNKS)
            for j, value in enumerate((top, mass, weighted)):
                kept[slot, j, pl.ds(item[0], 1), :] = value

    over_items(plan, step)
    top = kept[0, 0]
    for c in range(1, CHUNKS):
        top = jnp.maximum(top, kept[c, 0])
    mass, weighted = jnp.zeros_like(top), jnp.zeros_like(top)
    for c in range(CHUNKS):
        shrink = jnp.exp2(kept[c, 0] - top)
        mass = mass + kept[c, 1] * shrink
        weighted = weighted + kept[c, 2] * shrink
    out[0], out[1], out[2] = top, mass, weighted


def share_kernel(stats, out, got, send_sem, recv_sem):
    y, zh, x, t = place()
    peers = [device(y, zh, rem(x + j, NX), t) for j in range(1, NX)]
    greet(peers)
    meet(peers)
    copies = [send(stats, got.at[j], (send_sem, recv_sem), j, peer) for j, peer in enumerate(peers)]
    for copy in copies:
        copy.wait_recv()
    parts = [[stats[i] for i in range(3)]] + [[got[j, i] for i in range(3)] for j in range(NX - 1)]
    top = parts[0][0]
    for p in parts[1:]:
        top = jnp.maximum(top, p[0])
    mass = jnp.zeros_like(top)
    weighted = jnp.zeros_like(top)
    for p in parts:
        shrink = jnp.exp2(p[0] - top)
        mass = mass + p[1] * shrink
        weighted = weighted + p[2] * shrink
    out[0] = top
    out[1] = 1.0 / mass
    out[2] = weighted / mass
    for copy in copies:
        copy.wait_send()


def back_kernel(
    places, plan, stats, keys, vals, qs, gs, dq, dk, dv, dq_sum, dk_sum, dv_sum
):
    starts = doc_starts(places)
    dq_sum[...] = jnp.zeros_like(dq_sum)
    dk_sum[...] = jnp.zeros_like(dk_sum)
    dv_sum[...] = jnp.zeros_like(dv_sum)

    def step(first, width):
        found = []
        for part in range(width):
            item = item_of(places, plan, starts, first + part)
            query = item[0]
            k, v, term, blocks = key_chunk(places, plan, item, keys, vals)
            q, g = head_stack(qs, query), head_stack(gs, query)
            top, scale, delta = [stats[j, pl.ds(query, 1), :] for j in range(3)]
            score = lax.dot_general(k, q, NT, preferred_element_type=F32) * LOG2 + term
            d_prob = lax.dot_general(v, g, NT, preferred_element_type=F32)
            prob = jnp.exp2(score - top) * scale
            d_score = (prob * (d_prob - delta)).astype(BF16)
            dv_part = jnp.dot(prob.astype(BF16), g, preferred_element_type=F32)
            dk_part = jnp.dot(d_score, q, preferred_element_type=F32)
            dq_part = jnp.dot(k.T, d_score, preferred_element_type=F32)
            found.append((query, blocks, dq_part, dk_part, dv_part))
        for query, blocks, dq_part, dk_part, dv_part in found:
            dq_sum[query] += dq_part
            for j, b in enumerate(blocks):
                rows = pl.ds(pl.multiple_of(b * BLK, BLK), BLK)
                dv_sum[rows, :] += dv_part[j * BLK : (j + 1) * BLK]
                dk_sum[rows, :] += dk_part[j * BLK : (j + 1) * BLK]

    over_items(plan, step)
    for query in range(QUERY_BLOCKS):
        dq_rows = (dq_sum[query] * SCALE).astype(BF16).T
        rows = slice((query % 2) * BLK, (query % 2 + 1) * BLK)
        for h in range(GROUP):
            dq[query // 2, rows, h * HD : (h + 1) * HD] = dq_rows[h * BLK : (h + 1) * BLK]
    dk[...] = (dk_sum[...] * SCALE).astype(BF16)
    dv[...] = dv_sum[...].astype(BF16)


class Fold:
    def __init__(self, block, me, n, ups, downs, far, near, made, last, sems, base):
        self.block, self.me, self.n, self.peers, self.sems, self.base = block, me, n, (ups, downs), sems, base
        self.got_far, self.got_near, self.made, self.got_last = far, near, made, last

    def at(self, way, far):
        return self.block(rem(self.me + (far if way == 0 else self.n - far), self.n))

    def go(self, src, dst, i, peer):
        return send(src, dst, self.sems, self.base + i, peer)

    def first(self):
        self.far, self.half, self.near = [], [], []
        for way, peers in enumerate(self.peers):
            part = pl.ds(way * (ROWS // 2), ROWS // 2)
            self.half.append(
                self.go(self.at(way, 4).at[part], self.got_far.at[way, pl.ds(ROWS, ROWS // 2)], way, peers[1])
            )
            self.far.append(
                self.go(self.at(way, 3), self.got_far.at[way, pl.ds(0, ROWS)], 2 + way, peers[0])
            )
        for way, peers in enumerate(self.peers):
            self.near.append(self.go(self.at(way, 1), self.got_near.at[way], 4 + way, peers[0]))

    def second(self):
        self.last = []
        middle = ROWS // 2
        for way, peers in enumerate(self.peers):
            self.far[way].wait_recv()
            self.half[way].wait_recv()
            own, far, out = self.at(way, 2), self.got_far.at[way], self.made.at[way]
            with_half = pl.ds(way * middle, middle)
            without = pl.ds((1 - way) * middle, middle)
            out[without] = (own[without].astype(F32) + far[without].astype(F32)).astype(BF16)
            out[with_half] = (
                own[with_half].astype(F32)
                + far[with_half].astype(F32)
                + far[pl.ds(ROWS, middle)].astype(F32)
            ).astype(BF16)
            self.last.append(self.go(out, self.got_last.at[way], 6 + way, peers[1]))

    def total(self):
        for copy in self.near + self.last:
            copy.wait_recv()
        out = self.block(self.me)[...].astype(F32)
        for way in range(2):
            out = out + self.got_near[way].astype(F32) + self.got_last[way].astype(F32)
        return out

    def drain(self):
        for copy in self.far + self.half + self.near + self.last:
            copy.wait_send()


def reduce_kernel(
    dq, dk, dv, turned, w_all, w_split, d_query, d_value, d_input, d_wkey,
    f_far, f_near, f_made, f_last, q_got, w_got, z_out, z_got,
    kg, kg_quad, xg, w_last, w_part, in_part, in_got, zw_out, zw_got,
    f_send, f_recv, w_send, w_recv, x_send, x_recv, z_send, z_recv, s_send, s_recv, load_sem,
):
    y, zh, x, t = place()
    zl, core = lax.div(t, jnp.int32(NC)), rem(t, NC)
    others_y = [device(rem(y + j, NY), zh, x, t) for j in range(1, NY)]
    ups, downs = others_y[:2], [others_y[-1], others_y[-2]]
    others_x = [device(y, zh, rem(x + j, NX), t) for j in range(1, NX)]
    partner = device(y, 1 - zh, x, t)
    half = lax.div(zl, jnp.int32(2))
    quarter, quad = quad_of(y, zh, x, zl, core)
    over = device(y, zh, x, rem(zl + 2, 4) * NC + core)
    x_sems, z_sems, s_sems = (x_send, x_recv), (z_send, z_recv), (s_send, s_recv)
    peers = [partner] + others_y + others_x + quad + [over]
    greet(peers)
    own_x = pltpu.make_async_copy(turned.at[x], xg.at[x], load_sem.at[0])
    own_x.start()
    meet(peers)

    def fold(arr, z, i):
        return Fold(
            lambda o: arr.at[z, o], y, NY, ups, downs,
            f_far.at[i], f_near.at[i], f_made.at[i], f_last.at[i], (f_send, f_recv), 8 * i,
        )

    far = 1 - zh
    v_far, v_own = fold(dv, far, 0), fold(dv, zh, 1)

    k_far, k_own = fold(dk, far, 3), fold(dk, zh, 2)
    k_far.first()
    k_own.first()
    x_sends = [
        send(turned.at[rem(x + j, NX)], xg.at[x], x_sems, j - 1, others_x[j - 1]) for j in (2, 1, 3)
    ]
    w_swap = send(w_split.at[:, 1 - quarter, 1 - core], w_last, s_sems, 4, quad[2])
    k_far.second()
    k_own.second()
    z_out[0] = k_far.total().astype(BF16)
    z_key = send(z_out.at[0], z_got.at[0], z_sems, 0, partner)
    v_far.first()
    v_own.first()
    key_sum = k_own.total()
    z_key.wait_recv()
    kg[x] = (key_sum + z_got[0].astype(F32)).astype(BF16)

    kg_sends = [send(kg.at[x], kg.at[x], x_sems, 2 + j, others_x[j - 1]) for j in (2, 1, 3)]
    kg_swaps = [send(kg.at[x], kg_quad.at[j], s_sems, j, quad[j]) for j in range(3)]
    q_sends = [
        send(dq.at[rem(x + j, NX)], q_got.at[j - 1], x_sems, 5 + j, others_x[j - 1]) for j in (2, 1, 3)
    ]
    v_far.second()
    v_own.second()
    own_x.wait()
    for copy in x_sends + kg_sends:
        copy.wait_recv()
    heads = [kg[src] for src in range(NX)]
    w_sends = []

    def spread_product(turn, z):
        product = jnp.zeros((NY * BLK, HD), F32)
        for src in range(NX):
            rows = xg[src, z].reshape(NY * BLK, ROWS)
            product = product + jnp.dot(rows, heads[src], preferred_element_type=F32)
        w_part[turn] = product.astype(BF16).reshape(NY, BLK, HD)
        for j in (4, 3, 5, 2, 6, 1, 7):
            w_sends.append(
                send(
                    w_part.at[turn, rem(y + j, NY)], w_got.at[turn, j - 1],
                    (w_send, w_recv), turn * (NY - 1) + j - 1, others_y[j - 1],
                )
            )

    spread_product(0, far)

    def w_total(turn):
        for copy in w_sends[turn * (NY - 1) : (turn + 1) * (NY - 1)]:
            copy.wait_recv()
        out = w_part[turn, y].astype(F32)
        for j in range(NY - 1):
            out = out + w_got[turn, j].astype(F32)
        return out

    for copy in [w_swap] + kg_swaps:
        copy.wait_recv()
    quad_heads = [kg[x]] + [kg_quad[j] for j in range(3)]

    def in_block(h):
        out = jnp.zeros((ROWS, w_all.shape[2]), F32)
        for j, head in enumerate(quad_heads):
            rows = w_all[j, h] if j < 3 else w_last[h]
            out = out + lax.dot_general(head, rows, NT, preferred_element_type=F32)
        return out

    in_part[...] = in_block(1 - half).astype(BF16)
    in_send = send(in_part, in_got, s_sems, 3, over)

    spread_product(1, zh)
    z_out[1] = v_far.total().astype(BF16)
    z_val = send(z_out.at[1], z_got.at[1], z_sems, 1, partner)
    in_sum = in_block(half)
    zw_out[...] = w_total(0).astype(BF16)
    z_w = send(zw_out, zw_got, z_sems, 2, partner)
    q_sum = dq[x].astype(F32)
    for copy in q_sends:
        copy.wait_recv()
    for j in range(NX - 1):
        q_sum = q_sum + q_got[j].astype(F32)
    d_query[...] = q_sum.astype(BF16)
    in_send.wait_recv()
    d_input[...] = (in_sum + in_got[...].astype(F32)).astype(BF16)
    z_val.wait_recv()
    d_value[...] = (v_own.total() + z_got[1].astype(F32)).astype(BF16)
    w_sum = w_total(1)
    z_w.wait_recv()
    d_wkey[...] = w_sum + zw_got[...].astype(F32)

    for f in (v_far, v_own, k_far, k_own):
        f.drain()
    for copy in [z_key, z_val, z_w, in_send, w_swap] + x_sends + kg_sends + q_sends + w_sends + kg_swaps:
        copy.wait_send()


def dma(n):
    return pltpu.SemaphoreType.DMA((n,))


def params(collective_id=None):
    return pltpu.CompilerParams(
        collective_id=collective_id,
        has_side_effects=collective_id is not None,
        vmem_limit_bytes=VMEM_LIMIT,
    )


def in_hbm(array):
    return pltpu.with_memory_space_constraint(array, pltpu.HBM)


def hand_over_kernel(*refs):
    n = (len(refs) - 1) // 2
    copies = [
        pltpu.make_async_copy(refs[i], refs[n + i], refs[-1].at[i]) for i in range(n)
    ]
    for copy in copies:
        copy.start()
    for copy in copies:
        copy.wait()


def on_device(nl, inputs, w_key, values, queries, d_out, doc_lens, block_pos):
    width = inputs.shape[1]
    pairs = NZ * NY
    shape = jax.ShapeDtypeStruct
    slice_width = width // (nl * NC)
    w_split = w_key.reshape(2, 2, NC, slice_width, HD)
    keys, vals, qs, gs, turned, w_all, places = pl.pallas_call(
        gather_kernel,
        out_shape=(
            shape((NZ, NY, ROWS, HD), BF16),
            shape((NZ, NY, ROWS + 16, HD), BF16),
            shape((NX, ROWS, GROUP * HD), BF16),
            shape((NX, ROWS + 16, GROUP * HD), BF16),
            shape((NX, NZ, NY, BLK, ROWS), BF16),
            shape((3, 2, slice_width, HD), BF16),
            shape((8, ROWS), jnp.int32),
        ),
        in_specs=[hbm] * 8,
        out_specs=(vmem,) * 7,
        scratch_shapes=[
            pltpu.VMEM((ROWS, width), BF16),
            pltpu.VMEM((width, HD), BF16),
            pltpu.SMEM((4,), jnp.int32),
            pltpu.SMEM((2,), jnp.int32),
            dma(32), dma(32), dma(8), dma(8), dma(2), dma(2), dma(2), dma(2), dma(6 + 2 * PARTS),
        ],
        compiler_params=params(1),
        name="gather_rows",
    )(*(in_hbm(a) for a in (inputs, w_key, w_split, values, queries, d_out, doc_lens, block_pos)))
    keys = keys.reshape(KEY_BLOCKS * BLK, HD)
    vals = vals.reshape(pairs, ROWS + 16, HD)
    stats, plan = pl.pallas_call(
        stats_kernel,
        out_shape=(shape((3, QUERY_BLOCKS, STACK), F32), shape((PLAN,), jnp.int32)),
        in_specs=[smem, vmem, vmem, vmem, vmem],
        out_specs=(vmem, smem),
        scratch_shapes=[pltpu.VMEM((CHUNKS + 1, 3, QUERY_BLOCKS, STACK), F32)],
        compiler_params=params(),
        name="row_stats",
    )(places, keys, vals, qs, gs)
    stats = pl.pallas_call(
        share_kernel,
        out_shape=shape((3, QUERY_BLOCKS, STACK), F32),
        in_specs=[vmem],
        out_specs=vmem,
        scratch_shapes=[
            pltpu.VMEM((NX - 1, 3, QUERY_BLOCKS, STACK), F32), dma(NX - 1), dma(NX - 1),
        ],
        compiler_params=params(2),
        name="share_stats",
    )(stats)
    dq, dk, dv = pl.pallas_call(
        back_kernel,
        out_shape=(
            shape((NX, ROWS, GROUP * HD), BF16),
            shape((KEY_BLOCKS * BLK, HD), BF16),
            shape((KEY_BLOCKS * BLK, HD), BF16),
        ),
        in_specs=[smem, smem, vmem, vmem, vmem, vmem, vmem],
        out_specs=(vmem,) * 3,
        scratch_shapes=[
            pltpu.VMEM((QUERY_BLOCKS, HD, STACK), F32),
            pltpu.VMEM((KEY_BLOCKS * BLK, HD), F32),
            pltpu.VMEM((KEY_BLOCKS * BLK, HD), F32),
        ],
        compiler_params=params(),
        name="back_tiles",
    )(places, plan, stats, keys, vals, qs, gs)
    block = (ROWS, HD)
    results = pl.pallas_call(
        reduce_kernel,
        out_shape=(
            shape((ROWS, GROUP * HD), BF16),
            shape((ROWS, HD), BF16),
            shape((ROWS, slice_width), BF16),
            shape((BLK, HD), F32),
        ),
        in_specs=[vmem] * 5 + [hbm],
        out_specs=(vmem,) * 4,
        scratch_shapes=[
            pltpu.VMEM((4, 2, ROWS + ROWS // 2, HD), BF16),
            pltpu.VMEM((4, 2) + block, BF16),
            pltpu.VMEM((4, 2) + block, BF16),
            pltpu.VMEM((4, 2) + block, BF16),
            pltpu.VMEM((NX - 1, ROWS, GROUP * HD), BF16),
            pltpu.VMEM((NZ, NY - 1, BLK, HD), BF16),
            pltpu.VMEM((2,) + block, BF16),
            pltpu.VMEM((2,) + block, BF16),
            pltpu.VMEM((NX,) + block, BF16),
            pltpu.VMEM((3,) + block, BF16),
            pltpu.VMEM((NX, NZ, NY, BLK, ROWS), BF16),
            pltpu.VMEM((2, slice_width, HD), BF16),
            pltpu.VMEM((NZ, NY, BLK, HD), BF16),
            pltpu.VMEM((ROWS, slice_width), BF16),
            pltpu.VMEM((ROWS, slice_width), BF16),
            pltpu.VMEM((BLK, HD), BF16),
            pltpu.VMEM((BLK, HD), BF16),
            dma(32), dma(32), dma(2 * (NY - 1)), dma(2 * (NY - 1)), dma(9), dma(9), dma(3), dma(3),
            dma(5), dma(5), dma(1),
        ],
        compiler_params=params(3),
        name="reduce_grads",
    )(dq, dk.reshape(NZ, NY, ROWS, HD), dv.reshape(NZ, NY, ROWS, HD), turned, w_all, in_hbm(w_split))
    return pl.pallas_call(
        hand_over_kernel,
        out_shape=tuple(shape(r.shape, r.dtype) for r in results),
        in_specs=[vmem] * 4,
        out_specs=(hbm,) * 4,
        scratch_shapes=[dma(4)],
        compiler_params=params(),
        name="hand_over",
    )(*results)


def solution(mesh):
    nl = mesh.shape["tensor"] // NC
    return jax.shard_map(
        functools.partial(on_device, nl),
        mesh=mesh,
        in_specs=(
            P("dp", None),
            P(None, "tensor"),
            P("dp", "tensor"),
            P("dp", "tensor"),
            P("dp", "tensor"),
            P(),
            P("dp"),
        ),
        out_specs=(P("dp", "tensor"), P("dp", "tensor"), P("dp", "tensor"), P("dp", "tensor")),
        check_vma=False,
    )
```
